32 devices in a mesh: wide: 16 (over z, x, core), narrow: 2 (over y).
Axes of the slice: x: 2, y: 2, z: 4, core: 2. Of those that a mesh axis runs over, the one named last changes fastest.
Arguments:
- tokens: bfloat16 [2, 4096, 1024], P(None, ('wide', 'narrow')), may hold values from -6 to 6
- cotangent: bfloat16 [2, 4096, 1024], P(None, ('wide', 'narrow')), may hold values from -6 to 6
- lengths: int32 [2], replicated, may hold values from 3584 to 4096, as said below
- loss_mask: int32 [2, 4096], P(None, ('wide', 'narrow')), may hold values 0 or 1
- norm_gain: bfloat16 [1024], P(('wide', 'narrow')), may hold values from 0.5 to 1.5
- in_weight: bfloat16 [1024, 3072], P(('wide', 'narrow')), may hold values from -0.1875 to 0.1875
- conv_kernel: bfloat16 [3, 1024], P(None, ('wide', 'narrow')), may hold values from -3.5 to 3.5
- out_weight: bfloat16 [1024, 1024], P(('wide', 'narrow')), may hold values from -0.1875 to 0.1875
- ffn_gain: bfloat16 [1024], P(('wide', 'narrow')), may hold values from 0.5 to 1.5
- gate_weight: bfloat16 [1024, 4608], P(('wide', 'narrow')), may hold values from -0.1875 to 0.1875
- up_weight: bfloat16 [1024, 4608], P(('wide', 'narrow')), may hold values from -0.1875 to 0.1875
- down_weight: bfloat16 [4608, 1024], P(('wide', 'narrow')), may hold values from -0.09375 to 0.09375
Outputs:
- block_out: bfloat16 [2, 4096, 1024], P(None, ('wide', 'narrow'))
- input_grad: float32 [2, 4096, 1024], P(None, ('wide', 'narrow'))
- norm_gain_grad: float32 [1024], P(('wide', 'narrow'))
- in_weight_grad: float32 [1024, 3072], P(('wide', 'narrow'))
- conv_kernel_grad: float32 [3, 1024], P(None, ('wide', 'narrow'))
- out_weight_grad: float32 [1024, 1024], P(('wide', 'narrow'))
- ffn_gain_grad: float32 [1024], P(('wide', 'narrow'))
- gate_weight_grad: float32 [1024, 4608], P(('wide', 'narrow'))
- up_weight_grad: float32 [1024, 4608], P(('wide', 'narrow'))
- down_weight_grad: float32 [4608, 1024], P(('wide', 'narrow'))
The draws below stay inside these ranges and needn't reach their ends.
Inputs may be any that keep to these rules, and one draw needn't show every extreme that they name: `lengths`: in every draw one micro-batch, drawn from the seed, has the full length 4096.
All inputs are finite; a program needn't handle non-finite values. No bound on the sum of `loss_mask` on one device may be relied on, other than what follows from the above.
Results may differ from the reference program's by a relative error of at most 0.0095.
Values may be sent and summed in bfloat16 or wider, within the bound.
A program may use at most 256 MiB of HBM per device.

```python
import jax
import jax.numpy as jnp
from jax import lax

D = 1024
FF = 4608
MICRO = 2
TOKENS = 4096


def draw_lengths(key, part):
    key = jax.random.fold_in(key, 11)
    key_lengths, key_full = jax.random.split(key)
    drawn = jax.random.randint(key_lengths, (MICRO,), TOKENS - TOKENS // 8, TOKENS + 1)
    chosen = jax.random.randint(key_full, (), 0, MICRO)
    drawn = jnp.where(jnp.arange(MICRO) == chosen, TOKENS, drawn)
    return drawn.astype(jnp.int32)


def touch_ends(array, rng, least, top_value):
    extent = array.shape
    place = [jax.random.randint(jax.random.fold_in(rng, axis), (), 0, extent[axis]) for axis in range(len(extent))]
    array = array.at[tuple(place)].set(least)
    longest = extent.index(max(extent))
    place[longest] = (place[longest] + 1) % extent[longest]
    return array.at[tuple(place)].set(top_value)


def strengthened(values, rng, source, target, blocks, factor):
    def block_of(dim):
        return (jnp.arange(values.shape[dim]) // (values.shape[dim] // blocks)).reshape((-1,) + (1,) * (values.ndim - 1 - dim))

    first = jax.random.permutation(rng, blocks)[block_of(target)]
    far = (block_of(target) + blocks // 2) % blocks
    return jnp.where((block_of(source) == first) | (block_of(source) == far), factor * values, values)


def block_levels(stream_key, extent, cuts, least, largest):
    gain, own = 1.0, jax.random.fold_in(stream_key, 6)
    for position, blocks in cuts:
        heights = jnp.exp(jax.random.uniform(jax.random.fold_in(own, position), (blocks,), jnp.float32, least / len(cuts), largest / len(cuts)))
        gain = gain * jnp.repeat(heights, extent[position] // blocks).reshape([-1 if axis == position else 1 for axis in range(len(extent))])
    return gain


def noise(key, extent, spread, most, shards=(), held_as=jnp.bfloat16):
    values = spread * jax.random.normal(key, extent, jnp.float32)
    if shards:
        values = values * block_levels(key, extent, shards, -0.22, 0.18)
    return jnp.clip(values, -most, most).astype(held_as)


def gaussian_with(rng, extent, scale, bound, cuts, heavy, kind=jnp.bfloat16):
    values = scale * jax.random.normal(rng, extent, jnp.float32)
    if cuts:
        values = values * block_levels(rng, extent, cuts, -0.22, 0.18)
    return jnp.clip(strengthened(values, jax.random.fold_in(rng, 3), *heavy), -bound, bound).astype(kind)


def setup_inputs(seed: int = 0) -> dict:
    streams_of = jax.random.split(jax.random.key(seed), 13)
    tokens = gaussian_with(streams_of[0], (MICRO, TOKENS, D), 1.0, 6.0, ((1, 32),), (1, 2, 32, 2.75))
    cotangent = noise(streams_of[1], (MICRO, TOKENS, D), 1.0, 6.0, ((1, 32),))
    lengths = draw_lengths(jax.random.fold_in(streams_of[12], 71), 0)
    loss_mask = touch_ends((jax.random.randint(streams_of[3], (MICRO, TOKENS), 0, 8) < 7).astype(jnp.int32), jax.random.fold_in(streams_of[3], 1), 0, 1)
    norm_gain = jnp.clip(1.0 + 0.1 * jax.random.normal(streams_of[4], (D,), jnp.float32), 0.5, 1.5).astype(jnp.bfloat16)
    in_weight = noise(streams_of[5], (D, 3 * D), D ** -0.5, 0.1875, ((0, 32),))
    conv_kernel = noise(streams_of[6], (3, D), 3 ** -0.5, 3.5, ((1, 32),))
    out_weight = noise(streams_of[7], (D, D), D ** -0.5, 0.1875, ((0, 32),))
    ffn_gain = jnp.clip(1.0 + 0.1 * jax.random.normal(streams_of[8], (D,), jnp.float32), 0.5, 1.5).astype(jnp.bfloat16)
    gate_weight = noise(streams_of[9], (D, FF), D ** -0.5, 0.1875, ((0, 32),))
    up_weight = noise(streams_of[10], (D, FF), D ** -0.5, 0.1875, ((0, 32),))
    down_weight = noise(streams_of[11], (FF, D), FF ** -0.5, 0.09375, ((0, 32),))
    return {"tokens": tokens, "cotangent": cotangent, "lengths": lengths, "loss_mask": loss_mask, "norm_gain": norm_gain, "in_weight": in_weight, "conv_kernel": conv_kernel, "out_weight": out_weight, "ffn_gain": ffn_gain, "gate_weight": gate_weight, "up_weight": up_weight, "down_weight": down_weight}


EPSILON = 1e-05

@jax.custom_vjp
def low(v):
    return lax.optimization_barrier(v.astype(jnp.bfloat16)).astype(jnp.float32)

@jax.custom_vjp
def low_back(v):
    return v

def low_keep(v):
    return (low(v), None)

def low_pass(kept, grad):
    return (grad,)

def back_keep(v):
    return (v, None)

def back_low(kept, grad):
    return (low(grad),)
low.defvjp(low_keep, low_pass)
low_back.defvjp(back_keep, back_low)

def product(left, right):
    return jnp.dot(left, right, precision=lax.Precision.HIGHEST, preferred_element_type=jnp.float32)

def block_forward(inputs, norm_gain, in_weight, conv_kernel, out_weight, ffn_gain, gate_weight, up_weight, down_weight):
    scale_one = lax.rsqrt(lax.optimization_barrier(jnp.mean(inputs * inputs, axis=-1, keepdims=True)) + EPSILON)
    normed_one = low(inputs * scale_one * norm_gain)
    projected = low_back(product(normed_one, in_weight))
    b_gate = projected[:, :D]
    c_gate = projected[:, D:2 * D]
    conv_input = projected[:, 2 * D:]
    gated_input = b_gate * conv_input
    padded = jnp.concatenate([jnp.zeros((2, D), jnp.float32), gated_input], axis=0)
    mixed_conv = conv_kernel[0] * padded[:-2] + conv_kernel[1] * padded[1:-1] + conv_kernel[2] * padded[2:]
    branch = low(c_gate * mixed_conv)
    attended = low_back(product(branch, out_weight))
    hidden = inputs + attended
    scale_two = lax.rsqrt(lax.optimization_barrier(jnp.mean(hidden * hidden, axis=-1, keepdims=True)) + EPSILON)
    normed_two = low(hidden * scale_two * ffn_gain)
    gate_out = low_back(product(normed_two, gate_weight))
    up_out = low_back(product(normed_two, up_weight))
    activated = low(jax.nn.silu(gate_out) * up_out)
    ffn_out = low_back(product(activated, down_weight))
    return hidden + ffn_out

def reference(tokens, cotangent, lengths, loss_mask, norm_gain, in_weight, conv_kernel, out_weight, ffn_gain, gate_weight, up_weight, down_weight):
    weights = tuple((member.astype(jnp.float32) for member in (norm_gain, in_weight, conv_kernel, out_weight, ffn_gain, gate_weight, up_weight, down_weight)))
    positions = jnp.arange(TOKENS, dtype=jnp.int32)

    def one_batch(totals, inputs):
        token_rows, cot_rows, length, mask_row = inputs
        result, pullback = jax.vjp(block_forward, token_rows.astype(jnp.float32), *weights)
        validity = (positions < length).astype(jnp.float32) * mask_row.astype(jnp.float32)
        gradients = pullback(cot_rows.astype(jnp.float32) * validity[:, None])
        totals = tuple((running + addend for running, addend in zip(totals, gradients[1:])))
        return (totals, (result.astype(jnp.bfloat16), gradients[0]))
    starting = tuple((jnp.zeros_like(member) for member in weights))
    totals, outputs = lax.scan(one_batch, starting, (tokens, cotangent, lengths, loss_mask))
    block_out, input_grad = outputs
    gain_one, in_grad, kernel_grad, out_grad, gain_two, gate_grad, up_grad, down_grad = totals
    return (block_out, input_grad, gain_one, in_grad, kernel_grad, out_grad, gain_two, gate_grad, up_grad, down_grad)
```

```python
import functools

import jax
import jax.numpy as jnp
from jax import lax
from jax.experimental import pallas as pl
from jax.experimental.pallas import tpu as pltpu
from jax.sharding import PartitionSpec as P

EPSILON = 1e-05


def shifted(block, axis, distance):
    devices = range(lax.axis_size(axis))
    route = [(i - distance, i) for i in devices if i - distance in devices]
    return lax.ppermute(block, axis, route)


def along_rows(left, weight):
    return lax.dot_general(
        left, weight, (((1,), (1,)), ((), ())), preferred_element_type=jnp.float32
    )


def over_rows(left, right):
    return lax.dot_general(
        left, right, (((0,), (0,)), ((), ())), preferred_element_type=jnp.float32
    )


def collect(shards):
    partial_set = (
        lax.all_gather(shards[0], "narrow", axis=0, tiled=True),
        lax.all_gather(shards[1], "narrow", axis=0, tiled=True),
        lax.all_gather(shards[2], "narrow", axis=1, tiled=True),
        lax.all_gather(shards[3], "narrow", axis=0, tiled=True),
        lax.all_gather(shards[4], "narrow", axis=0, tiled=True),
        lax.all_gather(shards[5], "narrow", axis=0, tiled=True),
        lax.all_gather(shards[6], "narrow", axis=0, tiled=True),
        lax.all_gather(shards[7], "narrow", axis=0, tiled=True),
    )
    return (
        lax.all_gather(partial_set[0], "wide", axis=0, tiled=True),
        lax.all_gather(partial_set[1], "wide", axis=0, tiled=True),
        lax.all_gather(partial_set[2], "wide", axis=1, tiled=True),
        lax.all_gather(partial_set[3], "wide", axis=0, tiled=True),
        lax.all_gather(partial_set[4], "wide", axis=0, tiled=True),
        lax.all_gather(partial_set[5], "wide", axis=0, tiled=True),
        lax.all_gather(partial_set[6], "wide", axis=0, tiled=True),
        lax.all_gather(partial_set[7], "wide", axis=0, tiled=True),
    )


def collect_tied(shards, anchor):
    tied_shards, _ = lax.optimization_barrier((shards, anchor))
    return collect(tied_shards)


def body(
    tokens,
    cotangent,
    lengths,
    loss_mask,
    norm_gain,
    in_weight,
    conv_kernel,
    out_weight,
    ffn_gain,
    gate_weight,
    up_weight,
    down_weight,
):
    micro_count = tokens.shape[0]
    local_rows = tokens.shape[1]
    width = tokens.shape[2]
    shards = (
        norm_gain,
        in_weight,
        conv_kernel,
        out_weight,
        ffn_gain,
        gate_weight,
        up_weight,
        down_weight,
    )
    positions = lax.axis_index(("wide", "narrow")) * local_rows + jnp.arange(
        local_rows, dtype=jnp.int32
    )
    gain_one_grad = jnp.zeros((width,), jnp.float32)
    gain_two_grad = jnp.zeros((width,), jnp.float32)
    kernel_grad = jnp.zeros((3, width), jnp.float32)
    outputs = []
    input_grads = []
    kept_normed_one = []
    kept_proj_seed = []
    kept_branch = []
    kept_out_seed = []
    kept_normed_two = []
    kept_gate_seed = []
    kept_up_seed = []
    kept_activated = []
    kept_down_seed = []
    for batch in range(micro_count):
        gathered = collect_tied(shards, tokens[batch])
        gain_full, in_full, kernel_full, out_full, ffn_full, gate_full, up_full, down_full = (
            gathered
        )
        gain_f32 = gain_full.astype(jnp.float32)
        ffn_f32 = ffn_full.astype(jnp.float32)
        kernel_f32 = kernel_full.astype(jnp.float32)
        inputs = tokens[batch].astype(jnp.float32)
        scale_one = lax.rsqrt(jnp.mean(inputs * inputs, axis=-1, keepdims=True) + EPSILON)
        normed_one = (inputs * scale_one * gain_f32).astype(jnp.bfloat16)
        projected = jnp.dot(normed_one, in_full, preferred_element_type=jnp.float32)
        b_gate = projected[:, :width]
        c_gate = projected[:, width : 2 * width]
        conv_input = projected[:, 2 * width :]
        gated_input = b_gate * conv_input
        earlier = shifted(gated_input[local_rows - 2 :], ("wide", "narrow"), 1)
        padded = jnp.concatenate([earlier, gated_input], axis=0)
        mixed_conv = (
            kernel_f32[0] * padded[:-2] + kernel_f32[1] * padded[1:-1] + kernel_f32[2] * gated_input
        )
        branch = (c_gate * mixed_conv).astype(jnp.bfloat16)
        hidden = inputs + jnp.dot(branch, out_full, preferred_element_type=jnp.float32)
        scale_two = lax.rsqrt(jnp.mean(hidden * hidden, axis=-1, keepdims=True) + EPSILON)
        normed_two = (hidden * scale_two * ffn_f32).astype(jnp.bfloat16)
        gate_out = jnp.dot(normed_two, gate_full, preferred_element_type=jnp.float32)
        up_out = jnp.dot(normed_two, up_full, preferred_element_type=jnp.float32)
        sigmoid_gate = jax.nn.sigmoid(gate_out)
        silu_gate = gate_out * sigmoid_gate
        activated = (silu_gate * up_out).astype(jnp.bfloat16)
        result = hidden + jnp.dot(activated, down_full, preferred_element_type=jnp.float32)
        outputs.append(result.astype(jnp.bfloat16))
        validity = (positions < lengths[batch]).astype(jnp.float32) * loss_mask[batch].astype(
            jnp.float32
        )
        seed = cotangent[batch].astype(jnp.float32) * validity[:, None]
        down_seed = seed.astype(jnp.bfloat16)
        act_grad = along_rows(down_seed, down_full)
        up_seed = (act_grad * silu_gate).astype(jnp.bfloat16)
        gate_seed = (
            act_grad * up_out * sigmoid_gate * (1.0 + gate_out * (1.0 - sigmoid_gate))
        ).astype(jnp.bfloat16)
        normed_two_grad = along_rows(gate_seed, gate_full) + along_rows(up_seed, up_full)
        gain_two_grad = gain_two_grad + jnp.sum(normed_two_grad * hidden * scale_two, axis=0)
        scaled_two = normed_two_grad * ffn_f32
        hidden_grad = (
            seed
            + scale_two * scaled_two
            - hidden
            * (scale_two * scale_two * scale_two)
            * jnp.mean(scaled_two * hidden, axis=-1, keepdims=True)
        )
        out_seed = hidden_grad.astype(jnp.bfloat16)
        branch_grad = along_rows(out_seed, out_full)
        c_grad = branch_grad * mixed_conv
        conv_grad = branch_grad * c_gate
        kernel_grad = kernel_grad + jnp.stack(
            [
                jnp.sum(conv_grad * padded[:-2], axis=0),
                jnp.sum(conv_grad * padded[1:-1], axis=0),
                jnp.sum(conv_grad * gated_input, axis=0),
            ],
            axis=0,
        )
        later = shifted(conv_grad[:2], ("wide", "narrow"), -1)
        extended = jnp.concatenate([conv_grad, later], axis=0)
        gated_grad = (
            kernel_f32[2] * conv_grad
            + kernel_f32[1] * extended[1 : local_rows + 1]
            + kernel_f32[0] * extended[2:]
        )
        proj_seed = jnp.concatenate(
            [gated_grad * conv_input, c_grad, gated_grad * b_gate], axis=1
        ).astype(jnp.bfloat16)
        normed_one_grad = along_rows(proj_seed, in_full)
        gain_one_grad = gain_one_grad + jnp.sum(normed_one_grad * inputs * scale_one, axis=0)
        scaled_one = normed_one_grad * gain_f32
        input_grads.append(
            hidden_grad
            + scale_one * scaled_one
            - inputs
            * (scale_one * scale_one * scale_one)
            * jnp.mean(scaled_one * inputs, axis=-1, keepdims=True)
        )
        kept_normed_one.append(normed_one)
        kept_proj_seed.append(proj_seed)
        kept_branch.append(branch)
        kept_out_seed.append(out_seed)
        kept_normed_two.append(normed_two)
        kept_gate_seed.append(gate_seed)
        kept_up_seed.append(up_seed)
        kept_activated.append(activated)
        kept_down_seed.append(down_seed)
    all_normed_two = jnp.concatenate(kept_normed_two, axis=0)
    in_grad = over_rows(
        jnp.concatenate(kept_normed_one, axis=0), jnp.concatenate(kept_proj_seed, axis=0)
    )
    out_grad = over_rows(
        jnp.concatenate(kept_branch, axis=0), jnp.concatenate(kept_out_seed, axis=0)
    )
    gate_grad = over_rows(all_normed_two, jnp.concatenate(kept_gate_seed, axis=0))
    up_grad = over_rows(all_normed_two, jnp.concatenate(kept_up_seed, axis=0))
    down_grad = over_rows(
        jnp.concatenate(kept_activated, axis=0), jnp.concatenate(kept_down_seed, axis=0)
    )
    gain_one_part, in_part, kernel_part, out_part, gain_two_part, gate_part, up_part, down_part = (
        lax.psum_scatter(gain_one_grad, "wide", scatter_dimension=0, tiled=True),
        lax.psum_scatter(in_grad, "wide", scatter_dimension=0, tiled=True),
        lax.psum_scatter(kernel_grad, "wide", scatter_dimension=1, tiled=True),
        lax.psum_scatter(out_grad, "wide", scatter_dimension=0, tiled=True),
        lax.psum_scatter(gain_two_grad, "wide", scatter_dimension=0, tiled=True),
        lax.psum_scatter(gate_grad, "wide", scatter_dimension=0, tiled=True),
        lax.psum_scatter(up_grad, "wide", scatter_dimension=0, tiled=True),
        lax.psum_scatter(down_grad, "wide", scatter_dimension=0, tiled=True),
    )
    gain_one_sum, in_sum, kernel_sum, out_sum, gain_two_sum, gate_sum, up_sum, down_sum = (
        lax.psum_scatter(gain_one_part, "narrow", scatter_dimension=0, tiled=True),
        lax.psum_scatter(in_part, "narrow", scatter_dimension=0, tiled=True),
        lax.psum_scatter(kernel_part, "narrow", scatter_dimension=1, tiled=True),
        lax.psum_scatter(out_part, "narrow", scatter_dimension=0, tiled=True),
        lax.psum_scatter(gain_two_part, "narrow", scatter_dimension=0, tiled=True),
        lax.psum_scatter(gate_part, "narrow", scatter_dimension=0, tiled=True),
        lax.psum_scatter(up_part, "narrow", scatter_dimension=0, tiled=True),
        lax.psum_scatter(down_part, "narrow", scatter_dimension=0, tiled=True),
    )
    block_out = jnp.stack(outputs, axis=0)
    input_grad = jnp.stack(input_grads, axis=0)
    return (
        block_out,
        input_grad,
        gain_one_sum,
        in_sum,
        kernel_sum,
        out_sum,
        gain_two_sum,
        gate_sum,
        up_sum,
        down_sum,
    )


MESH = pl.DeviceIdType.MESH
BF16, F32 = jnp.bfloat16, jnp.float32
VMEM_LIMIT = 62 * 1024 * 1024


def nn(a, b):
    return lax.dot_general(a, b, (((1,), (0,)), ((), ())), preferred_element_type=F32)


def nt(a, b):
    return lax.dot_general(a, b, (((1,), (1,)), ((), ())), preferred_element_type=F32)


def tn(a, b):
    return lax.dot_general(a, b, (((0,), (0,)), ((), ())), preferred_element_type=F32)


def column_tiles(total, most):
    units = total // 128
    best = max(u for u in range(1, units + 1) if units % u == 0 and u * 128 <= most)
    return [(start, best * 128) for start in range(0, total, best * 128)]


def row_scale(block):
    return lax.rsqrt(jnp.mean(block * block, axis=-1, keepdims=True) + EPSILON)


IN, OUT, GATE, UP, DOWN = range(5)
LANES = (0, 0, 1, 1)


def block_kernel(
    plan,
    tokens, seed, small, in_own, out_own, gate_own, up_own, down_own,
    block_out, input_grad, in_grad, out_grad, gate_grad, up_grad, down_grad, small_grad,
    w_in, w_out, w_gate, w_up, w_down, g_down,
    rx_in, rx_out, rx_gate, rx_up, rx_down,
    rz_in, rz_out, rz_gate, rz_up, rz_down,
    fin_in, fin_out, fin_gate, fin_up, fin_down,
    toks, seeds, normed_one, normed_two, out_seed,
    hidden, hidden_grad, own_out, own_grad,
    projected, gated, conv, mixed, branch, proj_seed,
    silu, slope, activated,
    core_send, core_recv, side_send, side_recv, keep,
    sum_in, sum_back,
    local_sem, a_send, a_recv, up_send, up_recv, dn_send, dn_recv, x_send, x_recv,
    gather_send, gather_recv, part_send, part_recv, halo_send, halo_recv,
    rx_send, rx_recv, rz_send, rz_recv, back_send, back_recv, tree_send, tree_recv, store_sem,
):
    Z, X, N, T, Q = plan["Z"], 2, 2, 4, plan["Z"] * 2
    L, D, FS, CS = plan["L"], plan["D"], plan["FS"], plan["CS"]
    HALF, GROUP = 2 * L, 4 * L
    wide, n = lax.axis_index("wide"), lax.axis_index("narrow")
    c, q = lax.rem(wide, 2), wide // 2
    x, z = lax.rem(q, X), q // X
    t = c * N + n

    def device(z_, x_, c_, n_):
        return ((z_ * X + x_) * 2 + c_, n_)

    over_core = device(z, x, 1 - c, n)
    over_side = device(z, x, c, 1 - n)
    over_both = device(z, x, 1 - c, 1 - n)
    over_x = device(z, 1 - x, c, n)
    z_ahead = [lax.rem(z + k, Z) for k in range(Z)]
    z_behind = [lax.rem(z - k + Z, Z) for k in range(Z)]
    q_next, q_prev = lax.rem(q + 1, Q), lax.rem(q - 1 + Q, Q)
    over_next, over_prev = (q_next * 2 + c, n), (q_prev * 2 + c, n)

    def remote(src, dst, send, recv, to):
        return pltpu.make_async_remote_copy(
            src_ref=src, dst_ref=dst, send_sem=send, recv_sem=recv, device_id=to, device_id_type=MESH
        )

    weights = (w_in, w_out, w_gate, w_up, w_down)
    grads = (w_in, w_out, w_gate, w_up, g_down)
    chunk_rows = [ref.shape[0] // Q for ref in weights]
    rx = (rx_in, rx_out, rx_gate, rx_up, rx_down)
    rz = (rz_in, rz_out, rz_gate, rz_up, rz_down)
    fin = (fin_in, fin_out, fin_gate, fin_up, fin_down)
    own_parts = {IN: in_own, GATE: gate_own, UP: up_own}
    piece = chunk_rows[IN] // T

    def chunk(refs, i, z_, x_):
        rows = chunk_rows[i]
        start = pl.multiple_of((z_ * X + x_) * rows, 16)
        return refs[i].at[pl.ds(start, rows), :]

    def block(ref, batch, member, rows=L):
        return ref.at[batch, pl.ds(pl.multiple_of(member * L, 16), rows), :]

    def own_rows(i):
        return weights[i].at[pl.ds(pl.multiple_of(q * chunk_rows[i] + t * piece, 16), piece), :]

    loads = [
        pltpu.make_async_copy(in_own.at[t], own_rows(IN), local_sem.at[0]),
        pltpu.make_async_copy(out_own, chunk(weights, OUT, z, x), local_sem.at[1]),
        pltpu.make_async_copy(gate_own.at[t], own_rows(GATE), local_sem.at[2]),
        pltpu.make_async_copy(up_own.at[t], own_rows(UP), local_sem.at[3]),
        pltpu.make_async_copy(down_own, chunk(weights, DOWN, z, x), local_sem.at[4]),
        pltpu.make_async_copy(small, sum_in.at[0], local_sem.at[5]),
        pltpu.make_async_copy(tokens.at[0], block(toks, 0, t), local_sem.at[6]),
        pltpu.make_async_copy(tokens.at[1], block(toks, 1, t), local_sem.at[7]),
        pltpu.make_async_copy(seed.at[0], block(seeds, 0, t), local_sem.at[8]),
        pltpu.make_async_copy(seed.at[1], block(seeds, 1, t), local_sem.at[9]),
    ]
    for load in loads:
        load.start()

    barrier = pltpu.get_barrier_semaphore()
    partners = [over_core, over_side, over_both, over_x, over_next, over_prev]
    partners += [device(z_ahead[k], x, c, n) for k in range(1, Z)]
    for partner in partners:
        pl.semaphore_signal(barrier, inc=1, device_id=partner, device_id_type=MESH)
    pl.semaphore_wait(barrier, len(partners))

    group = [(over_core, (1 - c) * N + n), (over_side, c * N + 1 - n), (over_both, (1 - c) * N + 1 - n)]

    def slices(i):
        s = (IN, GATE, UP).index(i)
        return [
            remote(own_parts[i].at[member], own_rows(i), a_send.at[s, k], a_recv.at[s, k], to)
            for k, (to, member) in enumerate(group)
        ]

    def gather_copies(ref, use, batch):
        mine = block(ref, batch, t)
        side = block(ref, batch, c * N + 1 - n)
        return (
            remote(mine, mine, gather_send.at[use, batch, 0], gather_recv.at[use, batch, 0], over_side),
            remote(mine, mine, gather_send.at[use, batch, 1], gather_recv.at[use, batch, 1], over_core),
            remote(side, side, gather_send.at[use, batch, 2], gather_recv.at[use, batch, 2], over_core),
        )

    def gather_start(ref, use, batch):
        to_side, to_core, _ = gather_copies(ref, use, batch)
        to_side.start()
        to_core.start()

    def gather_relay(ref, use, batch):
        to_side, _, relay = gather_copies(ref, use, batch)
        to_side.wait_recv()
        relay.start()

    def gather_finish(ref, use, batch):
        to_side, to_core, relay = gather_copies(ref, use, batch)
        to_core.wait_recv()
        relay.wait_recv()
        for copy in (to_side, to_core, relay):
            copy.wait_send()

    def tree_copies(ref, use):
        found = [
            remote(ref.at[r], ref.at[4 + r], tree_send.at[use, r], tree_recv.at[use, r], to)
            for r, to in enumerate((over_core, over_side, over_x))
        ]
        for k in range(1, Z):
            found.append(
                remote(
                    ref.at[3], ref.at[6 + k], tree_send.at[use, 2 + k], tree_recv.at[use, 2 + k],
                    device(z_ahead[k], x, c, n),
                )
            )
        return found

    def tree_step(ref, use, r):
        copies = tree_copies(ref, use)
        copies[r].wait_recv()
        ref[r + 1] = ref[r] + ref[4 + r]
        if r < 2:
            copies[r + 1].start()
        else:
            for copy in copies[3:]:
                copy.start()

    def tree_finish(ref, use):
        copies = tree_copies(ref, use)
        total = ref[3]
        for k in range(1, Z):
            copies[2 + k].wait_recv()
            total = total + ref[6 + k]
        for copy in copies:
            copy.wait_send()
        return total

    def z_copy(i, j, line, upward):
        if upward:
            src_z, to, send, recv = z - (j - 1), device(z + 1, line_x(0), c, n), up_send, up_recv
        else:
            src_z, to, send, recv = z + (j - 1), device(z - 1, line_x(0), c, n), dn_send, dn_recv
        part = chunk(weights, i, src_z, line_x(line))
        return remote(part, part, send.at[i, j - 1, line], recv.at[i, j - 1, line], to)

    def z_arrival(i, j, line, upward):
        src_z = z - j if upward else z + j
        part = chunk(weights, i, src_z, line_x(line))
        send, recv = (up_send, up_recv) if upward else (dn_send, dn_recv)
        return remote(part, part, send.at[i, j - 1, line], recv.at[i, j - 1, line], over_x)

    def line_x(line):
        return x if line == 0 else 1 - x

    def z_launch(i, line):
        @pl.when(z < Z - 1)
        def _():
            z_copy(i, 1, line, True).start()

        @pl.when(z > 0)
        def _():
            z_copy(i, 1, line, False).start()

    def x_copy(i, z_, arrival=False):
        part = chunk(weights, i, z_, 1 - x if arrival else x)
        return remote(part, part, x_send.at[i, z_], x_recv.at[i, z_], over_x)

    def z_pass(i, j, line, to_x):
        @pl.when(z - j >= 0)
        def _():
            z_arrival(i, j, line, True).wait_recv()
            if j < Z - 1:
                @pl.when(z < Z - 1)
                def _():
                    z_copy(i, j + 1, line, True).start()
            if to_x:
                x_copy(i, z - j).start()

        @pl.when(z + j <= Z - 1)
        def _():
            z_arrival(i, j, line, False).wait_recv()
            if j < Z - 1:
                @pl.when(z > 0)
                def _():
                    z_copy(i, j + 1, line, False).start()
            if to_x:
                x_copy(i, z + j).start()

    def z_settle(i, line):
        for j in range(1, Z):
            @pl.when((z < Z - 1) & (z - (j - 1) >= 0))
            def _():
                z_copy(i, j, line, True).wait_send()

            @pl.when((z > 0) & (z + (j - 1) <= Z - 1))
            def _():
                z_copy(i, j, line, False).wait_send()

    def x_arrive(i):
        for z_ in range(Z):
            x_copy(i, z_, True).wait_recv()

    def x_settle(i):
        for z_ in range(Z):
            x_copy(i, z_).wait_send()

    def part_copies(use, batch):
        lane = LANES[use]
        return (
            remote(
                core_send.at[batch], core_recv.at[lane, batch],
                part_send.at[use, batch, 0], part_recv.at[use, batch, 0], over_core,
            ),
            remote(
                side_send.at[batch], side_recv.at[lane, batch],
                part_send.at[use, batch, 1], part_recv.at[use, batch, 1], over_side,
            ),
        )

    def parts_begin(use, product):
        for batch in range(2):
            def put(cols, value, batch=batch):
                core_send[batch, :, cols] = value.astype(BF16)

            product(batch, (1 - c) * HALF, put)
            part_copies(use, batch)[0].start()
        for batch in range(2):
            def put(cols, value, batch=batch):
                keep[batch, :, cols] = value

            product(batch, c * HALF, put)

    def parts_middle(use):
        lane = LANES[use]
        for batch in range(2):
            to_core, to_side = part_copies(use, batch)
            to_core.wait_recv()
            rows = pl.ds(pl.multiple_of((1 - n) * L, 16), L)
            side_send[batch] = (
                keep[batch, rows, :] + core_recv[lane, batch, rows, :].astype(F32)
            ).astype(BF16)
            to_side.start()

    def parts_end(use, batch):
        lane = LANES[use]
        to_core, to_side = part_copies(use, batch)
        to_side.wait_recv()
        rows = pl.ds(pl.multiple_of(n * L, 16), L)
        total = (
            keep[batch, rows, :]
            + core_recv[lane, batch, rows, :].astype(F32)
            + side_recv[lane, batch].astype(F32)
        )
        to_core.wait_send()
        to_side.wait_send()
        return total

    def rx_copy(i, z_):
        return remote(chunk(grads, i, z_, 1 - x), rx[i].at[z_], rx_send.at[i, z_], rx_recv.at[i, z_], over_x)

    def rz_copy(i, k):
        return remote(
            chunk(grads, i, z_ahead[k], x), rz[i].at[k - 1], rz_send.at[i, k - 1], rz_recv.at[i, k - 1],
            device(z_ahead[k], x, c, n),
        )

    def reduce_start(i):
        for k in list(range(1, Z)) + [0]:
            rx_copy(i, z_ahead[k]).start()

    def reduce_pass(i):
        for k in range(1, Z):
            z_ = z_ahead[k]
            rx_copy(i, z_).wait_recv()
            part = chunk(grads, i, z_, x)
            part[...] = (part[...].astype(F32) + rx[i][z_].astype(F32)).astype(BF16)
            rz_copy(i, k).start()

    def reduce_end(i):
        rx_copy(i, z).wait_recv()
        total = chunk(grads, i, z, x)[...].astype(F32) + rx[i][z].astype(F32)
        for k in range(1, Z):
            rz_copy(i, k).wait_recv()
            total = total + rz[i][k - 1].astype(F32)
        fin[i][...] = total
        for z_ in range(Z):
            rx_copy(i, z_).wait_send()
        for k in range(1, Z):
            rz_copy(i, k).wait_send()

    results = {IN: in_grad, GATE: gate_grad, UP: up_grad, OUT: out_grad, DOWN: down_grad}

    def back_copies(i):
        s = (IN, GATE, UP).index(i)
        own = fin[i].at[pl.ds(pl.multiple_of(t * piece, 8), piece), :]
        found = [pltpu.make_async_copy(own, results[i].at[t], store_sem.at[i])]
        for k, (to, member) in enumerate(group):
            part = fin[i].at[pl.ds(pl.multiple_of(member * piece, 8), piece), :]
            found.append(remote(part, results[i].at[t], back_send.at[s, k], back_recv.at[s, k], to))
        return found

    def back_arrivals(i):
        s = (IN, GATE, UP).index(i)
        found = []
        for k, (to, member) in enumerate(group):
            part = fin[i].at[pl.ds(pl.multiple_of(member * piece, 8), piece), :]
            found.append(remote(part, results[i].at[member], back_send.at[s, k], back_recv.at[s, k], to))
        return found

    def store_start(i):
        if i in own_parts:
            for copy in back_copies(i):
                copy.start()
        else:
            pltpu.make_async_copy(fin[i], results[i], store_sem.at[i]).start()

    def store_finish(i):
        if i in own_parts:
            copies = back_copies(i)
            copies[0].wait()
            for copy in copies[1:]:
                copy.wait_send()
            for copy in back_arrivals(i):
                copy.wait_recv()
        else:
            pltpu.make_async_copy(fin[i], results[i], store_sem.at[i]).wait()

    for copy in slices(IN):
        copy.start()
    loads[5].wait()
    tree_copies(sum_in, 0)[0].start()
    for load in loads[6:8]:
        load.wait()
    for batch in range(2):
        gather_start(toks, 0, batch)
    loads[1].wait()
    z_launch(OUT, 0)
    x_copy(OUT, z).start()
    for i in (GATE, UP):
        for copy in slices(i):
            copy.start()
    loads[0].wait()
    for copy in slices(IN):
        copy.wait_recv()
    x_copy(IN, z).start()
    z_launch(IN, 0)
    loads[2].wait()
    for copy in slices(GATE):
        copy.wait_recv()
    x_copy(GATE, z).start()
    loads[3].wait()
    for copy in slices(UP):
        copy.wait_recv()
    x_copy(UP, z).start()
    loads[4].wait()
    x_copy(DOWN, z).start()
    tree_step(sum_in, 0, 0)
    x_copy(IN, z, True).wait_recv()
    z_launch(IN, 1)
    z_launch(GATE, 0)
    z_launch(UP, 0)
    z_launch(DOWN, 0)
    loads[8].wait()
    loads[9].wait()
    for batch in range(2):
        gather_start(seeds, 1, batch)
    tree_step(sum_in, 0, 1)
    gather_relay(toks, 0, 0)
    gather_relay(toks, 0, 1)
    tree_step(sum_in, 0, 2)
    z_pass(OUT, 1, 0, True)
    z_pass(IN, 1, 0, False)
    z_pass(IN, 1, 1, False)
    sum_in[0] = tree_finish(sum_in, 0)

    def norm_rows(ref, gain):
        block_ = ref.astype(F32)
        return (block_ * row_scale(block_) * gain).astype(BF16)

    for batch in range(2):
        gather_finish(toks, 0, batch)

        @pl.loop(0, GROUP // 64)
        def _(step, batch=batch):
            rows = pl.ds(pl.multiple_of(step * 64, 64), 64)
            normed_one[batch, rows, :] = norm_rows(toks[batch, rows, :], sum_in[0, 0:1, :])

    for j in range(2, Z):
        z_pass(IN, j, 0, False)
        z_pass(IN, j, 1, False)
        z_pass(OUT, j, 0, True)

    for batch in range(2):
        for start, size in column_tiles(3 * CS, 256):
            projected[batch, :, start : start + size] = nn(normed_one[batch], w_in[:, start : start + size])
        gated[batch, 8 : 8 + GROUP, :] = projected[batch, :, :CS] * projected[batch, :, 2 * CS :]

    def halo_copies(batch):
        ahead = remote(
            gated.at[batch, pl.ds(GROUP, 8), :], gated.at[batch, pl.ds(0, 8), :],
            halo_send.at[0, batch], halo_recv.at[0, batch], over_next,
        )
        back = remote(
            conv.at[batch, pl.ds(0, 8), :], conv.at[batch, pl.ds(GROUP, 8), :],
            halo_send.at[1, batch], halo_recv.at[1, batch], over_prev,
        )
        return ahead, back

    for batch in range(2):
        halo_copies(batch)[0].start()
    gather_relay(seeds, 1, 0)
    gather_relay(seeds, 1, 1)
    taps = sum_in[0, 2:5, pl.ds(pl.multiple_of(t * CS, 128), CS)]
    for batch in range(2):
        halo_copies(batch)[0].wait_recv()

        @pl.when(q == 0)
        def _():
            gated[batch, 0:8, :] = jnp.zeros((8, CS), F32)

        for r in range(0, GROUP, HALF):
            value = (
                taps[0:1] * gated[batch, r + 6 : r + 6 + HALF, :]
                + taps[1:2] * gated[batch, r + 7 : r + 7 + HALF, :]
                + taps[2:3] * gated[batch, r + 8 : r + 8 + HALF, :]
            )
            mixed[batch, r : r + HALF, :] = value
            branch[batch, r : r + HALF, :] = (projected[batch, r : r + HALF, CS : 2 * CS] * value).astype(BF16)
    x_arrive(OUT)

    def product_out(batch, start, put):
        rows = pl.ds(pl.multiple_of(start, 16), HALF)
        for at, size in column_tiles(D, 512):
            put(slice(at, at + size), nn(branch[batch, rows, :], w_out[:, at : at + size]))

    parts_begin(0, product_out)
    parts_middle(0)
    z_pass(GATE, 1, 0, True)
    for batch in range(2):
        mine = pl.ds(pl.multiple_of(t * L, 16), L)
        hidden[batch] = toks[batch, mine, :].astype(F32) + parts_end(0, batch)
        normed_two[batch, mine, :] = norm_rows(hidden[batch], sum_in[0, 1:2, :])
        gather_start(normed_two, 2, batch)
    z_pass(UP, 1, 0, True)
    z_pass(GATE, 2, 0, True)
    gather_relay(normed_two, 2, 0)
    gather_relay(normed_two, 2, 1)
    z_pass(UP, 2, 0, True)
    if Z > 3:
        for j in range(3, Z):
            z_pass(GATE, j, 0, True)
            z_pass(UP, j, 0, True)
    z_pass(DOWN, 1, 0, True)
    for batch in range(2):
        gather_finish(normed_two, 2, batch)
        gather_finish(seeds, 1, batch)

    x_arrive(GATE)
    x_arrive(UP)
    for batch in range(2):
        for r in range(0, GROUP, HALF):
            for start, size in column_tiles(FS, 384):
                cols = slice(start, start + size)
                rows = slice(r, r + HALF)
                left = normed_two[batch, rows, :]
                gate = nn(left, w_gate[:, cols])
                up = nn(left, w_up[:, cols])
                sig = 1.0 / (1.0 + jnp.exp(-gate))
                act = gate * sig
                silu[batch, rows, cols] = act.astype(BF16)
                slope[batch, rows, cols] = (up * sig * (1.0 + gate * (1.0 - sig))).astype(BF16)
                activated[batch, rows, cols] = (act * up).astype(BF16)
        if batch == 0:
            for j in range(2, Z):
                z_pass(DOWN, j, 0, True)

    def weight_grad(dst, left, right, most_rows, most_cols):
        for a, rows in column_tiles(dst.shape[0], most_rows):
            for b, cols in column_tiles(dst.shape[1], most_cols):
                value = tn(left[0, :, a : a + rows], right[0, :, b : b + cols])
                value = value + tn(left[1, :, a : a + rows], right[1, :, b : b + cols])
                dst[a : a + rows, b : b + cols] = value.astype(BF16)

    weight_grad(g_down, activated, seeds, 384, 512)
    reduce_start(DOWN)
    x_arrive(DOWN)

    for batch in range(2):
        for r in range(0, GROUP, HALF):
            for start, size in column_tiles(FS, 384):
                cols = slice(start, start + size)
                rows = slice(r, r + HALF)
                act_grad = nt(seeds[batch, rows, :], w_down[cols, :])
                silu[batch, rows, cols] = (act_grad * silu[batch, rows, cols].astype(F32)).astype(BF16)
                slope[batch, rows, cols] = (act_grad * slope[batch, rows, cols].astype(F32)).astype(BF16)
    up_seed, gate_seed = silu, slope

    def product_ffn(batch, start, put):
        rows = pl.ds(pl.multiple_of(start, 16), HALF)
        for at, size in column_tiles(D, 512):
            put(
                slice(at, at + size),
                nt(gate_seed[batch, rows, :], w_gate[at : at + size, :])
                + nt(up_seed[batch, rows, :], w_up[at : at + size, :]),
            )

    def product_down(batch, start, put):
        rows = pl.ds(pl.multiple_of(start, 16), HALF)
        for at, size in column_tiles(D, 512):
            put(slice(at, at + size), nn(activated[batch, rows, :], w_down[:, at : at + size]))

    parts_begin(2, product_ffn)
    parts_middle(2)
    for i, line in ((IN, 0), (IN, 1), (OUT, 0), (GATE, 0), (UP, 0), (DOWN, 0)):
        z_settle(i, line)
    x_copy(IN, z).wait_send()
    for i in (OUT, GATE, UP, DOWN):
        x_settle(i)
    for i in (IN, GATE, UP):
        for copy in slices(i):
            copy.wait_send()
    weight_grad(w_gate, normed_two, gate_seed, 256, 384)
    reduce_start(GATE)
    weight_grad(w_up, normed_two, up_seed, 256, 384)
    reduce_start(UP)
    gain_two = jnp.zeros((1, D), F32)
    for batch in range(2):
        mine = pl.ds(pl.multiple_of(t * L, 16), L)
        n2g = parts_end(2, batch)
        hid = hidden[batch]
        scale = row_scale(hid)
        gain_two = gain_two + jnp.sum(n2g * hid * scale, axis=0, keepdims=True)
        scaled = n2g * sum_in[0, 1:2, :]
        value = (
            seeds[batch, mine, :].astype(F32)
            + scale * scaled
            - hid * (scale * scale * scale) * jnp.mean(scaled * hid, axis=-1, keepdims=True)
        )
        hidden_grad[batch] = value
        out_seed[batch, mine, :] = value.astype(BF16)
        gather_start(out_seed, 3, batch)
    sum_back[0] = jnp.zeros((8, D), F32)
    sum_back[0, 1:2, :] = gain_two
    parts_begin(1, product_down)
    gather_relay(out_seed, 3, 0)
    gather_relay(out_seed, 3, 1)
    parts_middle(1)
    reduce_pass(DOWN)
    for batch in range(2):
        gather_finish(out_seed, 3, batch)

    for batch in range(2):
        for r in range(0, GROUP, HALF):
            rows = slice(r, r + HALF)
            branch_grad = nt(out_seed[batch, rows, :], w_out[...])
            conv_grad = branch_grad * projected[batch, rows, CS : 2 * CS]
            conv[batch, rows, :] = conv_grad
            proj_seed[batch, rows, CS : 2 * CS] = (branch_grad * mixed[batch, rows, :]).astype(BF16)
        halo_copies(batch)[1].start()
    kernel_grad = [jnp.zeros((1, CS), F32) for _ in range(3)]
    for batch in range(2):
        for r in range(0, GROUP, HALF):
            conv_grad = conv[batch, r : r + HALF, :]
            for k in range(3):
                kernel_grad[k] = kernel_grad[k] + jnp.sum(
                    conv_grad * gated[batch, r + 6 + k : r + 6 + k + HALF, :], axis=0, keepdims=True
                )
    for k in range(3):
        sum_back[0, 2 + k : 3 + k, pl.ds(pl.multiple_of(t * CS, 128), CS)] = kernel_grad[k]
    weight_grad(w_out, branch, out_seed, 256, 512)
    reduce_start(OUT)
    for batch in range(2):
        halo_copies(batch)[1].wait_recv()

        @pl.when(q == Q - 1)
        def _():
            conv[batch, GROUP : GROUP + 8, :] = jnp.zeros((8, CS), F32)

        for r in range(0, GROUP, HALF):
            rows = slice(r, r + HALF)
            value = (
                taps[2:3] * conv[batch, r : r + HALF, :]
                + taps[1:2] * conv[batch, r + 1 : r + 1 + HALF, :]
                + taps[0:1] * conv[batch, r + 2 : r + 2 + HALF, :]
            )
            proj_seed[batch, rows, :CS] = (value * projected[batch, rows, 2 * CS :]).astype(BF16)
            proj_seed[batch, rows, 2 * CS :] = (value * projected[batch, rows, :CS]).astype(BF16)

    for batch in range(2):
        own_out[batch] = (hidden[batch] + parts_end(1, batch)).astype(BF16)
    out_copy = pltpu.make_async_copy(own_out, block_out, local_sem.at[0])
    out_copy.start()

    def product_in(batch, start, put):
        rows = pl.ds(pl.multiple_of(start, 16), HALF)
        for at, size in column_tiles(D, 512):
            put(slice(at, at + size), nt(proj_seed[batch, rows, :], w_in[at : at + size, :]))

    parts_begin(3, product_in)
    parts_middle(3)
    weight_grad(w_in, normed_one, proj_seed, 256, 384)
    reduce_start(IN)
    reduce_pass(GATE)
    gain_one = jnp.zeros((1, D), F32)
    for batch in range(2):
        mine = pl.ds(pl.multiple_of(t * L, 16), L)
        n1g = parts_end(3, batch)
        inputs = toks[batch, mine, :].astype(F32)
        scale = row_scale(inputs)
        gain_one = gain_one + jnp.sum(n1g * inputs * scale, axis=0, keepdims=True)
        scaled = n1g * sum_in[0, 0:1, :]
        own_grad[batch] = (
            hidden_grad[batch]
            + scale * scaled
            - inputs * (scale * scale * scale) * jnp.mean(scaled * inputs, axis=-1, keepdims=True)
        )
    grad_copy = pltpu.make_async_copy(own_grad, input_grad, local_sem.at[1])
    grad_copy.start()
    sum_back[0, 0:1, :] = gain_one
    tree_copies(sum_back, 1)[0].start()
    reduce_end(DOWN)
    store_start(DOWN)
    tree_step(sum_back, 1, 0)
    reduce_pass(UP)
    tree_step(sum_back, 1, 1)
    reduce_end(GATE)
    store_start(GATE)
    tree_step(sum_back, 1, 2)
    reduce_pass(OUT)
    reduce_pass(IN)
    reduce_end(UP)
    store_start(UP)
    sum_back[0] = tree_finish(sum_back, 1)
    small_copy = pltpu.make_async_copy(sum_back.at[0], small_grad, local_sem.at[2])
    small_copy.start()
    reduce_end(OUT)
    store_start(OUT)
    reduce_end(IN)
    store_start(IN)
    for batch in range(2):
        for copy in halo_copies(batch):
            copy.wait_send()
    for i in (DOWN, GATE, UP, OUT, IN):
        store_finish(i)
    out_copy.wait()
    grad_copy.wait()
    small_copy.wait()


def fused(plan, tokens, cotangent, lengths, loss_mask, norm_gain, in_weight, conv_kernel, out_weight, ffn_gain, gate_weight, up_weight, down_weight):
    Z, Q, T = plan["Z"], plan["Q"], 4
    L, D, FS, CS = plan["L"], plan["D"], plan["FS"], plan["CS"]
    width, hid = D // (Q * T), FS // Q
    wide, n = lax.axis_index("wide"), lax.axis_index("narrow")
    c, q = wide % 2, wide // 2
    t = c * 2 + n
    place = wide * 2 + n
    positions = place * L + jnp.arange(L, dtype=jnp.int32)
    valid = (positions[None, :] < lengths[:, None]) & (loss_mask != 0)
    seed = jnp.where(valid[:, :, None], cotangent, jnp.zeros((), cotangent.dtype))
    small = jnp.zeros((8, D), F32)
    small = lax.dynamic_update_slice(
        small, jnp.stack([norm_gain, ffn_gain]).astype(F32), (0, place * width)
    )
    small = lax.dynamic_update_slice(small, conv_kernel.astype(F32), (2, t * CS + q * width))
    rows = in_weight.shape[0]
    in_own = in_weight.reshape(rows, 3, Q, T, width).transpose(3, 0, 1, 2, 4).reshape(T, rows, 3 * CS)
    gate_own = gate_weight.reshape(rows, Q, T, hid).transpose(2, 0, 1, 3).reshape(T, rows, FS)
    up_own = up_weight.reshape(rows, Q, T, hid).transpose(2, 0, 1, 3).reshape(T, rows, FS)

    shapes = [(T * rows, 3 * CS), (width, D), (T * rows, FS), (T * rows, FS), (hid, D)]
    vm, dma = pltpu.VMEM, pltpu.SemaphoreType.DMA
    group = 4 * L
    scratch = [vm((Q * r, k), BF16) for r, k in shapes]
    scratch += [vm((Q * hid, D), BF16)]
    scratch += [vm((Z, r, k), BF16) for r, k in shapes]
    scratch += [vm((Z - 1, r, k), BF16) for r, k in shapes]
    scratch += [vm((r, k), F32) for r, k in shapes]
    scratch += [vm((2, group, D), BF16) for _ in range(5)]
    scratch += [vm((2, L, D), F32), vm((2, L, D), F32), vm((2, L, D), BF16), vm((2, L, D), F32)]
    scratch += [
        vm((2, group, 3 * CS), F32), vm((2, group + 8, CS), F32), vm((2, group + 8, CS), F32),
        vm((2, group, CS), F32), vm((2, group, CS), BF16), vm((2, group, 3 * CS), BF16),
    ]
    scratch += [vm((2, group, FS), BF16) for _ in range(3)]
    scratch += [
        vm((2, 2 * L, D), BF16), vm((2, 2, 2 * L, D), BF16),
        vm((2, L, D), BF16), vm((2, 2, L, D), BF16), vm((2, 2 * L, D), F32),
    ]
    scratch += [vm((6 + Z, 8, D), F32), vm((6 + Z, 8, D), F32)]
    scratch += [
        dma((10,)), dma((3, 3)), dma((3, 3)),
        dma((5, Z - 1, 2)), dma((5, Z - 1, 2)), dma((5, Z - 1, 2)), dma((5, Z - 1, 2)),
        dma((5, Z)), dma((5, Z)),
        dma((4, 2, 3)), dma((4, 2, 3)), dma((4, 2, 2)), dma((4, 2, 2)), dma((2, 2)), dma((2, 2)),
        dma((5, Z)), dma((5, Z)), dma((5, Z - 1)), dma((5, Z - 1)), dma((3, 3)), dma((3, 3)),
        dma((2, 2 + Z)), dma((2, 2 + Z)), dma((5,)),
    ]
    out_shape = (
        jax.ShapeDtypeStruct((2, L, D), BF16),
        jax.ShapeDtypeStruct((2, L, D), F32),
        jax.ShapeDtypeStruct((T, rows, 3 * CS), F32),
        jax.ShapeDtypeStruct((width, D), F32),
        jax.ShapeDtypeStruct((T, rows, FS), F32),
        jax.ShapeDtypeStruct((T, rows, FS), F32),
        jax.ShapeDtypeStruct((hid, D), F32),
        jax.ShapeDtypeStruct((8, D), F32),
    )
    block_out, input_grad, in_g, out_g, gate_g, up_g, down_g, small_g = pl.pallas_call(
        functools.partial(block_kernel, plan),
        out_shape=out_shape,
        in_specs=[pl.BlockSpec(memory_space=pl.ANY)] * 8,
        out_specs=[pl.BlockSpec(memory_space=pl.ANY)] * 8,
        scratch_shapes=scratch,
        compiler_params=pltpu.CompilerParams(
            collective_id=0, has_side_effects=True, vmem_limit_bytes=VMEM_LIMIT
        ),
    )(tokens, seed, small, in_own, out_weight, gate_own, up_own, down_weight)
    in_g = in_g.reshape(T, rows, 3, Q, width).transpose(1, 2, 3, 0, 4).reshape(rows, 3 * D)
    gate_g = gate_g.reshape(T, rows, Q, hid).transpose(1, 2, 0, 3).reshape(rows, T * FS)
    up_g = up_g.reshape(T, rows, Q, hid).transpose(1, 2, 0, 3).reshape(rows, T * FS)
    gains = lax.dynamic_slice(small_g, (0, place * width), (2, width))
    taps = lax.dynamic_slice(small_g, (2, t * CS + q * width), (3, width))
    return block_out, input_grad, gains[0], in_g, taps, out_g, gains[1], gate_g, up_g, down_g


def planned(wide, narrow, arrays):
    tokens, in_weight, down_weight = arrays[0], arrays[5], arrays[11]
    if narrow != 2 or wide % 4 or wide < 8 or tokens.shape[0] != 2:
        return None
    groups = wide // 2
    rows, hid = in_weight.shape[0], down_weight.shape[0]
    sizes = {
        "Z": groups // 2, "Q": groups, "L": tokens.shape[1], "D": tokens.shape[2],
        "FS": hid * groups, "CS": rows * groups,
    }
    if rows % 16 or hid % 16 or sizes["L"] % 64 or sizes["FS"] % 128 or sizes["CS"] % 128:
        return None
    return sizes


def solution(mesh):
    in_specs = (
        P(None, ("wide", "narrow"), None),
        P(None, ("wide", "narrow"), None),
        P(),
        P(None, ("wide", "narrow")),
        P(("wide", "narrow")),
        P(("wide", "narrow"), None),
        P(None, ("wide", "narrow")),
        P(("wide", "narrow"), None),
        P(("wide", "narrow")),
        P(("wide", "narrow"), None),
        P(("wide", "narrow"), None),
        P(("wide", "narrow"), None),
    )
    out_specs = (
        P(None, ("wide", "narrow"), None),
        P(None, ("wide", "narrow"), None),
        P(("wide", "narrow")),
        P(("wide", "narrow"), None),
        P(None, ("wide", "narrow")),
        P(("wide", "narrow"), None),
        P(("wide", "narrow")),
        P(("wide", "narrow"), None),
        P(("wide", "narrow"), None),
        P(("wide", "narrow"), None),
    )
    wide, narrow = mesh.shape["wide"], mesh.shape["narrow"]

    def step(*arrays):
        plan = planned(wide, narrow, arrays)
        run = body if plan is None else functools.partial(fused, plan)
        return run(*arrays)

    return jax.shard_map(step, mesh=mesh, in_specs=in_specs, out_specs=out_specs, check_vma=False)
```

```python
import functools

import jax
import jax.numpy as jnp
from jax import lax
from jax.experimental import pallas as pl
from jax.experimental.pallas import tpu as pltpu
from jax.sharding import PartitionSpec as P

EPSILON = 1e-05


def shifted(block, axis, distance):
    devices = range(lax.axis_size(axis))
    route = [(i - distance, i) for i in devices if i - distance in devices]
    return lax.ppermute(block, axis, route)


def along_rows(left, weight):
    return lax.dot_general(
        left, weight, (((1,), (1,)), ((), ())), preferred_element_type=jnp.float32
    )


def over_rows(left, right):
    return lax.dot_general(
        left, right, (((0,), (0,)), ((), ())), preferred_element_type=jnp.float32
    )


def collect(shards):
    partial_set = (
        lax.all_gather(shards[0], "narrow", axis=0, tiled=True),
        lax.all_gather(shards[1], "narrow", axis=0, tiled=True),
        lax.all_gather(shards[2], "narrow", axis=1, tiled=True),
        lax.all_gather(shards[3], "narrow", axis=0, tiled=True),
        lax.all_gather(shards[4], "narrow", axis=0, tiled=True),
        lax.all_gather(shards[5], "narrow", axis=0, tiled=True),
        lax.all_gather(shards[6], "narrow", axis=0, tiled=True),
        lax.all_gather(shards[7], "narrow", axis=0, tiled=True),
    )
    return (
        lax.all_gather(partial_set[0], "wide", axis=0, tiled=True),
        lax.all_gather(partial_set[1], "wide", axis=0, tiled=True),
        lax.all_gather(partial_set[2], "wide", axis=1, tiled=True),
        lax.all_gather(partial_set[3], "wide", axis=0, tiled=True),
        lax.all_gather(partial_set[4], "wide", axis=0, tiled=True),
        lax.all_gather(partial_set[5], "wide", axis=0, tiled=True),
        lax.all_gather(partial_set[6], "wide", axis=0, tiled=True),
        lax.all_gather(partial_set[7], "wide", axis=0, tiled=True),
    )


def collect_tied(shards, anchor):
    tied_shards, _ = lax.optimization_barrier((shards, anchor))
    return collect(tied_shards)


def body(
    tokens,
    cotangent,
    lengths,
    loss_mask,
    norm_gain,
    in_weight,
    conv_kernel,
    out_weight,
    ffn_gain,
    gate_weight,
    up_weight,
    down_weight,
):
    micro_count = tokens.shape[0]
    local_rows = tokens.shape[1]
    width = tokens.shape[2]
    shards = (
        norm_gain,
        in_weight,
        conv_kernel,
        out_weight,
        ffn_gain,
        gate_weight,
        up_weight,
        down_weight,
    )
    positions = lax.axis_index(("wide", "narrow")) * local_rows + jnp.arange(
        local_rows, dtype=jnp.int32
    )
    gain_one_grad = jnp.zeros((width,), jnp.float32)
    gain_two_grad = jnp.zeros((width,), jnp.float32)
    kernel_grad = jnp.zeros((3, width), jnp.float32)
    outputs = []
    input_grads = []
    kept_normed_one = []
    kept_proj_seed = []
    kept_branch = []
    kept_out_seed = []
    kept_normed_two = []
    kept_gate_seed = []
    kept_up_seed = []
    kept_activated = []
    kept_down_seed = []
    for batch in range(micro_count):
        gathered = collect_tied(shards, tokens[batch])
        gain_full, in_full, kernel_full, out_full, ffn_full, gate_full, up_full, down_full = (
            gathered
        )
        gain_f32 = gain_full.astype(jnp.float32)
        ffn_f32 = ffn_full.astype(jnp.float32)
        kernel_f32 = kernel_full.astype(jnp.float32)
        inputs = tokens[batch].astype(jnp.float32)
        scale_one = lax.rsqrt(jnp.mean(inputs * inputs, axis=-1, keepdims=True) + EPSILON)
        normed_one = (inputs * scale_one * gain_f32).astype(jnp.bfloat16)
        projected = jnp.dot(normed_one, in_full, preferred_element_type=jnp.float32)
        b_gate = projected[:, :width]
        c_gate = projected[:, width : 2 * width]
        conv_input = projected[:, 2 * width :]
        gated_input = b_gate * conv_input
        earlier = shifted(gated_input[local_rows - 2 :], ("wide", "narrow"), 1)
        padded = jnp.concatenate([earlier, gated_input], axis=0)
        mixed_conv = (
            kernel_f32[0] * padded[:-2] + kernel_f32[1] * padded[1:-1] + kernel_f32[2] * gated_input
        )
        branch = (c_gate * mixed_conv).astype(jnp.bfloat16)
        hidden = inputs + jnp.dot(branch, out_full, preferred_element_type=jnp.float32)
        scale_two = lax.rsqrt(jnp.mean(hidden * hidden, axis=-1, keepdims=True) + EPSILON)
        normed_two = (hidden * scale_two * ffn_f32).astype(jnp.bfloat16)
        gate_out = jnp.dot(normed_two, gate_full, preferred_element_type=jnp.float32)
        up_out = jnp.dot(normed_two, up_full, preferred_element_type=jnp.float32)
        sigmoid_gate = jax.nn.sigmoid(gate_out)
        silu_gate = gate_out * sigmoid_gate
        activated = (silu_gate * up_out).astype(jnp.bfloat16)
        result = hidden + jnp.dot(activated, down_full, preferred_element_type=jnp.float32)
        outputs.append(result.astype(jnp.bfloat16))
        validity = (positions < lengths[batch]).astype(jnp.float32) * loss_mask[batch].astype(
            jnp.float32
        )
        seed = cotangent[batch].astype(jnp.float32) * validity[:, None]
        down_seed = seed.astype(jnp.bfloat16)
        act_grad = along_rows(down_seed, down_full)
        up_seed = (act_grad * silu_gate).astype(jnp.bfloat16)
        gate_seed = (
            act_grad * up_out * sigmoid_gate * (1.0 + gate_out * (1.0 - sigmoid_gate))
        ).astype(jnp.bfloat16)
        normed_two_grad = along_rows(gate_seed, gate_full) + along_rows(up_seed, up_full)
        gain_two_grad = gain_two_grad + jnp.sum(normed_two_grad * hidden * scale_two, axis=0)
        scaled_two = normed_two_grad * ffn_f32
        hidden_grad = (
            seed
            + scale_two * scaled_two
            - hidden
            * (scale_two * scale_two * scale_two)
            * jnp.mean(scaled_two * hidden, axis=-1, keepdims=True)
        )
        out_seed = hidden_grad.astype(jnp.bfloat16)
        branch_grad = along_rows(out_seed, out_full)
        c_grad = branch_grad * mixed_conv
        conv_grad = branch_grad * c_gate
        kernel_grad = kernel_grad + jnp.stack(
            [
                jnp.sum(conv_grad * padded[:-2], axis=0),
                jnp.sum(conv_grad * padded[1:-1], axis=0),
                jnp.sum(conv_grad * gated_input, axis=0),
            ],
            axis=0,
        )
        later = shifted(conv_grad[:2], ("wide", "narrow"), -1)
        extended = jnp.concatenate([conv_grad, later], axis=0)
        gated_grad = (
            kernel_f32[2] * conv_grad
            + kernel_f32[1] * extended[1 : local_rows + 1]
            + kernel_f32[0] * extended[2:]
        )
        proj_seed = jnp.concatenate(
            [gated_grad * conv_input, c_grad, gated_grad * b_gate], axis=1
        ).astype(jnp.bfloat16)
        normed_one_grad = along_rows(proj_seed, in_full)
        gain_one_grad = gain_one_grad + jnp.sum(normed_one_grad * inputs * scale_one, axis=0)
        scaled_one = normed_one_grad * gain_f32
        input_grads.append(
            hidden_grad
            + scale_one * scaled_one
            - inputs
            * (scale_one * scale_one * scale_one)
            * jnp.mean(scaled_one * inputs, axis=-1, keepdims=True)
        )
        kept_normed_one.append(normed_one)
        kept_proj_seed.append(proj_seed)
        kept_branch.append(branch)
        kept_out_seed.append(out_seed)
        kept_normed_two.append(normed_two)
        kept_gate_seed.append(gate_seed)
        kept_up_seed.append(up_seed)
        kept_activated.append(activated)
        kept_down_seed.append(down_seed)
    all_normed_two = jnp.concatenate(kept_normed_two, axis=0)
    in_grad = over_rows(
        jnp.concatenate(kept_normed_one, axis=0), jnp.concatenate(kept_proj_seed, axis=0)
    )
    out_grad = over_rows(
        jnp.concatenate(kept_branch, axis=0), jnp.concatenate(kept_out_seed, axis=0)
    )
    gate_grad = over_rows(all_normed_two, jnp.concatenate(kept_gate_seed, axis=0))
    up_grad = over_rows(all_normed_two, jnp.concatenate(kept_up_seed, axis=0))
    down_grad = over_rows(
        jnp.concatenate(kept_activated, axis=0), jnp.concatenate(kept_down_seed, axis=0)
    )
    gain_one_part, in_part, kernel_part, out_part, gain_two_part, gate_part, up_part, down_part = (
        lax.psum_scatter(gain_one_grad, "wide", scatter_dimension=0, tiled=True),
        lax.psum_scatter(in_grad, "wide", scatter_dimension=0, tiled=True),
        lax.psum_scatter(kernel_grad, "wide", scatter_dimension=1, tiled=True),
        lax.psum_scatter(out_grad, "wide", scatter_dimension=0, tiled=True),
        lax.psum_scatter(gain_two_grad, "wide", scatter_dimension=0, tiled=True),
        lax.psum_scatter(gate_grad, "wide", scatter_dimension=0, tiled=True),
        lax.psum_scatter(up_grad, "wide", scatter_dimension=0, tiled=True),
        lax.psum_scatter(down_grad, "wide", scatter_dimension=0, tiled=True),
    )
    gain_one_sum, in_sum, kernel_sum, out_sum, gain_two_sum, gate_sum, up_sum, down_sum = (
        lax.psum_scatter(gain_one_part, "narrow", scatter_dimension=0, tiled=True),
        lax.psum_scatter(in_part, "narrow", scatter_dimension=0, tiled=True),
        lax.psum_scatter(kernel_part, "narrow", scatter_dimension=1, tiled=True),
        lax.psum_scatter(out_part, "narrow", scatter_dimension=0, tiled=True),
        lax.psum_scatter(gain_two_part, "narrow", scatter_dimension=0, tiled=True),
        lax.psum_scatter(gate_part, "narrow", scatter_dimension=0, tiled=True),
        lax.psum_scatter(up_part, "narrow", scatter_dimension=0, tiled=True),
        lax.psum_scatter(down_part, "narrow", scatter_dimension=0, tiled=True),
    )
    block_out = jnp.stack(outputs, axis=0)
    input_grad = jnp.stack(input_grads, axis=0)
    return (
        block_out,
        input_grad,
        gain_one_sum,
        in_sum,
        kernel_sum,
        out_sum,
        gain_two_sum,
        gate_sum,
        up_sum,
        down_sum,
    )


MESH = pl.DeviceIdType.MESH
BF16, F32 = jnp.bfloat16, jnp.float32
VMEM_LIMIT = 62 * 1024 * 1024


def nn(a, b):
    return lax.dot_general(a, b, (((1,), (0,)), ((), ())), preferred_element_type=F32)


def nt(a, b):
    return lax.dot_general(a, b, (((1,), (1,)), ((), ())), preferred_element_type=F32)


def tn(a, b):
    return lax.dot_general(a, b, (((0,), (0,)), ((), ())), preferred_element_type=F32)


def column_tiles(total, most):
    units = total // 128
    best = max(u for u in range(1, units + 1) if units % u == 0 and u * 128 <= most)
    return [(start, best * 128) for start in range(0, total, best * 128)]


def row_scale(block):
    return lax.rsqrt(jnp.mean(block * block, axis=-1, keepdims=True) + EPSILON)


IN, OUT, GATE, UP, DOWN, SMALL = range(6)
X_FIRST = (DOWN,)
LANES = (0, 0, 1, 1)


def block_kernel(
    plan,
    tokens, cotangent, valid, small, in_weight, out_own, gate_weight, up_weight, down_own,
    block_out, input_grad, in_grad, out_grad, gate_grad, up_grad, down_grad, small_grad,
    w_in, w_out, w_gate, w_up, w_down, w_small, g_down, g_small,
    rx_in, rx_out, rx_gate, rx_up, rx_down, rx_small,
    rz_in, rz_out, rz_gate, rz_up, rz_down, rz_small,
    fin_in, fin_out, fin_gate, fin_up, fin_down, fin_small,
    home_in, home_gate, home_up, home_small, done_in, done_gate, done_up, done_small,
    raw_in, raw_gate, raw_up, valid_rows, params,
    toks, seeds, normed_one, normed_two, out_seed,
    hidden, hidden_grad, own_out,
    projected, gated, conv, mixed, branch, proj_seed,
    silu, slope, activated,
    core_send, core_recv, side_send, side_recv, keep,
    local_sem, a_send, a_recv, up_send, up_recv, dn_send, dn_recv, x_send, x_recv,
    gather_send, gather_recv, part_send, part_recv, halo_send, halo_recv,
    rx_send, rx_recv, rz_send, rz_recv, back_send, back_recv, store_sem,
):
    Z, X, N, T, Q = plan["Z"], 2, 2, 4, plan["Z"] * 2
    L, D, FS, CS = plan["L"], plan["D"], plan["FS"], plan["CS"]
    HALF, GROUP = 2 * L, 4 * L
    wide, n = lax.axis_index("wide"), lax.axis_index("narrow")
    c, q = lax.rem(wide, 2), wide // 2
    x, z = lax.rem(q, X), q // X
    t = c * N + n

    def device(z_, x_, c_, n_):
        return ((z_ * X + x_) * 2 + c_, n_)

    over_core = device(z, x, 1 - c, n)
    over_side = device(z, x, c, 1 - n)
    over_both = device(z, x, 1 - c, 1 - n)
    over_x = device(z, 1 - x, c, n)
    z_ahead = [lax.rem(z + k, Z) for k in range(Z)]
    z_behind = [lax.rem(z - k + Z, Z) for k in range(Z)]
    q_next, q_prev = lax.rem(q + 1, Q), lax.rem(q - 1 + Q, Q)
    over_next, over_prev = (q_next * 2 + c, n), (q_prev * 2 + c, n)

    def remote(src, dst, send, recv, to):
        return pltpu.make_async_remote_copy(
            src_ref=src, dst_ref=dst, send_sem=send, recv_sem=recv, device_id=to, device_id_type=MESH
        )

    weights = (w_in, w_out, w_gate, w_up, w_down, w_small)
    grads = (w_in, w_out, w_gate, w_up, g_down, g_small)
    rx = (rx_in, rx_out, rx_gate, rx_up, rx_down, rx_small)
    rz = (rz_in, rz_out, rz_gate, rz_up, rz_down, rz_small)
    fin = (fin_in, fin_out, fin_gate, fin_up, fin_down, fin_small)
    raw = {IN: raw_in, GATE: raw_gate, UP: raw_up}
    staged = {
        IN: proj_seed.at[0, pl.ds(0, T * in_weight.shape[0]), :],
        GATE: silu.at[0, pl.ds(0, T * in_weight.shape[0]), :],
        UP: slope.at[0, pl.ds(0, T * in_weight.shape[0]), :],
    }
    home = {IN: home_in, GATE: home_gate, UP: home_up}
    done = {IN: done_in, GATE: done_gate, UP: done_up}
    piece = in_weight.shape[0]
    width = out_own.shape[0]

    def chunk(refs, i, z_, x_):
        rows = refs[i].shape[0] // Q
        start = pl.multiple_of((z_ * X + x_) * rows, 8 if rows == 8 else 16)
        return refs[i].at[pl.ds(start, rows), :]

    def block(ref, batch, member, rows=L):
        return ref.at[batch, pl.ds(pl.multiple_of(member * L, 16), rows), :]

    def own_rows(i):
        start = q * T * piece + t * piece
        return weights[i].at[pl.ds(pl.multiple_of(start, 16), piece), :]

    def small_block(member):
        lanes = pl.ds(pl.multiple_of(member * 128, 128), 128)
        return w_small.at[pl.ds(pl.multiple_of(q * 16, 16), 16), lanes]

    loads = {}
    for name, src, dst in (
        ("small", small, small_block(t)),
        (IN, in_weight, raw_in),
        (OUT, out_own, chunk(weights, OUT, z, x)),
        ("tokens0", tokens.at[0], block(toks, 0, t)),
        ("tokens1", tokens.at[1], block(toks, 1, t)),
        (GATE, gate_weight, raw_gate),
        (UP, up_weight, raw_up),
        ("valid", valid, valid_rows),
        ("cot0", cotangent.at[0], block(seeds, 0, t)),
        ("cot1", cotangent.at[1], block(seeds, 1, t)),
        (DOWN, down_own, chunk(weights, DOWN, z, x)),
    ):
        loads[name] = pltpu.make_async_copy(src, dst, local_sem.at[len(loads)])
        loads[name].start()

    barrier = pltpu.get_barrier_semaphore()
    partners = [over_core, over_side, over_both, over_x, over_next, over_prev]
    partners += [device(z_ahead[k], x, c, n) for k in range(1, Z)]
    for partner in partners:
        pl.semaphore_signal(barrier, inc=1, device_id=partner, device_id_type=MESH)
    pl.semaphore_wait(barrier, len(partners))

    group = [(over_core, (1 - c) * N + n), (over_side, c * N + 1 - n), (over_both, (1 - c) * N + 1 - n)]

    def split(i, parts):
        loads[i].wait()
        cols = raw[i].shape[1] // (parts * T)
        run = cols // Q
        for member in range(T):
            for part in range(parts):
                first = part * cols * T + member * run
                runs = [raw[i][:, first + k * T * run : first + (k * T + 1) * run].astype(F32) for k in range(Q)]
                staged[i][member * piece : (member + 1) * piece, part * cols : (part + 1) * cols] = (
                    jnp.concatenate(runs, axis=1).astype(BF16)
                )
        mine = staged[i].at[pl.ds(pl.multiple_of(t * piece, 16), piece), :]
        own_rows(i)[...] = mine[...]

    def slices(i):
        s = (IN, GATE, UP, SMALL).index(i)
        found = []
        for k, (to, member) in enumerate(group):
            if i == SMALL:
                src, dst = small_block(t), small_block(t)
            else:
                src, dst = staged[i].at[pl.ds(pl.multiple_of(member * piece, 16), piece), :], own_rows(i)
            found.append(remote(src, dst, a_send.at[s, k], a_recv.at[s, k], to))
        return found

    def slices_arrive(i):
        s = (IN, GATE, UP, SMALL).index(i)
        for k, (to, member) in enumerate(group):
            if i == SMALL:
                dst = small_block(member)
            else:
                start = q * T * piece + member * piece
                dst = weights[i].at[pl.ds(pl.multiple_of(start, 16), piece), :]
            remote(dst, dst, a_send.at[s, k], a_recv.at[s, k], to).wait_recv()

    def gather_copies(ref, use, batch):
        mine = block(ref, batch, t)
        side = block(ref, batch, c * N + 1 - n)
        return (
            remote(mine, mine, gather_send.at[use, batch, 0], gather_recv.at[use, batch, 0], over_side),
            remote(mine, mine, gather_send.at[use, batch, 1], gather_recv.at[use, batch, 1], over_core),
            remote(side, side, gather_send.at[use, batch, 2], gather_recv.at[use, batch, 2], over_core),
        )

    def gather_start(ref, use, batch):
        to_side, to_core, _ = gather_copies(ref, use, batch)
        to_side.start()
        to_core.start()

    def gather_relay(ref, use, batch):
        to_side, _, relay = gather_copies(ref, use, batch)
        to_side.wait_recv()
        relay.start()

    def gather_finish(ref, use, batch):
        to_side, to_core, relay = gather_copies(ref, use, batch)
        to_core.wait_recv()
        relay.wait_recv()
        for copy in (to_side, to_core, relay):
            copy.wait_send()

    def z_copy(i, j, line, upward):
        if upward:
            src_z, to, send, recv = z - (j - 1), device(z + 1, line_x(0), c, n), up_send, up_recv
        else:
            src_z, to, send, recv = z + (j - 1), device(z - 1, line_x(0), c, n), dn_send, dn_recv
        part = chunk(weights, i, src_z, line_x(line))
        return remote(part, part, send.at[i, j - 1, line], recv.at[i, j - 1, line], to)

    def z_arrival(i, j, line, upward):
        src_z = z - j if upward else z + j
        part = chunk(weights, i, src_z, line_x(line))
        send, recv = (up_send, up_recv) if upward else (dn_send, dn_recv)
        return remote(part, part, send.at[i, j - 1, line], recv.at[i, j - 1, line], over_x)

    def line_x(line):
        return x if line == 0 else 1 - x

    def z_launch(i, line):
        @pl.when(z < Z - 1)
        def _():
            z_copy(i, 1, line, True).start()

        @pl.when(z > 0)
        def _():
            z_copy(i, 1, line, False).start()

    def x_copy(i, z_, arrival=False):
        part = chunk(weights, i, z_, 1 - x if arrival else x)
        return remote(part, part, x_send.at[i, z_], x_recv.at[i, z_], over_x)

    def z_pass(i, j, line, to_x):
        @pl.when(z - j >= 0)
        def _():
            z_arrival(i, j, line, True).wait_recv()
            if j < Z - 1:
                @pl.when(z < Z - 1)
                def _():
                    z_copy(i, j + 1, line, True).start()
            if to_x:
                x_copy(i, z - j).start()

        @pl.when(z + j <= Z - 1)
        def _():
            z_arrival(i, j, line, False).wait_recv()
            if j < Z - 1:
                @pl.when(z > 0)
                def _():
                    z_copy(i, j + 1, line, False).start()
            if to_x:
                x_copy(i, z + j).start()

    def z_settle(i, line):
        for j in range(1, Z):
            @pl.when((z < Z - 1) & (z - (j - 1) >= 0))
            def _():
                z_copy(i, j, line, True).wait_send()

            @pl.when((z > 0) & (z + (j - 1) <= Z - 1))
            def _():
                z_copy(i, j, line, False).wait_send()

    def x_arrive(i):
        for z_ in range(Z):
            x_copy(i, z_, True).wait_recv()

    def x_settle(i):
        for z_ in range(Z):
            x_copy(i, z_).wait_send()

    def part_copies(use, batch):
        lane = LANES[use]
        return (
            remote(
                core_send.at[batch], core_recv.at[lane, batch],
                part_send.at[use, batch, 0], part_recv.at[use, batch, 0], over_core,
            ),
            remote(
                side_send.at[batch], side_recv.at[lane, batch],
                part_send.at[use, batch, 1], part_recv.at[use, batch, 1], over_side,
            ),
        )

    def parts_begin(use, product):
        for batch in range(2):
            def put(cols, value, batch=batch):
                core_send[batch, :, cols] = value.astype(BF16)

            product(batch, (1 - c) * HALF, put)
            part_copies(use, batch)[0].start()
        for batch in range(2):
            def put(cols, value, batch=batch):
                keep[batch, :, cols] = value

            product(batch, c * HALF, put)

    def parts_middle(use):
        lane = LANES[use]
        for batch in range(2):
            to_core, to_side = part_copies(use, batch)
            to_core.wait_recv()
            rows = pl.ds(pl.multiple_of((1 - n) * L, 16), L)
            side_send[batch] = (
                keep[batch, rows, :] + core_recv[lane, batch, rows, :].astype(F32)
            ).astype(BF16)
            to_side.start()

    def parts_end(use, batch):
        lane = LANES[use]
        to_core, to_side = part_copies(use, batch)
        to_side.wait_recv()
        rows = pl.ds(pl.multiple_of(n * L, 16), L)
        total = (
            keep[batch, rows, :]
            + core_recv[lane, batch, rows, :].astype(F32)
            + side_recv[lane, batch].astype(F32)
        )
        to_core.wait_send()
        to_side.wait_send()
        return total

    def rx_copy(i, z_):
        return remote(chunk(grads, i, z_, 1 - x), rx[i].at[z_], rx_send.at[i, z_], rx_recv.at[i, z_], over_x)

    def rz_copy(i, k):
        return remote(
            chunk(grads, i, z_ahead[k], x), rz[i].at[k - 1], rz_send.at[i, k - 1], rz_recv.at[i, k - 1],
            device(z_ahead[k], x, c, n),
        )

    def reduce_start(i):
        for k in list(range(1, Z)) + [0]:
            rx_copy(i, z_ahead[k]).start()

    def reduce_pass(i, k):
        z_ = z_ahead[k]
        rx_copy(i, z_).wait_recv()
        part = chunk(grads, i, z_, x)
        part[...] = (part[...].astype(F32) + rx[i][z_].astype(F32)).astype(part.dtype)
        rz_copy(i, k).start()

    def reduce_end(i):
        rx_copy(i, z).wait_recv()
        total = chunk(grads, i, z, x)[...].astype(F32) + rx[i][z].astype(F32)
        for k in range(1, Z):
            rz_copy(i, k).wait_recv()
            total = total + rz[i][k - 1].astype(F32)
        fin[i][...] = total.astype(fin[i].dtype)
        for z_ in range(Z):
            rx_copy(i, z_).wait_send()
        for k in range(1, Z):
            rz_copy(i, k).wait_send()

    results = {IN: in_grad, GATE: gate_grad, UP: up_grad, OUT: out_grad, DOWN: down_grad}

    def back_copies(i):
        s = (IN, GATE, UP, SMALL).index(i)
        found = []
        for k, (to, member) in enumerate(group):
            if i == SMALL:
                src, dst = fin_small, home_small.at[t]
            else:
                src, dst = fin[i].at[pl.ds(pl.multiple_of(member * piece, 16), piece), :], home[i].at[t]
            found.append(remote(src, dst, back_send.at[s, k], back_recv.at[s, k], to))
        return found

    def store_start(i):
        if i in (OUT, DOWN):
            pltpu.make_async_copy(fin[i], results[i], store_sem.at[i]).start()
            return
        for copy in back_copies(i):
            copy.start()
        if i == SMALL:
            home_small[t] = fin_small[...]
        else:
            home[i][t] = fin[i][pl.ds(pl.multiple_of(t * piece, 16), piece), :]

    def store_copy(i):
        if i in (OUT, DOWN):
            return pltpu.make_async_copy(fin[i], results[i], store_sem.at[i])
        if i == SMALL:
            return pltpu.make_async_copy(done_small, small_grad, store_sem.at[i])
        return pltpu.make_async_copy(done[i], results[i], store_sem.at[i])

    def merge(i, parts):
        s = (IN, GATE, UP, SMALL).index(i)
        for k, (to, member) in enumerate(group):
            dst = home_small.at[member] if i == SMALL else home[i].at[member]
            remote(dst, dst, back_send.at[s, k], back_recv.at[s, k], to).wait_recv()
        for copy in back_copies(i):
            copy.wait_send()
        if i == SMALL:
            both = home_small[0] + home_small[1] + home_small[2] + home_small[3]
            done_small[...] = both
            done_small[2:5, :] = home_small[t, 2:5, :]
        else:
            cols = home[i].shape[2] // parts
            run = cols // Q
            for part in range(parts):
                runs = [
                    home[i][member, :, part * cols + k * run : part * cols + (k + 1) * run].astype(F32)
                    for k in range(Q)
                    for member in range(T)
                ]
                done[i][:, part * cols * T : (part + 1) * cols * T] = jnp.concatenate(runs, axis=1)
        store_copy(i).start()

    loads["small"].wait()
    for copy in slices(SMALL):
        copy.start()
    loads[OUT].wait()
    z_launch(OUT, 0)
    x_copy(OUT, z).start()
    split(IN, 3)
    for copy in slices(IN):
        copy.start()
    slices_arrive(SMALL)
    z_launch(SMALL, 0)
    x_copy(SMALL, z).start()
    split(GATE, 1)
    for copy in slices(GATE):
        copy.start()
    for batch in range(2):
        loads["tokens%d" % batch].wait()
        gather_start(toks, 0, batch)
    slices_arrive(IN)
    z_launch(IN, 0)
    x_copy(IN, z).start()
    split(UP, 1)
    for copy in slices(UP):
        copy.start()
    for i in (OUT, SMALL, IN):
        z_pass(i, 1, 0, True)
    loads["valid"].wait()
    for batch in range(2):
        loads["cot%d" % batch].wait()
        mine = pl.ds(pl.multiple_of(t * L, 16), L)
        column = jnp.transpose(jnp.broadcast_to(valid_rows[batch : batch + 1, :], (128, L)))[:, :1]
        seeds[batch, mine, :] = (seeds[batch, mine, :].astype(F32) * column).astype(BF16)
    for i in (OUT, SMALL, IN):
        z_pass(i, 2, 0, True)
    slices_arrive(GATE)
    z_launch(GATE, 0)
    x_copy(GATE, z).start()
    gather_relay(toks, 0, 0)
    gather_relay(toks, 0, 1)
    for batch in range(2):
        gather_start(seeds, 1, batch)
    for i in (OUT, SMALL, IN):
        for j in range(3, Z):
            z_pass(i, j, 0, True)
    x_arrive(SMALL)
    pieces = [
        jnp.concatenate(
            [w_small[k * 16 : k * 16 + 8, m * 128 : m * 128 + width].astype(F32) for m in range(T)], axis=1
        )
        for k in range(Q)
    ]
    params[...] = jnp.concatenate(pieces, axis=1)

    def norm_rows(ref, gain):
        block_ = ref.astype(F32)
        return (block_ * row_scale(block_) * gain).astype(BF16)

    for batch in range(2):
        gather_finish(toks, 0, batch)

        @pl.loop(0, GROUP // 64)
        def _(step, batch=batch):
            rows = pl.ds(pl.multiple_of(step * 64, 64), 64)
            normed_one[batch, rows, :] = norm_rows(toks[batch, rows, :], params[0:1, :])

    x_arrive(IN)
    for batch in range(2):
        for start, size in column_tiles(3 * CS, 256):
            projected[batch, :, start : start + size] = nn(normed_one[batch], w_in[:, start : start + size])
        gated[batch, 8 : 8 + GROUP, :] = projected[batch, :, :CS] * projected[batch, :, 2 * CS :]

    def halo_copies(batch):
        ahead = remote(
            gated.at[batch, pl.ds(GROUP, 8), :], gated.at[batch, pl.ds(0, 8), :],
            halo_send.at[0, batch], halo_recv.at[0, batch], over_next,
        )
        back = remote(
            conv.at[batch, pl.ds(0, 8), :], conv.at[batch, pl.ds(GROUP, 8), :],
            halo_send.at[1, batch], halo_recv.at[1, batch], over_prev,
        )
        return ahead, back

    for batch in range(2):
        halo_copies(batch)[0].start()
    z_pass(GATE, 1, 0, True)
    my_lanes = pl.ds(pl.multiple_of(t * 128, 128), 128)
    taps = jnp.concatenate(
        [w_small[k * 16 : k * 16 + 8, my_lanes].astype(F32)[2:5, :width] for k in range(Q)], axis=1
    )
    for batch in range(2):
        halo_copies(batch)[0].wait_recv()

        @pl.when(q == 0)
        def _():
            gated[batch, 0:8, :] = jnp.zeros((8, CS), F32)

        for r in range(0, GROUP, HALF):
            value = (
                taps[0:1] * gated[batch, r + 6 : r + 6 + HALF, :]
                + taps[1:2] * gated[batch, r + 7 : r + 7 + HALF, :]
                + taps[2:3] * gated[batch, r + 8 : r + 8 + HALF, :]
            )
            mixed[batch, r : r + HALF, :] = value
            branch[batch, r : r + HALF, :] = (projected[batch, r : r + HALF, CS : 2 * CS] * value).astype(BF16)
    z_pass(GATE, 2, 0, True)
    x_arrive(OUT)

    def product_out(batch, start, put):
        rows = pl.ds(pl.multiple_of(start, 16), HALF)
        for at, size in column_tiles(D, 512):
            put(slice(at, at + size), nn(branch[batch, rows, :], w_out[:, at : at + size]))

    parts_begin(0, product_out)
    parts_middle(0)
    slices_arrive(UP)
    z_launch(UP, 0)
    x_copy(UP, z).start()
    for j in range(3, Z):
        z_pass(GATE, j, 0, True)
    gather_relay(seeds, 1, 0)
    gather_relay(seeds, 1, 1)
    for batch in range(2):
        mine = pl.ds(pl.multiple_of(t * L, 16), L)
        hidden[batch] = toks[batch, mine, :].astype(F32) + parts_end(0, batch)
        normed_two[batch, mine, :] = norm_rows(hidden[batch], params[1:2, :])
        gather_start(normed_two, 2, batch)
    z_pass(UP, 1, 0, True)
    gather_relay(normed_two, 2, 0)
    z_pass(UP, 2, 0, True)
    gather_relay(normed_two, 2, 1)
    loads[DOWN].wait()
    if DOWN in X_FIRST:
        x_copy(DOWN, z).start()
    z_launch(DOWN, 0)
    for j in range(3, Z):
        z_pass(UP, j, 0, True)
    if DOWN not in X_FIRST:
        x_copy(DOWN, z).start()
    for batch in range(2):
        gather_finish(normed_two, 2, batch)
        gather_finish(seeds, 1, batch)

    def down_pass(j):
        z_pass(DOWN, j, 0, DOWN not in X_FIRST)
        if DOWN in X_FIRST:
            z_pass(DOWN, j, 1, False)

    if DOWN in X_FIRST:
        x_copy(DOWN, z, True).wait_recv()
        z_launch(DOWN, 1)
    down_pass(1)

    x_arrive(GATE)
    x_arrive(UP)
    for i in (IN, GATE, UP, SMALL):
        for copy in slices(i):
            copy.wait_send()
    for batch in range(2):
        for r in range(0, GROUP, HALF):
            for start, size in column_tiles(FS, 384):
                cols = slice(start, start + size)
                rows = slice(r, r + HALF)
                left = normed_two[batch, rows, :]
                gate = nn(left, w_gate[:, cols])
                up = nn(left, w_up[:, cols])
                sig = 1.0 / (1.0 + jnp.exp(-gate))
                act = gate * sig
                silu[batch, rows, cols] = act.astype(BF16)
                slope[batch, rows, cols] = (up * sig * (1.0 + gate * (1.0 - sig))).astype(BF16)
                activated[batch, rows, cols] = (act * up).astype(BF16)
        if batch == 0:
            down_pass(2)

    def weight_grad(dst, left, right, most_rows, most_cols):
        for a, rows in column_tiles(dst.shape[0], most_rows):
            for b, cols in column_tiles(dst.shape[1], most_cols):
                value = tn(left[0, :, a : a + rows], right[0, :, b : b + cols])
                value = value + tn(left[1, :, a : a + rows], right[1, :, b : b + cols])
                dst[a : a + rows, b : b + cols] = value.astype(BF16)

    weight_grad(g_down, activated, seeds, 384, 512)
    reduce_start(DOWN)
    for j in range(3, Z):
        down_pass(j)
    if DOWN not in X_FIRST:
        x_arrive(DOWN)

    for batch in range(2):
        for r in range(0, GROUP, HALF):
            for start, size in column_tiles(FS, 384):
                cols = slice(start, start + size)
                rows = slice(r, r + HALF)
                act_grad = nt(seeds[batch, rows, :], w_down[cols, :])
                silu[batch, rows, cols] = (act_grad * silu[batch, rows, cols].astype(F32)).astype(BF16)
                slope[batch, rows, cols] = (act_grad * slope[batch, rows, cols].astype(F32)).astype(BF16)
    up_seed, gate_seed = silu, slope

    def product_ffn(batch, start, put):
        rows = pl.ds(pl.multiple_of(start, 16), HALF)
        for at, size in column_tiles(D, 512):
            put(
                slice(at, at + size),
                nt(gate_seed[batch, rows, :], w_gate[at : at + size, :])
                + nt(up_seed[batch, rows, :], w_up[at : at + size, :]),
            )

    def product_down(batch, start, put):
        rows = pl.ds(pl.multiple_of(start, 16), HALF)
        for at, size in column_tiles(D, 512):
            put(slice(at, at + size), nn(activated[batch, rows, :], w_down[:, at : at + size]))

    parts_begin(2, product_ffn)
    parts_middle(2)
    reduce_pass(DOWN, 1)
    for i in (IN, OUT, GATE, UP, DOWN, SMALL):
        z_settle(i, 0)
        if i in X_FIRST:
            z_settle(i, 1)
            x_copy(i, z).wait_send()
        else:
            x_settle(i)
    weight_grad(w_gate, normed_two, gate_seed, 256, 384)
    reduce_start(GATE)
    reduce_pass(DOWN, 2)
    weight_grad(w_up, normed_two, up_seed, 256, 384)
    for k in range(3, Z):
        reduce_pass(DOWN, k)
    gain_two = jnp.zeros((1, D), F32)
    for batch in range(2):
        mine = pl.ds(pl.multiple_of(t * L, 16), L)
        n2g = parts_end(2, batch)
        hid = hidden[batch]
        scale = row_scale(hid)
        gain_two = gain_two + jnp.sum(n2g * hid * scale, axis=0, keepdims=True)
        scaled = n2g * params[1:2, :]
        value = (
            seeds[batch, mine, :].astype(F32)
            + scale * scaled
            - hid * (scale * scale * scale) * jnp.mean(scaled * hid, axis=-1, keepdims=True)
        )
        hidden_grad[batch] = value
        out_seed[batch, mine, :] = value.astype(BF16)
        gather_start(out_seed, 3, batch)
    parts_begin(1, product_down)
    gather_relay(out_seed, 3, 0)
    gather_relay(out_seed, 3, 1)
    parts_middle(1)
    reduce_pass(GATE, 1)
    for batch in range(2):
        gather_finish(out_seed, 3, batch)

    for batch in range(2):
        for r in range(0, GROUP, HALF):
            rows = slice(r, r + HALF)
            branch_grad = nt(out_seed[batch, rows, :], w_out[...])
            conv_grad = branch_grad * projected[batch, rows, CS : 2 * CS]
            conv[batch, rows, :] = conv_grad
            proj_seed[batch, rows, CS : 2 * CS] = (branch_grad * mixed[batch, rows, :]).astype(BF16)
        halo_copies(batch)[1].start()
    reduce_start(UP)
    kernel_grad = [jnp.zeros((1, CS), F32) for _ in range(3)]
    for batch in range(2):
        for r in range(0, GROUP, HALF):
            conv_grad = conv[batch, r : r + HALF, :]
            for k in range(3):
                kernel_grad[k] = kernel_grad[k] + jnp.sum(
                    conv_grad * gated[batch, r + 6 + k : r + 6 + k + HALF, :], axis=0, keepdims=True
                )
    weight_grad(w_out, branch, out_seed, 256, 512)
    reduce_pass(GATE, 2)
    for batch in range(2):
        halo_copies(batch)[1].wait_recv()

        @pl.when(q == Q - 1)
        def _():
            conv[batch, GROUP : GROUP + 8, :] = jnp.zeros((8, CS), F32)

        for r in range(0, GROUP, HALF):
            rows = slice(r, r + HALF)
            value = (
                taps[2:3] * conv[batch, r : r + HALF, :]
                + taps[1:2] * conv[batch, r + 1 : r + 1 + HALF, :]
                + taps[0:1] * conv[batch, r + 2 : r + 2 + HALF, :]
            )
            proj_seed[batch, rows, :CS] = (value * projected[batch, rows, 2 * CS :]).astype(BF16)
            proj_seed[batch, rows, 2 * CS :] = (value * projected[batch, rows, :CS]).astype(BF16)

    def product_in(batch, start, put):
        rows = pl.ds(pl.multiple_of(start, 16), HALF)
        for at, size in column_tiles(D, 512):
            put(slice(at, at + size), nt(proj_seed[batch, rows, :], w_in[at : at + size, :]))

    for batch in range(2):
        own_out[batch] = (hidden[batch] + parts_end(1, batch)).astype(BF16)
    out_copy = pltpu.make_async_copy(own_out, block_out, local_sem.at[0])
    out_copy.start()
    parts_begin(3, product_in)
    for k in range(3, Z):
        reduce_pass(GATE, k)
    parts_middle(3)
    weight_grad(w_in, normed_one, proj_seed, 256, 384)
    reduce_start(IN)
    reduce_start(OUT)
    reduce_pass(UP, 1)
    reduce_end(DOWN)
    store_start(DOWN)
    gain_one = jnp.zeros((1, D), F32)
    for batch in range(2):
        mine = pl.ds(pl.multiple_of(t * L, 16), L)
        n1g = parts_end(3, batch)
        inputs = toks[batch, mine, :].astype(F32)
        scale = row_scale(inputs)
        gain_one = gain_one + jnp.sum(n1g * inputs * scale, axis=0, keepdims=True)
        scaled = n1g * params[0:1, :]
        hidden_grad[batch] = (
            hidden_grad[batch]
            + scale * scaled
            - inputs * (scale * scale * scale) * jnp.mean(scaled * inputs, axis=-1, keepdims=True)
        )
    grad_copy = pltpu.make_async_copy(hidden_grad, input_grad, local_sem.at[1])
    grad_copy.start()
    for k in range(Q):
        lanes = slice(k * 128, (k + 1) * 128)
        runs = [jnp.pad(g[:, k * width : (k + 1) * width], ((0, 0), (0, 128 - width))) for g in kernel_grad]
        rows = [gain_one[:, lanes], gain_two[:, lanes], *runs, jnp.zeros((3, 128), F32)]
        g_small[k * 8 : (k + 1) * 8, :] = jnp.concatenate(rows, axis=0)
    reduce_start(SMALL)
    for k in range(2, Z):
        reduce_pass(UP, k)
    reduce_end(GATE)
    store_start(GATE)
    for k in range(1, Z):
        reduce_pass(IN, k)
    reduce_end(UP)
    store_start(UP)
    merge(GATE, 1)
    for k in range(1, Z):
        reduce_pass(OUT, k)
    for k in range(1, Z):
        reduce_pass(SMALL, k)
    merge(UP, 1)
    reduce_end(IN)
    store_start(IN)
    reduce_end(OUT)
    store_start(OUT)
    reduce_end(SMALL)
    store_start(SMALL)
    for batch in range(2):
        for copy in halo_copies(batch):
            copy.wait_send()
    merge(SMALL, 1)
    merge(IN, 3)
    for i in (DOWN, GATE, UP, OUT, IN, SMALL):
        store_copy(i).wait()
    out_copy.wait()
    grad_copy.wait()


def fused(plan, tokens, cotangent, lengths, loss_mask, norm_gain, in_weight, conv_kernel, out_weight, ffn_gain, gate_weight, up_weight, down_weight):
    Z, Q, T = plan["Z"], plan["Q"], 4
    L, D, FS, CS = plan["L"], plan["D"], plan["FS"], plan["CS"]
    width, hid, rows = out_weight.shape[0], down_weight.shape[0], in_weight.shape[0]
    place = lax.axis_index(("wide", "narrow"))
    positions = place * L + jnp.arange(L, dtype=jnp.int32)
    valid = ((positions[None, :] < lengths[:, None]) & (loss_mask != 0)).astype(F32)
    valid = jnp.pad(valid, ((0, 6), (0, 0)))
    small = jnp.concatenate([norm_gain[None], ffn_gain[None], conv_kernel], axis=0)
    small = jnp.pad(small, ((0, 11), (0, 128 - width)))

    shapes = [(T * rows, 3 * CS), (width, D), (T * rows, FS), (T * rows, FS), (hid, D)]
    vm, dma = pltpu.VMEM, pltpu.SemaphoreType.DMA
    group = T * L
    scratch = [vm((Q * r, k), BF16) for r, k in shapes]
    scratch += [vm((Q * 16, T * 128), BF16), vm((Q * hid, D), BF16), vm((Q * 8, 128), F32)]
    scratch += [vm((Z, r, k), BF16) for r, k in shapes] + [vm((Z, 8, 128), F32)]
    scratch += [vm((Z - 1, r, k), BF16) for r, k in shapes] + [vm((Z - 1, 8, 128), F32)]
    scratch += [vm((r, k), BF16 if i in (IN, GATE, UP) else F32) for i, (r, k) in enumerate(shapes)]
    scratch += [vm((8, 128), F32)]
    scratch += [vm((T, rows, 3 * CS), BF16), vm((T, rows, FS), BF16), vm((T, rows, FS), BF16), vm((T, 8, 128), F32)]
    scratch += [vm(a.shape, F32) for a in (in_weight, gate_weight, up_weight)] + [vm((8, 128), F32)]
    scratch += [vm(a.shape, BF16) for a in (in_weight, gate_weight, up_weight)] + [vm((8, L), F32), vm((8, D), F32)]
    scratch += [vm((2, group, D), BF16) for _ in range(5)]
    scratch += [vm((2, L, D), F32), vm((2, L, D), F32), vm((2, L, D), BF16)]
    scratch += [
        vm((2, group, 3 * CS), F32), vm((2, group + 8, CS), F32), vm((2, group + 8, CS), F32),
        vm((2, group, CS), F32), vm((2, group, CS), BF16), vm((2, group, 3 * CS), BF16),
    ]
    scratch += [vm((2, group, FS), BF16) for _ in range(3)]
    scratch += [
        vm((2, 2 * L, D), BF16), vm((2, 2, 2 * L, D), BF16),
        vm((2, L, D), BF16), vm((2, 2, L, D), BF16), vm((2, 2 * L, D), F32),
    ]
    scratch += [
        dma((11,)), dma((4, 3)), dma((4, 3)),
        dma((6, Z - 1, 2)), dma((6, Z - 1, 2)), dma((6, Z - 1, 2)), dma((6, Z - 1, 2)),
        dma((6, Z)), dma((6, Z)),
        dma((4, 2, 3)), dma((4, 2, 3)), dma((4, 2, 2)), dma((4, 2, 2)), dma((2, 2)), dma((2, 2)),
        dma((6, Z)), dma((6, Z)), dma((6, Z - 1)), dma((6, Z - 1)), dma((4, 3)), dma((4, 3)), dma((6,)),
    ]
    out_shape = (
        jax.ShapeDtypeStruct((2, L, D), BF16),
        jax.ShapeDtypeStruct((2, L, D), F32),
        jax.ShapeDtypeStruct(in_weight.shape, F32),
        jax.ShapeDtypeStruct(out_weight.shape, F32),
        jax.ShapeDtypeStruct(gate_weight.shape, F32),
        jax.ShapeDtypeStruct(up_weight.shape, F32),
        jax.ShapeDtypeStruct(down_weight.shape, F32),
        jax.ShapeDtypeStruct((8, 128), F32),
    )
    block_out, input_grad, in_g, out_g, gate_g, up_g, down_g, small_g = pl.pallas_call(
        functools.partial(block_kernel, plan),
        out_shape=out_shape,
        in_specs=[pl.BlockSpec(memory_space=pl.ANY)] * 9,
        out_specs=[pl.BlockSpec(memory_space=pl.ANY)] * 8,
        scratch_shapes=scratch,
        compiler_params=pltpu.CompilerParams(
            collective_id=0, has_side_effects=True, vmem_limit_bytes=VMEM_LIMIT
        ),
    )(tokens, cotangent, valid, small, in_weight, out_weight, gate_weight, up_weight, down_weight)
    member = place % T
    gains = lax.dynamic_slice(small_g, (0, member * width), (2, width))
    return block_out, input_grad, gains[0], in_g, small_g[2:5, :width], out_g, gains[1], gate_g, up_g, down_g


def planned(wide, narrow, arrays):
    tokens, in_weight, down_weight = arrays[0], arrays[5], arrays[11]
    if narrow != 2 or wide % 4 or wide < 8 or tokens.shape[0] != 2:
        return None
    groups = wide // 2
    rows, hid = in_weight.shape[0], down_weight.shape[0]
    sizes = {
        "Z": groups // 2, "Q": groups, "L": tokens.shape[1], "D": tokens.shape[2],
        "FS": hid * groups, "CS": rows * groups,
    }
    if rows % 16 or hid % 16 or sizes["L"] != 128 or sizes["FS"] % 128 or sizes["CS"] % 128 or rows != 32:
        return None
    return sizes


def solution(mesh):
    in_specs = (
        P(None, ("wide", "narrow"), None),
        P(None, ("wide", "narrow"), None),
        P(),
        P(None, ("wide", "narrow")),
        P(("wide", "narrow")),
        P(("wide", "narrow"), None),
        P(None, ("wide", "narrow")),
        P(("wide", "narrow"), None),
        P(("wide", "narrow")),
        P(("wide", "narrow"), None),
        P(("wide", "narrow"), None),
        P(("wide", "narrow"), None),
    )
    out_specs = (
        P(None, ("wide", "narrow"), None),
        P(None, ("wide", "narrow"), None),
        P(("wide", "narrow")),
        P(("wide", "narrow"), None),
        P(None, ("wide", "narrow")),
        P(("wide", "narrow"), None),
        P(("wide", "narrow")),
        P(("wide", "narrow"), None),
        P(("wide", "narrow"), None),
        P(("wide", "narrow"), None),
    )
    wide, narrow = mesh.shape["wide"], mesh.shape["narrow"]

    def step(*arrays):
        plan = planned(wide, narrow, arrays)
        run = body if plan is None else functools.partial(fused, plan)
        return run(*arrays)

    return jax.shard_map(step, mesh=mesh, in_specs=in_specs, out_specs=out_specs, check_vma=False)
```

```python
import functools

import jax
import jax.numpy as jnp
from jax import lax
from jax.experimental import pallas as pl
from jax.experimental.pallas import tpu as pltpu
from jax.sharding import PartitionSpec as P

EPSILON = 1e-05


def shifted(block, axis, distance):
    devices = range(lax.axis_size(axis))
    route = [(i - distance, i) for i in devices if i - distance in devices]
    return lax.ppermute(block, axis, route)


def along_rows(left, weight):
    return lax.dot_general(
        left, weight, (((1,), (1,)), ((), ())), preferred_element_type=jnp.float32
    )


def over_rows(left, right):
    return lax.dot_general(
        left, right, (((0,), (0,)), ((), ())), preferred_element_type=jnp.float32
    )


def collect(shards):
    partial_set = (
        lax.all_gather(shards[0], "narrow", axis=0, tiled=True),
        lax.all_gather(shards[1], "narrow", axis=0, tiled=True),
        lax.all_gather(shards[2], "narrow", axis=1, tiled=True),
        lax.all_gather(shards[3], "narrow", axis=0, tiled=True),
        lax.all_gather(shards[4], "narrow", axis=0, tiled=True),
        lax.all_gather(shards[5], "narrow", axis=0, tiled=True),
        lax.all_gather(shards[6], "narrow", axis=0, tiled=True),
        lax.all_gather(shards[7], "narrow", axis=0, tiled=True),
    )
    return (
        lax.all_gather(partial_set[0], "wide", axis=0, tiled=True),
        lax.all_gather(partial_set[1], "wide", axis=0, tiled=True),
        lax.all_gather(partial_set[2], "wide", axis=1, tiled=True),
        lax.all_gather(partial_set[3], "wide", axis=0, tiled=True),
        lax.all_gather(partial_set[4], "wide", axis=0, tiled=True),
        lax.all_gather(partial_set[5], "wide", axis=0, tiled=True),
        lax.all_gather(partial_set[6], "wide", axis=0, tiled=True),
        lax.all_gather(partial_set[7], "wide", axis=0, tiled=True),
    )


def collect_tied(shards, anchor):
    tied_shards, _ = lax.optimization_barrier((shards, anchor))
    return collect(tied_shards)


def body(
    tokens,
    cotangent,
    lengths,
    loss_mask,
    norm_gain,
    in_weight,
    conv_kernel,
    out_weight,
    ffn_gain,
    gate_weight,
    up_weight,
    down_weight,
):
    micro_count = tokens.shape[0]
    local_rows = tokens.shape[1]
    width = tokens.shape[2]
    shards = (
        norm_gain,
        in_weight,
        conv_kernel,
        out_weight,
        ffn_gain,
        gate_weight,
        up_weight,
        down_weight,
    )
    positions = lax.axis_index(("wide", "narrow")) * local_rows + jnp.arange(
        local_rows, dtype=jnp.int32
    )
    gain_one_grad = jnp.zeros((width,), jnp.float32)
    gain_two_grad = jnp.zeros((width,), jnp.float32)
    kernel_grad = jnp.zeros((3, width), jnp.float32)
    outputs = []
    input_grads = []
    kept_normed_one = []
    kept_proj_seed = []
    kept_branch = []
    kept_out_seed = []
    kept_normed_two = []
    kept_gate_seed = []
    kept_up_seed = []
    kept_activated = []
    kept_down_seed = []
    for batch in range(micro_count):
        gathered = collect_tied(shards, tokens[batch])
        gain_full, in_full, kernel_full, out_full, ffn_full, gate_full, up_full, down_full = (
            gathered
        )
        gain_f32 = gain_full.astype(jnp.float32)
        ffn_f32 = ffn_full.astype(jnp.float32)
        kernel_f32 = kernel_full.astype(jnp.float32)
        inputs = tokens[batch].astype(jnp.float32)
        scale_one = lax.rsqrt(jnp.mean(inputs * inputs, axis=-1, keepdims=True) + EPSILON)
        normed_one = (inputs * scale_one * gain_f32).astype(jnp.bfloat16)
        projected = jnp.dot(normed_one, in_full, preferred_element_type=jnp.float32)
        b_gate = projected[:, :width]
        c_gate = projected[:, width : 2 * width]
        conv_input = projected[:, 2 * width :]
        gated_input = b_gate * conv_input
        earlier = shifted(gated_input[local_rows - 2 :], ("wide", "narrow"), 1)
        padded = jnp.concatenate([earlier, gated_input], axis=0)
        mixed_conv = (
            kernel_f32[0] * padded[:-2] + kernel_f32[1] * padded[1:-1] + kernel_f32[2] * gated_input
        )
        branch = (c_gate * mixed_conv).astype(jnp.bfloat16)
        hidden = inputs + jnp.dot(branch, out_full, preferred_element_type=jnp.float32)
        scale_two = lax.rsqrt(jnp.mean(hidden * hidden, axis=-1, keepdims=True) + EPSILON)
        normed_two = (hidden * scale_two * ffn_f32).astype(jnp.bfloat16)
        gate_out = jnp.dot(normed_two, gate_full, preferred_element_type=jnp.float32)
        up_out = jnp.dot(normed_two, up_full, preferred_element_type=jnp.float32)
        sigmoid_gate = jax.nn.sigmoid(gate_out)
        silu_gate = gate_out * sigmoid_gate
        activated = (silu_gate * up_out).astype(jnp.bfloat16)
        result = hidden + jnp.dot(activated, down_full, preferred_element_type=jnp.float32)
        outputs.append(result.astype(jnp.bfloat16))
        validity = (positions < lengths[batch]).astype(jnp.float32) * loss_mask[batch].astype(
            jnp.float32
        )
        seed = cotangent[batch].astype(jnp.float32) * validity[:, None]
        down_seed = seed.astype(jnp.bfloat16)
        act_grad = along_rows(down_seed, down_full)
        up_seed = (act_grad * silu_gate).astype(jnp.bfloat16)
        gate_seed = (
            act_grad * up_out * sigmoid_gate * (1.0 + gate_out * (1.0 - sigmoid_gate))
        ).astype(jnp.bfloat16)
        normed_two_grad = along_rows(gate_seed, gate_full) + along_rows(up_seed, up_full)
        gain_two_grad = gain_two_grad + jnp.sum(normed_two_grad * hidden * scale_two, axis=0)
        scaled_two = normed_two_grad * ffn_f32
        hidden_grad = (
            seed
            + scale_two * scaled_two
            - hidden
            * (scale_two * scale_two * scale_two)
            * jnp.mean(scaled_two * hidden, axis=-1, keepdims=True)
        )
        out_seed = hidden_grad.astype(jnp.bfloat16)
        branch_grad = along_rows(out_seed, out_full)
        c_grad = branch_grad * mixed_conv
        conv_grad = branch_grad * c_gate
        kernel_grad = kernel_grad + jnp.stack(
            [
                jnp.sum(conv_grad * padded[:-2], axis=0),
                jnp.sum(conv_grad * padded[1:-1], axis=0),
                jnp.sum(conv_grad * gated_input, axis=0),
            ],
            axis=0,
        )
        later = shifted(conv_grad[:2], ("wide", "narrow"), -1)
        extended = jnp.concatenate([conv_grad, later], axis=0)
        gated_grad = (
            kernel_f32[2] * conv_grad
            + kernel_f32[1] * extended[1 : local_rows + 1]
            + kernel_f32[0] * extended[2:]
        )
        proj_seed = jnp.concatenate(
            [gated_grad * conv_input, c_grad, gated_grad * b_gate], axis=1
        ).astype(jnp.bfloat16)
        normed_one_grad = along_rows(proj_seed, in_full)
        gain_one_grad = gain_one_grad + jnp.sum(normed_one_grad * inputs * scale_one, axis=0)
        scaled_one = normed_one_grad * gain_f32
        input_grads.append(
            hidden_grad
            + scale_one * scaled_one
            - inputs
            * (scale_one * scale_one * scale_one)
            * jnp.mean(scaled_one * inputs, axis=-1, keepdims=True)
        )
        kept_normed_one.append(normed_one)
        kept_proj_seed.append(proj_seed)
        kept_branch.append(branch)
        kept_out_seed.append(out_seed)
        kept_normed_two.append(normed_two)
        kept_gate_seed.append(gate_seed)
        kept_up_seed.append(up_seed)
        kept_activated.append(activated)
        kept_down_seed.append(down_seed)
    all_normed_two = jnp.concatenate(kept_normed_two, axis=0)
    in_grad = over_rows(
        jnp.concatenate(kept_normed_one, axis=0), jnp.concatenate(kept_proj_seed, axis=0)
    )
    out_grad = over_rows(
        jnp.concatenate(kept_branch, axis=0), jnp.concatenate(kept_out_seed, axis=0)
    )
    gate_grad = over_rows(all_normed_two, jnp.concatenate(kept_gate_seed, axis=0))
    up_grad = over_rows(all_normed_two, jnp.concatenate(kept_up_seed, axis=0))
    down_grad = over_rows(
        jnp.concatenate(kept_activated, axis=0), jnp.concatenate(kept_down_seed, axis=0)
    )
    gain_one_part, in_part, kernel_part, out_part, gain_two_part, gate_part, up_part, down_part = (
        lax.psum_scatter(gain_one_grad, "wide", scatter_dimension=0, tiled=True),
        lax.psum_scatter(in_grad, "wide", scatter_dimension=0, tiled=True),
        lax.psum_scatter(kernel_grad, "wide", scatter_dimension=1, tiled=True),
        lax.psum_scatter(out_grad, "wide", scatter_dimension=0, tiled=True),
        lax.psum_scatter(gain_two_grad, "wide", scatter_dimension=0, tiled=True),
        lax.psum_scatter(gate_grad, "wide", scatter_dimension=0, tiled=True),
        lax.psum_scatter(up_grad, "wide", scatter_dimension=0, tiled=True),
        lax.psum_scatter(down_grad, "wide", scatter_dimension=0, tiled=True),
    )
    gain_one_sum, in_sum, kernel_sum, out_sum, gain_two_sum, gate_sum, up_sum, down_sum = (
        lax.psum_scatter(gain_one_part, "narrow", scatter_dimension=0, tiled=True),
        lax.psum_scatter(in_part, "narrow", scatter_dimension=0, tiled=True),
        lax.psum_scatter(kernel_part, "narrow", scatter_dimension=1, tiled=True),
        lax.psum_scatter(out_part, "narrow", scatter_dimension=0, tiled=True),
        lax.psum_scatter(gain_two_part, "narrow", scatter_dimension=0, tiled=True),
        lax.psum_scatter(gate_part, "narrow", scatter_dimension=0, tiled=True),
        lax.psum_scatter(up_part, "narrow", scatter_dimension=0, tiled=True),
        lax.psum_scatter(down_part, "narrow", scatter_dimension=0, tiled=True),
    )
    block_out = jnp.stack(outputs, axis=0)
    input_grad = jnp.stack(input_grads, axis=0)
    return (
        block_out,
        input_grad,
        gain_one_sum,
        in_sum,
        kernel_sum,
        out_sum,
        gain_two_sum,
        gate_sum,
        up_sum,
        down_sum,
    )


MESH = pl.DeviceIdType.MESH
BF16, F32 = jnp.bfloat16, jnp.float32
VMEM_LIMIT = 62 * 1024 * 1024


def nn(a, b):
    return lax.dot_general(a, b, (((1,), (0,)), ((), ())), preferred_element_type=F32)


def nt(a, b):
    return lax.dot_general(a, b, (((1,), (1,)), ((), ())), preferred_element_type=F32)


def tn(a, b):
    return lax.dot_general(a, b, (((0,), (0,)), ((), ())), preferred_element_type=F32)


def column_tiles(total, most):
    units = total // 128
    count = -(-units // (most // 128))
    edges = [-(-units * k // count) * 128 for k in range(count + 1)]
    return [(a, b - a) for a, b in zip(edges, edges[1:])]


def row_scale(block):
    return lax.rsqrt(jnp.mean(block * block, axis=-1, keepdims=True) + EPSILON)


IN, OUT, GATE0, GATE1, UP0, UP1, DOWN, SMALL, DOWN1 = range(9)
GATE, UP = (GATE0, GATE1), (UP0, UP1)
SLICED = (IN, GATE0, GATE1, UP0, UP1, SMALL)
LANES = (0, 0, 1, 1)


def block_kernel(
    plan,
    tokens, cotangent, valid, small, in_weight, out_own, gate_weight, up_weight, down_own,
    block_out, input_grad, in_grad, out_grad, gate_grad, up_grad, down_grad, small_grad,
    w_in, w_out, w_gate, w_up, w_down, w_small, g_down, g_small,
    rx_in, rx_out, rx_gate, rx_up, rx_down, rx_small,
    rz_in, rz_out, rz_gate, rz_up, rz_down, rz_small,
    via_in, via_out, via_gate, via_up, via_down, via_small,
    fin_in, fin_out, fin_gate, fin_up, fin_down, fin_small,
    home_in, home_gate, home_up, home_small, done_in, done_gate, done_up, done_small,
    raw_in, raw_gate, raw_up, valid_rows, params,
    toks, seeds, normed_one, normed_two, out_seed,
    hidden, hidden_grad,
    projected, gated, conv, branch, proj_seed,
    silu, slope, activated,
    core_send, core_recv, side_send, side_recv, keep,
    local_sem, a_send, a_recv, up_send, up_recv, dn_send, dn_recv, x_send, x_recv,
    gather_send, gather_recv, part_send, part_recv, halo_send, halo_recv,
    rx_send, rx_recv, rz_send, rz_recv, via_send, via_recv, back_send, back_recv, store_sem,
):
    Z, X, N, T, Q = plan["Z"], 2, 2, 4, plan["Z"] * 2
    L, D, FS, CS = plan["L"], plan["D"], plan["FS"], plan["CS"]
    HALF, GROUP = 2 * L, 4 * L
    wide, n = lax.axis_index("wide"), lax.axis_index("narrow")
    c, q = lax.rem(wide, 2), wide // 2
    x, z = lax.rem(q, X), q // X
    t = c * N + n

    def device(z_, x_, c_, n_):
        return ((z_ * X + x_) * 2 + c_, n_)

    over_core = device(z, x, 1 - c, n)
    over_side = device(z, x, c, 1 - n)
    over_both = device(z, x, 1 - c, 1 - n)
    over_x = device(z, 1 - x, c, n)
    z_ahead = [lax.rem(z + k, Z) for k in range(Z)]
    z_behind = [lax.rem(z - k + Z, Z) for k in range(Z)]
    q_next, q_prev = lax.rem(q + 1, Q), lax.rem(q - 1 + Q, Q)
    over_next, over_prev = (q_next * 2 + c, n), (q_prev * 2 + c, n)

    def remote(src, dst, send, recv, to):
        return pltpu.make_async_remote_copy(
            src_ref=src, dst_ref=dst, send_sem=send, recv_sem=recv, device_id=to, device_id_type=MESH
        )

    cut = -(-FS // 256) * 128
    halves = (slice(0, cut), slice(cut, FS))

    def views(in_, out, gate, up, down, small_):
        def half(ref, cols):
            return None if ref is None else ref.at[..., pl.ds(cols.start, cols.stop - cols.start)]

        return (in_, out, *(half(gate, h) for h in halves), *(half(up, h) for h in halves), down, small_)

    weights = views(w_in, w_out, w_gate, w_up, w_down.at[:, pl.ds(0, D // 2)], w_small)
    weights += (w_down.at[:, pl.ds(D // 2, D - D // 2)],)
    grads = views(w_in, w_out, w_gate, w_up, g_down, g_small)
    rx = views(rx_in, rx_out, rx_gate, rx_up, rx_down, rx_small)
    rz = views(rz_in, rz_out, rz_gate, rz_up, rz_down, rz_small)
    via = views(via_in, via_out, via_gate, via_up, via_down, via_small)
    fin = views(fin_in, fin_out, fin_gate, fin_up, fin_down, fin_small)
    home = views(home_in, None, home_gate, home_up, None, home_small)
    piece = in_weight.shape[0]
    width = out_own.shape[0]
    stage_in = proj_seed.at[0, pl.ds(0, T * piece), :]
    stage_gate = silu.at[0, pl.ds(0, T * piece), :]
    stage_up = slope.at[0, pl.ds(0, T * piece), :]
    staged = views(stage_in, None, stage_gate, stage_up, None, None)

    def chunk_size(i):
        return weights[i].shape[0] // Q

    def chunk(refs, i, z_, x_):
        rows = refs[i].shape[0] // Q
        start = pl.multiple_of((z_ * X + x_) * rows, 8 if rows == 8 else 16)
        return refs[i].at[pl.ds(start, rows), :]

    def block(ref, batch, member, rows=L):
        return ref.at[batch, pl.ds(pl.multiple_of(member * L, 16), rows), :]

    def own_rows(i):
        start = q * T * piece + t * piece
        return weights[i].at[pl.ds(pl.multiple_of(start, 16), piece), :]

    def small_block(member):
        lanes = pl.ds(pl.multiple_of(member * 128, 128), 128)
        return w_small.at[pl.ds(pl.multiple_of(q * 16, 16), 16), lanes]

    loads = {}
    for name, src, dst in (
        ("small", small, small_block(t)),
        ("in", in_weight, raw_in),
        (OUT, out_own, chunk(weights, OUT, z, x)),
        (DOWN, down_own, chunk([w_down], 0, z, x)),
        ("tokens0", tokens.at[0], block(toks, 0, t)),
        ("tokens1", tokens.at[1], block(toks, 1, t)),
        ("gate", gate_weight, raw_gate),
        ("up", up_weight, raw_up),
        ("valid", valid, valid_rows),
        ("cot0", cotangent.at[0], block(seeds, 0, t)),
        ("cot1", cotangent.at[1], block(seeds, 1, t)),
    ):
        loads[name] = pltpu.make_async_copy(src, dst, local_sem.at[len(loads)])
        loads[name].start()

    barrier = pltpu.get_barrier_semaphore()
    partners = [over_core, over_side, over_both, over_x, over_next, over_prev]
    partners += [device(z_ahead[k], x, c, n) for k in range(1, Z)]
    for partner in partners:
        pl.semaphore_signal(barrier, inc=1, device_id=partner, device_id_type=MESH)
    pl.semaphore_wait(barrier, len(partners))

    group = [(over_core, (1 - c) * N + n), (over_side, c * N + 1 - n), (over_both, (1 - c) * N + 1 - n)]

    def split(raw, stage, full, parts):
        cols = raw.shape[1] // (parts * T)
        run = cols // Q
        for member in range(T):
            for part in range(parts):
                first = part * cols * T + member * run
                runs = [raw[:, first + k * T * run : first + (k * T + 1) * run].astype(F32) for k in range(Q)]
                stage[member * piece : (member + 1) * piece, part * cols : (part + 1) * cols] = (
                    jnp.concatenate(runs, axis=1).astype(BF16)
                )
        mine = stage[pl.ds(pl.multiple_of(t * piece, 16), piece), :]
        full[pl.ds(pl.multiple_of(q * T * piece + t * piece, 16), piece), :] = mine

    def slices(i):
        s = SLICED.index(i)
        found = []
        for k, (to, member) in enumerate(group):
            if i == SMALL:
                src, dst = small_block(t), small_block(t)
            else:
                src, dst = staged[i].at[pl.ds(pl.multiple_of(member * piece, 16), piece), :], own_rows(i)
            found.append(remote(src, dst, a_send.at[s, k], a_recv.at[s, k], to))
        return found

    def slices_arrive(i):
        s = SLICED.index(i)
        for k, (to, member) in enumerate(group):
            if i == SMALL:
                dst = small_block(member)
            else:
                start = q * T * piece + member * piece
                dst = weights[i].at[pl.ds(pl.multiple_of(start, 16), piece), :]
            remote(dst, dst, a_send.at[s, k], a_recv.at[s, k], to).wait_recv()

    def gather_copies(ref, use, batch):
        mine = block(ref, batch, t)
        side = block(ref, batch, c * N + 1 - n)
        return (
            remote(mine, mine, gather_send.at[use, batch, 0], gather_recv.at[use, batch, 0], over_side),
            remote(mine, mine, gather_send.at[use, batch, 1], gather_recv.at[use, batch, 1], over_core),
            remote(side, side, gather_send.at[use, batch, 2], gather_recv.at[use, batch, 2], over_core),
        )

    def gather_start(ref, use, batch):
        to_side, to_core, _ = gather_copies(ref, use, batch)
        to_side.start()
        to_core.start()

    def gather_relay(ref, use, batch):
        to_side, _, relay = gather_copies(ref, use, batch)
        to_side.wait_recv()
        relay.start()

    def gather_finish(ref, use, batch):
        to_side, to_core, relay = gather_copies(ref, use, batch)
        to_core.wait_recv()
        relay.wait_recv()
        for copy in (to_side, to_core, relay):
            copy.wait_send()

    def z_copy(i, j, line, upward):
        if upward:
            src_z, to, send, recv = z - (j - 1), device(z + 1, line_x(0), c, n), up_send, up_recv
        else:
            src_z, to, send, recv = z + (j - 1), device(z - 1, line_x(0), c, n), dn_send, dn_recv
        part = chunk(weights, i, src_z, line_x(line))
        return remote(part, part, send.at[i, j - 1, line], recv.at[i, j - 1, line], to)

    def z_arrival(i, j, line, upward):
        src_z = z - j if upward else z + j
        part = chunk(weights, i, src_z, line_x(line))
        send, recv = (up_send, up_recv) if upward else (dn_send, dn_recv)
        return remote(part, part, send.at[i, j - 1, line], recv.at[i, j - 1, line], over_x)

    def line_x(line):
        return x if line == 0 else 1 - x

    def z_launch(i, line):
        @pl.when(z < Z - 1)
        def _():
            z_copy(i, 1, line, True).start()

        @pl.when(z > 0)
        def _():
            z_copy(i, 1, line, False).start()

    def x_copy(i, z_, arrival=False):
        part = chunk(weights, i, z_, 1 - x if arrival else x)
        return remote(part, part, x_send.at[i, z_], x_recv.at[i, z_], over_x)

    def z_pass(i, j, line, to_x):
        @pl.when(z - j >= 0)
        def _():
            z_arrival(i, j, line, True).wait_recv()
            if j < Z - 1:
                @pl.when(z < Z - 1)
                def _():
                    z_copy(i, j + 1, line, True).start()
            if to_x:
                x_copy(i, z - j).start()

        @pl.when(z + j <= Z - 1)
        def _():
            z_arrival(i, j, line, False).wait_recv()
            if j < Z - 1:
                @pl.when(z > 0)
                def _():
                    z_copy(i, j + 1, line, False).start()
            if to_x:
                x_copy(i, z + j).start()

    def z_settle(i, line):
        for j in range(1, Z):
            @pl.when((z < Z - 1) & (z - (j - 1) >= 0))
            def _():
                z_copy(i, j, line, True).wait_send()

            @pl.when((z > 0) & (z + (j - 1) <= Z - 1))
            def _():
                z_copy(i, j, line, False).wait_send()

    def x_arrive(i):
        for z_ in range(Z):
            x_copy(i, z_, True).wait_recv()

    def x_settle(i):
        for z_ in range(Z):
            x_copy(i, z_).wait_send()

    def part_copies(use, batch):
        lane = LANES[use]
        return (
            remote(
                core_send.at[batch], core_recv.at[lane, batch],
                part_send.at[use, batch, 0], part_recv.at[use, batch, 0], over_core,
            ),
            remote(
                side_send.at[batch], side_recv.at[lane, batch],
                part_send.at[use, batch, 1], part_recv.at[use, batch, 1], over_side,
            ),
        )

    def parts_send(use, batch):
        lane = LANES[use]
        to_core, to_side = part_copies(use, batch)
        to_core.wait_recv()
        rows = pl.ds(pl.multiple_of((1 - n) * L, 16), L)
        side_send[batch] = (
            keep[batch, rows, :] + core_recv[lane, batch, rows, :].astype(F32)
        ).astype(BF16)
        to_side.start()

    def parts_begin(use, product, prepare=lambda batch: None):
        for batch in range(2):
            def put_away(cols, value, batch=batch):
                core_send[batch, :, cols] = value.astype(BF16)

            def put_keep(cols, value, batch=batch):
                keep[batch, :, cols] = value

            prepare(batch)
            product(batch, (1 - c) * HALF, put_away)
            part_copies(use, batch)[0].start()
            if batch == 1:
                parts_send(use, 0)
            product(batch, c * HALF, put_keep)

    def parts_middle(use):
        parts_send(use, 1)

    def parts_end(use, batch):
        lane = LANES[use]
        to_core, to_side = part_copies(use, batch)
        to_side.wait_recv()
        rows = pl.ds(pl.multiple_of(n * L, 16), L)
        total = (
            keep[batch, rows, :]
            + core_recv[lane, batch, rows, :].astype(F32)
            + side_recv[lane, batch].astype(F32)
        )
        to_core.wait_send()
        to_side.wait_send()
        return total

    def rx_copy(i, z_):
        return remote(chunk(grads, i, z_, 1 - x), rx[i].at[z_], rx_send.at[i, z_], rx_recv.at[i, z_], over_x)

    at_end = (z == 0) | (z == Z - 1)
    def steps(i):
        if i == DOWN:
            return (
                jnp.where(z < 2, 1 - z, jnp.where(z == 2, 1, 0)),
                jnp.where(z < 2, 2, jnp.where(z == 2, 0, 1)),
                jnp.where(z == 3, 2, 3),
            )
        return (
            jnp.where(z == 0, 3, jnp.where(z == 1, 2, jnp.where(z == 2, 3, 0))),
            jnp.where(z == 0, 2, jnp.where(z == 1, 0, 1)),
            jnp.where(z == 0, 1, jnp.where(z == 1, 3, jnp.where(z == 2, 0, 2))),
        )

    def rz_copy(i, k):
        to_z = lax.rem(z + k, Z)
        return remote(
            chunk(grads, i, to_z, x), rz[i].at[k - 1], rz_send.at[i, k - 1], rz_recv.at[i, k - 1],
            device(to_z, x, c, n),
        )

    def via_copy(i):
        src_z, to_z = jnp.where(z == 0, 3, 0), jnp.where(z == 0, 1, 2)
        return remote(chunk(grads, i, src_z, x), via[i], via_send.at[i], via_recv.at[i], device(to_z, x, c, n))

    def reduce_start(i, places=None):
        for z_ in (*steps(i), z) if places is None else places:
            rx_copy(i, z_).start()

    def reduce_pass(i, step):
        z_ = steps(i)[step - 1]
        k = lax.rem(z_ - z + Z, Z)
        rx_copy(i, z_).wait_recv()
        part = chunk(grads, i, z_, x)
        opposite = at_end & (z + z_ == Z - 1)
        helps = jnp.logical_not(at_end) & ((z_ - z == 2) | (z - z_ == 2))

        @pl.when(helps)
        def _():
            via_copy(i).wait_recv()
            total = part[...].astype(F32) + rx[i][z_].astype(F32) + via[i][...].astype(F32)
            part[...] = total.astype(part.dtype)

        @pl.when(jnp.logical_not(helps))
        def _():
            part[...] = (part[...].astype(F32) + rx[i][z_].astype(F32)).astype(part.dtype)

        @pl.when(opposite)
        def _():
            via_copy(i).start()

        @pl.when(jnp.logical_not(opposite))
        def _():
            rz_copy(i, k).start()

    def reduce_end(i):
        rx_copy(i, z).wait_recv()

        def total(arrivals):
            value = chunk(grads, i, z, x)[...].astype(F32) + rx[i][z].astype(F32)
            for k in arrivals:
                rz_copy(i, k).wait_recv()
                value = value + rz[i][k - 1].astype(F32)
            fin[i][...] = value.astype(fin[i].dtype)

        @pl.when(z == 0)
        def _():
            total((2, 3))

        @pl.when(z == Z - 1)
        def _():
            total((1, 2))

        @pl.when(jnp.logical_not(at_end))
        def _():
            total((1, 2, 3))
            rz_copy(i, 1).wait_send()
            rz_copy(i, 3).wait_send()

        @pl.when(at_end)
        def _():
            via_copy(i).wait_send()
            rz_copy(i, jnp.where(z == 0, 1, 3)).wait_send()

        rz_copy(i, 2).wait_send()
        for z_ in range(Z):
            rx_copy(i, z_).wait_send()

    wholes = {
        IN: (home_in, done_in, in_grad, 3), GATE: (home_gate, done_gate, gate_grad, 1),
        UP: (home_up, done_up, up_grad, 1),
    }

    def back_copies(i):
        s = SLICED.index(i)
        found = []
        for k, (to, member) in enumerate(group):
            src = fin[i] if i == SMALL else fin[i].at[pl.ds(pl.multiple_of(member * piece, 16), piece), :]
            found.append(remote(src, home[i].at[t], back_send.at[s, k], back_recv.at[s, k], to))
        return found

    def back_start(i):
        for copy in back_copies(i):
            copy.start()
        if i == SMALL:
            home_small[t] = fin_small[...]
        else:
            home[i][t] = fin[i][pl.ds(pl.multiple_of(t * piece, 16), piece), :]

    def back_arrive(i):
        s = SLICED.index(i)
        for k, (to, member) in enumerate(group):
            dst = home[i].at[member]
            remote(dst, dst, back_send.at[s, k], back_recv.at[s, k], to).wait_recv()
        for copy in back_copies(i):
            copy.wait_send()

    stores = []

    def store(src, dst):
        copy = pltpu.make_async_copy(src, dst, store_sem.at[len(stores)])
        copy.start()
        stores.append(copy)

    def merge(i):
        for half in i if i in (GATE, UP) else (i,):
            back_arrive(half)
        source, target, result, parts = wholes[i]
        cols = source.shape[2] // parts
        run = cols // Q
        for part in range(parts):
            runs = [
                source[member, :, part * cols + k * run : part * cols + (k + 1) * run].astype(F32)
                for k in range(Q)
                for member in range(T)
            ]
            target[:, part * cols * T : (part + 1) * cols * T] = jnp.concatenate(runs, axis=1)
        store(target, result)

    def merge_small():
        back_arrive(SMALL)
        gains = home_small[0] + home_small[1] + home_small[2] + home_small[3]
        mine = gains
        for member in range(1, T):
            moved = jnp.concatenate([gains[:, member * width :], gains[:, : member * width]], axis=1)
            mine = jnp.where(t == member, moved, mine)
        done_small[...] = mine
        done_small[2:5, :] = home_small[t, 2:5, :]
        store(done_small, small_grad)

    loads["small"].wait()
    for copy in slices(SMALL):
        copy.start()
    loads[OUT].wait()
    z_launch(OUT, 0)
    x_copy(OUT, z).start()
    loads[DOWN].wait()
    x_copy(DOWN1, z).start()
    z_launch(DOWN1, 0)
    loads["in"].wait()
    split(raw_in, stage_in, w_in, 3)
    for copy in slices(IN):
        copy.start()
    slices_arrive(SMALL)
    z_launch(SMALL, 0)
    x_copy(SMALL, z).start()
    loads["gate"].wait()
    split(raw_gate, stage_gate, w_gate, 1)
    for i in GATE:
        for copy in slices(i):
            copy.start()
    for batch in range(2):
        loads["tokens%d" % batch].wait()
        gather_start(toks, 0, batch)
    slices_arrive(IN)
    z_launch(IN, 0)
    x_copy(IN, z).start()
    loads["up"].wait()
    split(raw_up, stage_up, w_up, 1)
    for i in UP:
        for copy in slices(i):
            copy.start()
    for i in (OUT, SMALL, IN):
        z_pass(i, 1, 0, True)
    loads["valid"].wait()
    for batch in range(2):
        loads["cot%d" % batch].wait()
        mine = pl.ds(pl.multiple_of(t * L, 16), L)
        column = jnp.transpose(jnp.broadcast_to(valid_rows[batch : batch + 1, :], (128, L)))[:, :1]
        seeds[batch, mine, :] = (seeds[batch, mine, :].astype(F32) * column).astype(BF16)
    for i in (OUT, SMALL, IN):
        z_pass(i, 2, 0, True)
    slices_arrive(GATE0)
    z_launch(GATE0, 0)
    x_copy(GATE0, z).start()
    gather_relay(toks, 0, 0)
    gather_relay(toks, 0, 1)
    for batch in range(2):
        gather_start(seeds, 1, batch)
    for i in (OUT, SMALL, IN):
        z_pass(i, 3, 0, True)
    x_arrive(SMALL)
    pieces = [
        jnp.concatenate(
            [w_small[k * 16 : k * 16 + 8, m * 128 : m * 128 + width].astype(F32) for m in range(T)], axis=1
        )
        for k in range(Q)
    ]
    params[...] = jnp.concatenate(pieces, axis=1)

    def norm_rows(ref, gain):
        block_ = ref.astype(F32)
        return (block_ * row_scale(block_) * gain).astype(BF16)

    for batch in range(2):
        gather_finish(toks, 0, batch)

        @pl.loop(0, GROUP // 64)
        def _(step, batch=batch):
            rows = pl.ds(pl.multiple_of(step * 64, 64), 64)
            normed_one[batch, rows, :] = norm_rows(toks[batch, rows, :], params[0:1, :])

    x_arrive(IN)
    for batch in range(2):
        for start, size in column_tiles(3 * CS, 256):
            projected[batch, :, start : start + size] = nn(normed_one[batch], w_in[:, start : start + size])
        gated[batch, 8 : 8 + GROUP, :] = projected[batch, :, :CS] * projected[batch, :, 2 * CS :]

    def halo_copies(batch):
        ahead = remote(
            gated.at[batch, pl.ds(GROUP, 8), :], gated.at[batch, pl.ds(0, 8), :],
            halo_send.at[0, batch], halo_recv.at[0, batch], over_next,
        )
        back = remote(
            conv.at[batch, pl.ds(0, 8), :], conv.at[batch, pl.ds(GROUP, 8), :],
            halo_send.at[1, batch], halo_recv.at[1, batch], over_prev,
        )
        return ahead, back

    for batch in range(2):
        halo_copies(batch)[0].start()
    slices_arrive(UP0)
    z_launch(UP0, 0)
    x_copy(UP0, z).start()
    z_pass(GATE0, 1, 0, True)
    my_lanes = pl.ds(pl.multiple_of(t * 128, 128), 128)
    taps = jnp.concatenate(
        [w_small[k * 16 : k * 16 + 8, my_lanes].astype(F32)[2:5, :width] for k in range(Q)], axis=1
    )
    def mix(batch):
        halo_copies(batch)[0].wait_recv()

        @pl.when(q == 0)
        def _():
            gated[batch, 0:8, :] = jnp.zeros((8, CS), F32)

        for r in range(0, GROUP, HALF):
            value = (
                taps[0:1] * gated[batch, r + 6 : r + 6 + HALF, :]
                + taps[1:2] * gated[batch, r + 7 : r + 7 + HALF, :]
                + taps[2:3] * gated[batch, r + 8 : r + 8 + HALF, :]
            )
            branch[batch, r : r + HALF, :] = (projected[batch, r : r + HALF, CS : 2 * CS] * value).astype(BF16)

    z_pass(GATE0, 2, 0, True)
    x_arrive(OUT)

    def product_out(batch, start, put):
        rows = pl.ds(pl.multiple_of(start, 16), HALF)
        for at, size in column_tiles(D, 512):
            put(slice(at, at + size), nn(branch[batch, rows, :], w_out[:, at : at + size]))

    parts_begin(0, product_out, mix)
    z_pass(GATE0, 3, 0, True)
    z_pass(UP0, 1, 0, True)
    parts_middle(0)
    slices_arrive(GATE1)
    z_launch(GATE1, 0)
    x_copy(GATE1, z).start()
    gather_relay(seeds, 1, 0)
    gather_relay(seeds, 1, 1)
    z_pass(UP0, 2, 0, True)
    for batch in range(2):
        mine = pl.ds(pl.multiple_of(t * L, 16), L)
        hidden[batch] = toks[batch, mine, :].astype(F32) + parts_end(0, batch)
        normed_two[batch, mine, :] = norm_rows(hidden[batch], params[1:2, :])
        gather_start(normed_two, 2, batch)
    z_pass(UP0, 3, 0, True)
    slices_arrive(UP1)
    z_launch(UP1, 0)
    x_copy(UP1, z).start()
    z_pass(GATE1, 1, 0, True)
    z_launch(DOWN, 0)
    x_copy(DOWN1, z, True).wait_recv()
    z_launch(DOWN1, 1)
    gather_relay(normed_two, 2, 0)
    gather_relay(normed_two, 2, 1)
    z_pass(GATE1, 2, 0, True)
    for batch in range(2):
        gather_finish(normed_two, 2, batch)
        gather_finish(seeds, 1, batch)
    z_pass(GATE1, 3, 0, True)
    z_pass(UP1, 1, 0, True)

    x_arrive(GATE0)
    x_arrive(UP0)
    for i in SLICED:
        for copy in slices(i):
            copy.wait_send()

    def feed_forward(batch, part):
        for r in range(0, GROUP, HALF):
            for start, size in column_tiles(part.stop - part.start, 384):
                cols = slice(part.start + start, part.start + start + size)
                rows = slice(r, r + HALF)
                left = normed_two[batch, rows, :]
                gate = nn(left, w_gate[:, cols])
                up = nn(left, w_up[:, cols])
                sig = 1.0 / (1.0 + jnp.exp(-gate))
                act = gate * sig
                silu[batch, rows, cols] = act.astype(BF16)
                slope[batch, rows, cols] = (up * sig * (1.0 + gate * (1.0 - sig))).astype(BF16)
                activated[batch, rows, cols] = (act * up).astype(BF16)

    def weight_grad(dst, left, right, most_rows, most_cols):
        for a, rows in column_tiles(dst.shape[0], most_rows):
            for b, cols in column_tiles(dst.shape[1], most_cols):
                value = tn(left[0, :, a : a + rows], right[0, :, b : b + cols])
                value = value + tn(left[1, :, a : a + rows], right[1, :, b : b + cols])
                dst[a : a + rows, b : b + cols] = value.astype(BF16)

    feed_forward(0, halves[0])
    z_pass(UP1, 2, 0, True)
    feed_forward(1, halves[0])
    weight_grad(g_down.at[pl.ds(0, cut), :], activated.at[:, :, pl.ds(0, cut)], seeds, 384, 512)
    z_pass(UP1, 3, 0, True)
    x_copy(DOWN, z).start()

    def down_pass(j):
        z_pass(DOWN, j, 0, True)
        z_pass(DOWN1, j, 0, False)
        z_pass(DOWN1, j, 1, False)

    down_pass(1)
    x_arrive(GATE1)
    x_arrive(UP1)
    feed_forward(0, halves[1])
    down_pass(2)
    feed_forward(1, halves[1])
    down_pass(3)
    weight_grad(g_down.at[pl.ds(cut, FS - cut), :], activated.at[:, :, pl.ds(cut, FS - cut)], seeds, 384, 512)
    reduce_start(DOWN, range(Z))

    x_arrive(DOWN)
    def seed_batch(batch):
        for r in range(0, GROUP, HALF):
            for start, size in column_tiles(FS, 384):
                cols = slice(start, start + size)
                rows = slice(r, r + HALF)
                act_grad = nt(seeds[batch, rows, :], w_down[cols, :])
                silu[batch, rows, cols] = (act_grad * silu[batch, rows, cols].astype(F32)).astype(BF16)
                slope[batch, rows, cols] = (act_grad * slope[batch, rows, cols].astype(F32)).astype(BF16)

    up_seed, gate_seed = silu, slope

    def product_ffn(batch, start, put):
        rows = pl.ds(pl.multiple_of(start, 16), HALF)
        for at, size in column_tiles(D, 512):
            put(
                slice(at, at + size),
                nt(gate_seed[batch, rows, :], w_gate[at : at + size, :])
                + nt(up_seed[batch, rows, :], w_up[at : at + size, :]),
            )

    def product_down(batch, start, put):
        rows = pl.ds(pl.multiple_of(start, 16), HALF)
        for at, size in column_tiles(D, 512):
            put(slice(at, at + size), nn(activated[batch, rows, :], w_down[:, at : at + size]))

    parts_begin(2, product_ffn, seed_batch)
    parts_middle(2)
    reduce_pass(DOWN, 1)
    for i in (IN, OUT, *GATE, *UP, DOWN, SMALL, DOWN1):
        z_settle(i, 0)
        if i == DOWN1:
            z_settle(i, 1)
            x_copy(i, z).wait_send()
        else:
            x_settle(i)
    for i, part in zip(GATE, halves):
        weight_grad(grads[i], normed_two, gate_seed.at[:, :, pl.ds(part.start, part.stop - part.start)], 256, 384)
        reduce_start(i)
    reduce_pass(DOWN, 2)
    weight_grad(w_up, normed_two, up_seed, 256, 384)
    pass
    reduce_pass(DOWN, 3)
    gain_two = jnp.zeros((1, D), F32)
    for batch in range(2):
        mine = pl.ds(pl.multiple_of(t * L, 16), L)
        n2g = parts_end(2, batch)
        hid = hidden[batch]
        scale = row_scale(hid)
        gain_two = gain_two + jnp.sum(n2g * hid * scale, axis=0, keepdims=True)
        scaled = n2g * params[1:2, :]
        value = (
            seeds[batch, mine, :].astype(F32)
            + scale * scaled
            - hid * (scale * scale * scale) * jnp.mean(scaled * hid, axis=-1, keepdims=True)
        )
        hidden_grad[batch] = value
        out_seed[batch, mine, :] = value.astype(BF16)
        gather_start(out_seed, 3, batch)
    parts_begin(1, product_down)
    gather_relay(out_seed, 3, 0)
    gather_relay(out_seed, 3, 1)
    parts_middle(1)
    reduce_pass(GATE0, 1)
    for batch in range(2):
        gather_finish(out_seed, 3, batch)
        for r in range(0, GROUP, HALF):
            rows = slice(r, r + HALF)
            branch_grad = nt(out_seed[batch, rows, :], w_out[...])
            conv_grad = branch_grad * projected[batch, rows, CS : 2 * CS]
            conv[batch, rows, :] = conv_grad
            mixed = (
                taps[0:1] * gated[batch, r + 6 : r + 6 + HALF, :]
                + taps[1:2] * gated[batch, r + 7 : r + 7 + HALF, :]
                + taps[2:3] * gated[batch, r + 8 : r + 8 + HALF, :]
            )
            proj_seed[batch, rows, CS : 2 * CS] = (branch_grad * mixed).astype(BF16)
        halo_copies(batch)[1].start()
    reduce_start(UP0)
    reduce_start(UP1)
    kernel_grad = [jnp.zeros((1, CS), F32) for _ in range(3)]
    for batch in range(2):
        for r in range(0, GROUP, HALF):
            conv_grad = conv[batch, r : r + HALF, :]
            for k in range(3):
                kernel_grad[k] = kernel_grad[k] + jnp.sum(
                    conv_grad * gated[batch, r + 6 + k : r + 6 + k + HALF, :], axis=0, keepdims=True
                )
    weight_grad(w_out, branch, out_seed, 256, 512)
    reduce_pass(GATE0, 2)
    reduce_pass(GATE0, 3)
    def unmix(batch):
        halo_copies(batch)[1].wait_recv()

        @pl.when(q == Q - 1)
        def _():
            conv[batch, GROUP : GROUP + 8, :] = jnp.zeros((8, CS), F32)

        for r in range(0, GROUP, HALF):
            rows = slice(r, r + HALF)
            value = (
                taps[2:3] * conv[batch, r : r + HALF, :]
                + taps[1:2] * conv[batch, r + 1 : r + 1 + HALF, :]
                + taps[0:1] * conv[batch, r + 2 : r + 2 + HALF, :]
            )
            proj_seed[batch, rows, :CS] = (value * projected[batch, rows, 2 * CS :]).astype(BF16)
            proj_seed[batch, rows, 2 * CS :] = (value * projected[batch, rows, :CS]).astype(BF16)

    def product_in(batch, start, put):
        rows = pl.ds(pl.multiple_of(start, 16), HALF)
        for at, size in column_tiles(D, 512):
            put(slice(at, at + size), nt(proj_seed[batch, rows, :], w_in[at : at + size, :]))

    for batch in range(2):
        mine = pl.ds(pl.multiple_of(t * L, 16), L)
        seeds[batch, mine, :] = (hidden[batch] + parts_end(1, batch)).astype(BF16)
    out_copies = [
        pltpu.make_async_copy(block(seeds, batch, t), block_out.at[batch], local_sem.at[2 + batch])
        for batch in range(2)
    ]
    for copy in out_copies:
        copy.start()
    parts_begin(3, product_in, unmix)
    parts_middle(3)
    reduce_pass(GATE1, 1)
    weight_grad(w_in, normed_one, proj_seed, 256, 384)
    reduce_start(IN)
    reduce_start(OUT)
    reduce_pass(GATE1, 2)
    reduce_pass(GATE1, 3)
    reduce_end(DOWN)
    store(fin_down, down_grad)
    gain_one = jnp.zeros((1, D), F32)
    for batch in range(2):
        mine = pl.ds(pl.multiple_of(t * L, 16), L)
        n1g = parts_end(3, batch)
        inputs = toks[batch, mine, :].astype(F32)
        scale = row_scale(inputs)
        gain_one = gain_one + jnp.sum(n1g * inputs * scale, axis=0, keepdims=True)
        scaled = n1g * params[0:1, :]
        hidden_grad[batch] = (
            hidden_grad[batch]
            + scale * scaled
            - inputs * (scale * scale * scale) * jnp.mean(scaled * inputs, axis=-1, keepdims=True)
        )
    grad_copy = pltpu.make_async_copy(hidden_grad, input_grad, local_sem.at[1])
    grad_copy.start()
    for k in range(Q):
        lanes = slice(k * 128, (k + 1) * 128)
        runs = [jnp.pad(g[:, k * width : (k + 1) * width], ((0, 0), (0, 128 - width))) for g in kernel_grad]
        rows = [gain_one[:, lanes], gain_two[:, lanes], *runs, jnp.zeros((3, 128), F32)]
        g_small[k * 8 : (k + 1) * 8, :] = jnp.concatenate(rows, axis=0)
    reduce_start(SMALL)
    reduce_pass(UP0, 1)
    reduce_pass(UP0, 2)
    reduce_end(GATE0)
    back_start(GATE0)
    reduce_pass(UP0, 3)
    reduce_end(GATE1)
    back_start(GATE1)
    for step in (1, 2, 3):
        reduce_pass(UP1, step)
    merge(GATE)
    for step in (1, 2, 3):
        reduce_pass(IN, step)
    reduce_end(UP0)
    back_start(UP0)
    reduce_end(UP1)
    back_start(UP1)
    for i in (OUT, SMALL):
        for step in (1, 2, 3):
            reduce_pass(i, step)
    reduce_end(IN)
    back_start(IN)
    reduce_end(OUT)
    store(fin_out, out_grad)
    reduce_end(SMALL)
    back_start(SMALL)
    merge(UP)
    for batch in range(2):
        for copy in halo_copies(batch):
            copy.wait_send()
    merge(IN)
    merge_small()
    for copy in stores:
        copy.wait()
    for copy in out_copies:
        copy.wait()
    grad_copy.wait()


def hand_over(*refs):
    count = (len(refs) - 2) // 3
    sources, targets, held = refs[:count], refs[count : 2 * count], refs[2 * count : 3 * count]
    load_sem, store_sem = refs[3 * count :]
    loads = [pltpu.make_async_copy(sources[k], held[k], load_sem.at[k]) for k in range(count)]
    stores = [pltpu.make_async_copy(held[k], targets[k], store_sem.at[k]) for k in range(count)]
    for load in loads:
        load.start()
    for load, store in zip(loads, stores):
        load.wait()
        store.start()
    for store in stores:
        store.wait()


def fused(plan, tokens, cotangent, lengths, loss_mask, norm_gain, in_weight, conv_kernel, out_weight, ffn_gain, gate_weight, up_weight, down_weight):
    Z, Q, T = plan["Z"], plan["Q"], 4
    L, D, FS, CS = plan["L"], plan["D"], plan["FS"], plan["CS"]
    width, hid, rows = out_weight.shape[0], down_weight.shape[0], in_weight.shape[0]
    place = lax.axis_index(("wide", "narrow"))
    positions = place * L + jnp.arange(L, dtype=jnp.int32)
    valid = ((positions[None, :] < lengths[:, None]) & (loss_mask != 0)).astype(F32)
    valid = jnp.pad(valid, ((0, 6), (0, 0)))
    small = jnp.concatenate([norm_gain[None], ffn_gain[None], conv_kernel], axis=0)
    small = jnp.pad(small, ((0, 11), (0, 128 - width)))

    shapes = [(T * rows, 3 * CS), (width, D), (T * rows, FS), (T * rows, FS), (hid, D)]
    vm, dma = pltpu.VMEM, pltpu.SemaphoreType.DMA
    group = T * L
    scratch = [vm((Q * r, k), BF16) for r, k in shapes]
    scratch += [vm((Q * 16, T * 128), BF16), vm((Q * hid, D), BF16), vm((Q * 8, 128), F32)]
    scratch += [vm((Z, r, k), BF16) for r, k in shapes] + [vm((Z, 8, 128), F32)]
    scratch += [vm((Z - 1, r, k), BF16) for r, k in shapes] + [vm((Z - 1, 8, 128), F32)]
    scratch += [vm((r, k), BF16) for r, k in shapes] + [vm((8, 128), F32)]
    scratch += [vm((r, k), F32 if r in (width, hid) else BF16) for r, k in shapes]
    scratch += [vm((8, 128), F32)]
    scratch += [vm((T, rows, 3 * CS), BF16), vm((T, rows, FS), BF16), vm((T, rows, FS), BF16), vm((T, 8, 128), F32)]
    scratch += [vm(a.shape, F32) for a in (in_weight, gate_weight, up_weight)] + [vm((8, 128), F32)]
    scratch += [vm(a.shape, BF16) for a in (in_weight, gate_weight, up_weight)] + [vm((8, L), F32), vm((8, D), F32)]
    scratch += [vm((2, group, D), BF16) for _ in range(5)]
    scratch += [vm((2, L, D), F32), vm((2, L, D), F32)]
    scratch += [
        vm((2, group, 3 * CS), F32), vm((2, group + 8, CS), F32), vm((2, group + 8, CS), F32),
        vm((2, group, CS), BF16), vm((2, group, 3 * CS), BF16),
    ]
    scratch += [vm((2, group, FS), BF16) for _ in range(3)]
    scratch += [
        vm((2, 2 * L, D), BF16), vm((2, 2, 2 * L, D), BF16),
        vm((2, L, D), BF16), vm((2, 2, L, D), BF16), vm((2, 2 * L, D), F32),
    ]
    scratch += [
        dma((11,)), dma((6, 3)), dma((6, 3)),
        dma((9, Z - 1, 2)), dma((9, Z - 1, 2)), dma((9, Z - 1, 2)), dma((9, Z - 1, 2)),
        dma((9, Z)), dma((9, Z)),
        dma((4, 2, 3)), dma((4, 2, 3)), dma((4, 2, 2)), dma((4, 2, 2)), dma((2, 2)), dma((2, 2)),
        dma((8, Z)), dma((8, Z)), dma((8, Z - 1)), dma((8, Z - 1)), dma((8,)), dma((8,)), dma((6, 3)), dma((6, 3)), dma((6,)),
    ]
    out_shape = (
        jax.ShapeDtypeStruct((2, L, D), BF16),
        jax.ShapeDtypeStruct((2, L, D), F32),
        jax.ShapeDtypeStruct(in_weight.shape, F32),
        jax.ShapeDtypeStruct(out_weight.shape, F32),
        jax.ShapeDtypeStruct(gate_weight.shape, F32),
        jax.ShapeDtypeStruct(up_weight.shape, F32),
        jax.ShapeDtypeStruct(down_weight.shape, F32),
        jax.ShapeDtypeStruct((8, 128), F32),
    )
    block_out, input_grad, in_g, out_g, gate_g, up_g, down_g, small_g = pl.pallas_call(
        functools.partial(block_kernel, plan),
        out_shape=out_shape,
        in_specs=[pl.BlockSpec(memory_space=pl.ANY)] * 9,
        out_specs=[pl.BlockSpec(memory_space=pl.ANY)] * 8,
        scratch_shapes=scratch,
        compiler_params=pltpu.CompilerParams(
            collective_id=0, has_side_effects=True, vmem_limit_bytes=VMEM_LIMIT
        ),
    )(tokens, cotangent, valid, small, in_weight, out_weight, gate_weight, up_weight, down_weight)
    arrays = (block_out, input_grad, in_g, out_g, gate_g, up_g, down_g)
    block_out, input_grad, in_g, out_g, gate_g, up_g, down_g = pl.pallas_call(
        hand_over,
        out_shape=tuple(jax.ShapeDtypeStruct(a.shape, a.dtype) for a in arrays),
        in_specs=[pl.BlockSpec(memory_space=pltpu.HBM)] * len(arrays),
        out_specs=[pl.BlockSpec(memory_space=pltpu.HBM)] * len(arrays),
        scratch_shapes=[vm(a.shape, a.dtype) for a in arrays] + [dma((len(arrays),)), dma((len(arrays),))],
        compiler_params=pltpu.CompilerParams(vmem_limit_bytes=VMEM_LIMIT),
    )(*arrays)
    return (
        block_out, input_grad, small_g[0, :width], in_g, small_g[2:5, :width], out_g, small_g[1, :width],
        gate_g, up_g, down_g,
    )


def planned(wide, narrow, arrays):
    tokens, in_weight, down_weight = arrays[0], arrays[5], arrays[11]
    if narrow != 2 or wide != 16 or tokens.shape[0] != 2:
        return None
    groups = wide // 2
    rows, hid = in_weight.shape[0], down_weight.shape[0]
    sizes = {
        "Z": groups // 2, "Q": groups, "L": tokens.shape[1], "D": tokens.shape[2],
        "FS": hid * groups, "CS": rows * groups,
    }
    if rows % 16 or hid % 16 or sizes["L"] != 128 or sizes["FS"] % 128 or sizes["CS"] % 128 or rows != 32:
        return None
    return sizes


def solution(mesh):
    in_specs = (
        P(None, ("wide", "narrow"), None),
        P(None, ("wide", "narrow"), None),
        P(),
        P(None, ("wide", "narrow")),
        P(("wide", "narrow")),
        P(("wide", "narrow"), None),
        P(None, ("wide", "narrow")),
        P(("wide", "narrow"), None),
        P(("wide", "narrow")),
        P(("wide", "narrow"), None),
        P(("wide", "narrow"), None),
        P(("wide", "narrow"), None),
    )
    out_specs = (
        P(None, ("wide", "narrow"), None),
        P(None, ("wide", "narrow"), None),
        P(("wide", "narrow")),
        P(("wide", "narrow"), None),
        P(None, ("wide", "narrow")),
        P(("wide", "narrow"), None),
        P(("wide", "narrow")),
        P(("wide", "narrow"), None),
        P(("wide", "narrow"), None),
        P(("wide", "narrow"), None),
    )
    wide, narrow = mesh.shape["wide"], mesh.shape["narrow"]

    def step(*arrays):
        plan = planned(wide, narrow, arrays)
        run = body if plan is None else functools.partial(fused, plan)
        return run(*arrays)

    return jax.shard_map(step, mesh=mesh, in_specs=in_specs, out_specs=out_specs, check_vma=False)
```

```python
import functools

import jax
import jax.numpy as jnp
from jax import lax
from jax.experimental import pallas as pl
from jax.experimental.pallas import tpu as pltpu
from jax.sharding import PartitionSpec as P

EPSILON = 1e-05


def shifted(block, axis, distance):
    devices = range(lax.axis_size(axis))
    route = [(i - distance, i) for i in devices if i - distance in devices]
    return lax.ppermute(block, axis, route)


def along_rows(left, weight):
    return lax.dot_general(
        left, weight, (((1,), (1,)), ((), ())), preferred_element_type=jnp.float32
    )


def over_rows(left, right):
    return lax.dot_general(
        left, right, (((0,), (0,)), ((), ())), preferred_element_type=jnp.float32
    )


def collect(shards):
    partial_set = (
        lax.all_gather(shards[0], "narrow", axis=0, tiled=True),
        lax.all_gather(shards[1], "narrow", axis=0, tiled=True),
        lax.all_gather(shards[2], "narrow", axis=1, tiled=True),
        lax.all_gather(shards[3], "narrow", axis=0, tiled=True),
        lax.all_gather(shards[4], "narrow", axis=0, tiled=True),
        lax.all_gather(shards[5], "narrow", axis=0, tiled=True),
        lax.all_gather(shards[6], "narrow", axis=0, tiled=True),
        lax.all_gather(shards[7], "narrow", axis=0, tiled=True),
    )
    return (
        lax.all_gather(partial_set[0], "wide", axis=0, tiled=True),
        lax.all_gather(partial_set[1], "wide", axis=0, tiled=True),
        lax.all_gather(partial_set[2], "wide", axis=1, tiled=True),
        lax.all_gather(partial_set[3], "wide", axis=0, tiled=True),
        lax.all_gather(partial_set[4], "wide", axis=0, tiled=True),
        lax.all_gather(partial_set[5], "wide", axis=0, tiled=True),
        lax.all_gather(partial_set[6], "wide", axis=0, tiled=True),
        lax.all_gather(partial_set[7], "wide", axis=0, tiled=True),
    )


def collect_tied(shards, anchor):
    tied_shards, _ = lax.optimization_barrier((shards, anchor))
    return collect(tied_shards)


def body(
    tokens,
    cotangent,
    lengths,
    loss_mask,
    norm_gain,
    in_weight,
    conv_kernel,
    out_weight,
    ffn_gain,
    gate_weight,
    up_weight,
    down_weight,
):
    micro_count = tokens.shape[0]
    local_rows = tokens.shape[1]
    width = tokens.shape[2]
    shards = (
        norm_gain,
        in_weight,
        conv_kernel,
        out_weight,
        ffn_gain,
        gate_weight,
        up_weight,
        down_weight,
    )
    positions = lax.axis_index(("wide", "narrow")) * local_rows + jnp.arange(
        local_rows, dtype=jnp.int32
    )
    gain_one_grad = jnp.zeros((width,), jnp.float32)
    gain_two_grad = jnp.zeros((width,), jnp.float32)
    kernel_grad = jnp.zeros((3, width), jnp.float32)
    outputs = []
    input_grads = []
    kept_normed_one = []
    kept_proj_seed = []
    kept_branch = []
    kept_out_seed = []
    kept_normed_two = []
    kept_gate_seed = []
    kept_up_seed = []
    kept_activated = []
    kept_down_seed = []
    for batch in range(micro_count):
        gathered = collect_tied(shards, tokens[batch])
        gain_full, in_full, kernel_full, out_full, ffn_full, gate_full, up_full, down_full = (
            gathered
        )
        gain_f32 = gain_full.astype(jnp.float32)
        ffn_f32 = ffn_full.astype(jnp.float32)
        kernel_f32 = kernel_full.astype(jnp.float32)
        inputs = tokens[batch].astype(jnp.float32)
        scale_one = lax.rsqrt(jnp.mean(inputs * inputs, axis=-1, keepdims=True) + EPSILON)
        normed_one = (inputs * scale_one * gain_f32).astype(jnp.bfloat16)
        projected = jnp.dot(normed_one, in_full, preferred_element_type=jnp.float32)
        b_gate = projected[:, :width]
        c_gate = projected[:, width : 2 * width]
        conv_input = projected[:, 2 * width :]
        gated_input = b_gate * conv_input
        earlier = shifted(gated_input[local_rows - 2 :], ("wide", "narrow"), 1)
        padded = jnp.concatenate([earlier, gated_input], axis=0)
        mixed_conv = (
            kernel_f32[0] * padded[:-2] + kernel_f32[1] * padded[1:-1] + kernel_f32[2] * gated_input
        )
        branch = (c_gate * mixed_conv).astype(jnp.bfloat16)
        hidden = inputs + jnp.dot(branch, out_full, preferred_element_type=jnp.float32)
        scale_two = lax.rsqrt(jnp.mean(hidden * hidden, axis=-1, keepdims=True) + EPSILON)
        normed_two = (hidden * scale_two * ffn_f32).astype(jnp.bfloat16)
        gate_out = jnp.dot(normed_two, gate_full, preferred_element_type=jnp.float32)
        up_out = jnp.dot(normed_two, up_full, preferred_element_type=jnp.float32)
        sigmoid_gate = jax.nn.sigmoid(gate_out)
        silu_gate = gate_out * sigmoid_gate
        activated = (silu_gate * up_out).astype(jnp.bfloat16)
        result = hidden + jnp.dot(activated, down_full, preferred_element_type=jnp.float32)
        outputs.append(result.astype(jnp.bfloat16))
        validity = (positions < lengths[batch]).astype(jnp.float32) * loss_mask[batch].astype(
            jnp.float32
        )
        seed = cotangent[batch].astype(jnp.float32) * validity[:, None]
        down_seed = seed.astype(jnp.bfloat16)
        act_grad = along_rows(down_seed, down_full)
        up_seed = (act_grad * silu_gate).astype(jnp.bfloat16)
        gate_seed = (
            act_grad * up_out * sigmoid_gate * (1.0 + gate_out * (1.0 - sigmoid_gate))
        ).astype(jnp.bfloat16)
        normed_two_grad = along_rows(gate_seed, gate_full) + along_rows(up_seed, up_full)
        gain_two_grad = gain_two_grad + jnp.sum(normed_two_grad * hidden * scale_two, axis=0)
        scaled_two = normed_two_grad * ffn_f32
        hidden_grad = (
            seed
            + scale_two * scaled_two
            - hidden
            * (scale_two * scale_two * scale_two)
            * jnp.mean(scaled_two * hidden, axis=-1, keepdims=True)
        )
        out_seed = hidden_grad.astype(jnp.bfloat16)
        branch_grad = along_rows(out_seed, out_full)
        c_grad = branch_grad * mixed_conv
        conv_grad = branch_grad * c_gate
        kernel_grad = kernel_grad + jnp.stack(
            [
                jnp.sum(conv_grad * padded[:-2], axis=0),
                jnp.sum(conv_grad * padded[1:-1], axis=0),
                jnp.sum(conv_grad * gated_input, axis=0),
            ],
            axis=0,
        )
        later = shifted(conv_grad[:2], ("wide", "narrow"), -1)
        extended = jnp.concatenate([conv_grad, later], axis=0)
        gated_grad = (
            kernel_f32[2] * conv_grad
            + kernel_f32[1] * extended[1 : local_rows + 1]
            + kernel_f32[0] * extended[2:]
        )
        proj_seed = jnp.concatenate(
            [gated_grad * conv_input, c_grad, gated_grad * b_gate], axis=1
        ).astype(jnp.bfloat16)
        normed_one_grad = along_rows(proj_seed, in_full)
        gain_one_grad = gain_one_grad + jnp.sum(normed_one_grad * inputs * scale_one, axis=0)
        scaled_one = normed_one_grad * gain_f32
        input_grads.append(
            hidden_grad
            + scale_one * scaled_one
            - inputs
            * (scale_one * scale_one * scale_one)
            * jnp.mean(scaled_one * inputs, axis=-1, keepdims=True)
        )
        kept_normed_one.append(normed_one)
        kept_proj_seed.append(proj_seed)
        kept_branch.append(branch)
        kept_out_seed.append(out_seed)
        kept_normed_two.append(normed_two)
        kept_gate_seed.append(gate_seed)
        kept_up_seed.append(up_seed)
        kept_activated.append(activated)
        kept_down_seed.append(down_seed)
    all_normed_two = jnp.concatenate(kept_normed_two, axis=0)
    in_grad = over_rows(
        jnp.concatenate(kept_normed_one, axis=0), jnp.concatenate(kept_proj_seed, axis=0)
    )
    out_grad = over_rows(
        jnp.concatenate(kept_branch, axis=0), jnp.concatenate(kept_out_seed, axis=0)
    )
    gate_grad = over_rows(all_normed_two, jnp.concatenate(kept_gate_seed, axis=0))
    up_grad = over_rows(all_normed_two, jnp.concatenate(kept_up_seed, axis=0))
    down_grad = over_rows(
        jnp.concatenate(kept_activated, axis=0), jnp.concatenate(kept_down_seed, axis=0)
    )
    gain_one_part, in_part, kernel_part, out_part, gain_two_part, gate_part, up_part, down_part = (
        lax.psum_scatter(gain_one_grad, "wide", scatter_dimension=0, tiled=True),
        lax.psum_scatter(in_grad, "wide", scatter_dimension=0, tiled=True),
        lax.psum_scatter(kernel_grad, "wide", scatter_dimension=1, tiled=True),
        lax.psum_scatter(out_grad, "wide", scatter_dimension=0, tiled=True),
        lax.psum_scatter(gain_two_grad, "wide", scatter_dimension=0, tiled=True),
        lax.psum_scatter(gate_grad, "wide", scatter_dimension=0, tiled=True),
        lax.psum_scatter(up_grad, "wide", scatter_dimension=0, tiled=True),
        lax.psum_scatter(down_grad, "wide", scatter_dimension=0, tiled=True),
    )
    gain_one_sum, in_sum, kernel_sum, out_sum, gain_two_sum, gate_sum, up_sum, down_sum = (
        lax.psum_scatter(gain_one_part, "narrow", scatter_dimension=0, tiled=True),
        lax.psum_scatter(in_part, "narrow", scatter_dimension=0, tiled=True),
        lax.psum_scatter(kernel_part, "narrow", scatter_dimension=1, tiled=True),
        lax.psum_scatter(out_part, "narrow", scatter_dimension=0, tiled=True),
        lax.psum_scatter(gain_two_part, "narrow", scatter_dimension=0, tiled=True),
        lax.psum_scatter(gate_part, "narrow", scatter_dimension=0, tiled=True),
        lax.psum_scatter(up_part, "narrow", scatter_dimension=0, tiled=True),
        lax.psum_scatter(down_part, "narrow", scatter_dimension=0, tiled=True),
    )
    block_out = jnp.stack(outputs, axis=0)
    input_grad = jnp.stack(input_grads, axis=0)
    return (
        block_out,
        input_grad,
        gain_one_sum,
        in_sum,
        kernel_sum,
        out_sum,
        gain_two_sum,
        gate_sum,
        up_sum,
        down_sum,
    )


MESH = pl.DeviceIdType.MESH
BF16, F32 = jnp.bfloat16, jnp.float32
VMEM_LIMIT = 62 * 1024 * 1024


def nn(a, b):
    return lax.dot_general(a, b, (((1,), (0,)), ((), ())), preferred_element_type=F32)


def nt(a, b):
    return lax.dot_general(a, b, (((1,), (1,)), ((), ())), preferred_element_type=F32)


def tn(a, b):
    return lax.dot_general(a, b, (((0,), (0,)), ((), ())), preferred_element_type=F32)


def column_tiles(total, most):
    units = total // 128
    count = -(-units // (most // 128))
    edges = [-(-units * k // count) * 128 for k in range(count + 1)]
    return [(a, b - a) for a, b in zip(edges, edges[1:])]


def row_scale(block):
    return lax.rsqrt(jnp.mean(block * block, axis=-1, keepdims=True) + EPSILON)


IN, OUT, GATE0, GATE1, UP0, UP1, DOWN, SMALL, DOWN1 = range(9)
GATE, UP = (GATE0, GATE1), (UP0, UP1)
SLICED = (IN, GATE0, GATE1, UP0, UP1, SMALL)
LANES = (0, 0, 1, 1)


def block_kernel(
    plan,
    tokens, cotangent, valid, small, in_weight, out_own, gate_weight, up_weight, down_own,
    block_out, input_grad, in_grad, out_grad, gate_grad, up_grad, down_grad, small_grad,
    w_in, w_out, w_gate, w_up, w_down, w_small, g_down, g_small,
    rx_in, rx_out, rx_gate, rx_up, rx_down, rx_small,
    rz_in, rz_out, rz_gate, rz_up, rz_down, rz_small,
    via_in, via_out, via_gate, via_up, via_down, via_small,
    fin_in, fin_out, fin_gate, fin_up, fin_down, fin_small,
    home_in, home_gate, home_up, home_small, done_in, done_gate, done_up, done_small,
    raw_in, raw_gate, raw_up, valid_rows, params,
    toks, seeds, normed_one, normed_two, out_seed,
    hidden, hidden_grad,
    projected, gated, conv, branch, proj_seed,
    silu, slope, activated,
    core_send, core_recv, side_send, side_recv, keep,
    local_sem, a_send, a_recv, up_send, up_recv, dn_send, dn_recv, x_send, x_recv,
    gather_send, gather_recv, part_send, part_recv, halo_send, halo_recv,
    rx_send, rx_recv, rz_send, rz_recv, via_send, via_recv, back_send, back_recv, store_sem,
):
    Z, X, N, T, Q = plan["Z"], 2, 2, 4, plan["Z"] * 2
    L, D, FS, CS = plan["L"], plan["D"], plan["FS"], plan["CS"]
    HALF, GROUP = 2 * L, 4 * L
    wide, n = lax.axis_index("wide"), lax.axis_index("narrow")
    c, q = lax.rem(wide, 2), wide // 2
    x, z = lax.rem(q, X), q // X
    t = c * N + n

    def device(z_, x_, c_, n_):
        return ((z_ * X + x_) * 2 + c_, n_)

    over_core = device(z, x, 1 - c, n)
    over_side = device(z, x, c, 1 - n)
    over_both = device(z, x, 1 - c, 1 - n)
    over_x = device(z, 1 - x, c, n)
    z_ahead = [lax.rem(z + k, Z) for k in range(Z)]
    z_behind = [lax.rem(z - k + Z, Z) for k in range(Z)]
    q_next, q_prev = lax.rem(q + 1, Q), lax.rem(q - 1 + Q, Q)
    over_next, over_prev = (q_next * 2 + c, n), (q_prev * 2 + c, n)

    def remote(src, dst, send, recv, to):
        return pltpu.make_async_remote_copy(
            src_ref=src, dst_ref=dst, send_sem=send, recv_sem=recv, device_id=to, device_id_type=MESH
        )

    cut = -(-FS // 256) * 128
    halves = (slice(0, cut), slice(cut, FS))

    def views(in_, out, gate, up, down, small_):
        def half(ref, cols):
            return None if ref is None else ref.at[..., pl.ds(cols.start, cols.stop - cols.start)]

        return (in_, out, *(half(gate, h) for h in halves), *(half(up, h) for h in halves), down, small_)

    weights = views(w_in, w_out, w_gate, w_up, w_down.at[:, pl.ds(0, D // 2)], w_small)
    weights += (w_down.at[:, pl.ds(D // 2, D - D // 2)],)
    grads = views(w_in, w_out, w_gate, w_up, g_down, g_small)
    rx = views(rx_in, rx_out, rx_gate, rx_up, rx_down, rx_small)
    rz = views(rz_in, rz_out, rz_gate, rz_up, rz_down, rz_small)
    via = views(via_in, via_out, via_gate, via_up, via_down, via_small)
    fin = views(fin_in, fin_out, fin_gate, fin_up, fin_down, fin_small)
    home = views(home_in, None, home_gate, home_up, None, home_small)
    piece = in_weight.shape[0]
    width = out_own.shape[0]
    stage_in = proj_seed.at[0, pl.ds(0, T * piece), :]
    stage_gate = silu.at[0, pl.ds(0, T * piece), :]
    stage_up = slope.at[0, pl.ds(0, T * piece), :]
    staged = views(stage_in, None, stage_gate, stage_up, None, None)

    def chunk_size(i):
        return weights[i].shape[0] // Q

    def chunk(refs, i, z_, x_):
        rows = refs[i].shape[0] // Q
        start = pl.multiple_of((z_ * X + x_) * rows, 8 if rows == 8 else 16)
        return refs[i].at[pl.ds(start, rows), :]

    def block(ref, batch, member, rows=L):
        return ref.at[batch, pl.ds(pl.multiple_of(member * L, 16), rows), :]

    def own_rows(i):
        start = q * T * piece + t * piece
        return weights[i].at[pl.ds(pl.multiple_of(start, 16), piece), :]

    def small_block(member):
        lanes = pl.ds(pl.multiple_of(member * 128, 128), 128)
        return w_small.at[pl.ds(pl.multiple_of(q * 16, 16), 16), lanes]

    loads = {}
    for name, src, dst in (
        ("small", small, small_block(t)),
        ("in", in_weight, raw_in),
        (OUT, out_own, chunk(weights, OUT, z, x)),
        (DOWN, down_own, chunk([w_down], 0, z, x)),
        ("tokens0", tokens.at[0], block(toks, 0, t)),
        ("tokens1", tokens.at[1], block(toks, 1, t)),
        ("gate", gate_weight, raw_gate),
        ("up", up_weight, raw_up),
        ("valid", valid, valid_rows),
        ("cot0", cotangent.at[0], block(seeds, 0, t)),
        ("cot1", cotangent.at[1], block(seeds, 1, t)),
    ):
        loads[name] = pltpu.make_async_copy(src, dst, local_sem.at[len(loads)])
        loads[name].start()

    barrier = pltpu.get_barrier_semaphore()
    partners = [over_core, over_side, over_both, over_x, over_next, over_prev]
    partners += [device(z_ahead[k], x, c, n) for k in range(1, Z)]
    for partner in partners:
        pl.semaphore_signal(barrier, inc=1, device_id=partner, device_id_type=MESH)
    pl.semaphore_wait(barrier, len(partners))

    group = [(over_core, (1 - c) * N + n), (over_side, c * N + 1 - n), (over_both, (1 - c) * N + 1 - n)]

    def split(raw, stage, full, parts):
        cols = raw.shape[1] // (parts * T)
        run = cols // Q
        for member in range(T):
            for part in range(parts):
                first = part * cols * T + member * run
                runs = [raw[:, first + k * T * run : first + (k * T + 1) * run].astype(F32) for k in range(Q)]
                stage[member * piece : (member + 1) * piece, part * cols : (part + 1) * cols] = (
                    jnp.concatenate(runs, axis=1).astype(BF16)
                )
        mine = stage[pl.ds(pl.multiple_of(t * piece, 16), piece), :]
        full[pl.ds(pl.multiple_of(q * T * piece + t * piece, 16), piece), :] = mine

    def slices(i):
        s = SLICED.index(i)
        found = []
        for k, (to, member) in enumerate(group):
            if i == SMALL:
                src, dst = small_block(t), small_block(t)
            else:
                src, dst = staged[i].at[pl.ds(pl.multiple_of(member * piece, 16), piece), :], own_rows(i)
            found.append(remote(src, dst, a_send.at[s, k], a_recv.at[s, k], to))
        return found

    def slices_arrive(i):
        s = SLICED.index(i)
        for k, (to, member) in enumerate(group):
            if i == SMALL:
                dst = small_block(member)
            else:
                start = q * T * piece + member * piece
                dst = weights[i].at[pl.ds(pl.multiple_of(start, 16), piece), :]
            remote(dst, dst, a_send.at[s, k], a_recv.at[s, k], to).wait_recv()

    def gather_copies(ref, use, batch):
        mine = block(ref, batch, t)
        side = block(ref, batch, c * N + 1 - n)
        return (
            remote(mine, mine, gather_send.at[use, batch, 0], gather_recv.at[use, batch, 0], over_side),
            remote(mine, mine, gather_send.at[use, batch, 1], gather_recv.at[use, batch, 1], over_core),
            remote(side, side, gather_send.at[use, batch, 2], gather_recv.at[use, batch, 2], over_core),
        )

    def gather_start(ref, use, batch):
        to_side, to_core, _ = gather_copies(ref, use, batch)
        to_side.start()
        to_core.start()

    def gather_relay(ref, use, batch):
        to_side, _, relay = gather_copies(ref, use, batch)
        to_side.wait_recv()
        relay.start()

    def gather_finish(ref, use, batch):
        to_side, to_core, relay = gather_copies(ref, use, batch)
        to_core.wait_recv()
        relay.wait_recv()
        for copy in (to_side, to_core, relay):
            copy.wait_send()

    def z_copy(i, j, line, upward):
        if upward:
            src_z, to, send, recv = z - (j - 1), device(z + 1, line_x(0), c, n), up_send, up_recv
        else:
            src_z, to, send, recv = z + (j - 1), device(z - 1, line_x(0), c, n), dn_send, dn_recv
        part = chunk(weights, i, src_z, line_x(line))
        return remote(part, part, send.at[i, j - 1, line], recv.at[i, j - 1, line], to)

    def z_arrival(i, j, line, upward):
        src_z = z - j if upward else z + j
        part = chunk(weights, i, src_z, line_x(line))
        send, recv = (up_send, up_recv) if upward else (dn_send, dn_recv)
        return remote(part, part, send.at[i, j - 1, line], recv.at[i, j - 1, line], over_x)

    def line_x(line):
        return x if line == 0 else 1 - x

    def z_launch(i, line):
        @pl.when(z < Z - 1)
        def _():
            z_copy(i, 1, line, True).start()

        @pl.when(z > 0)
        def _():
            z_copy(i, 1, line, False).start()

    def x_copy(i, z_, arrival=False):
        part = chunk(weights, i, z_, 1 - x if arrival else x)
        return remote(part, part, x_send.at[i, z_], x_recv.at[i, z_], over_x)

    def z_pass(i, j, line, to_x):
        @pl.when(z - j >= 0)
        def _():
            z_arrival(i, j, line, True).wait_recv()
            if j < Z - 1:
                @pl.when(z < Z - 1)
                def _():
                    z_copy(i, j + 1, line, True).start()
            if to_x:
                x_copy(i, z - j).start()

        @pl.when(z + j <= Z - 1)
        def _():
            z_arrival(i, j, line, False).wait_recv()
            if j < Z - 1:
                @pl.when(z > 0)
                def _():
                    z_copy(i, j + 1, line, False).start()
            if to_x:
                x_copy(i, z + j).start()

    def z_settle(i, line):
        for j in range(1, Z):
            @pl.when((z < Z - 1) & (z - (j - 1) >= 0))
            def _():
                z_copy(i, j, line, True).wait_send()

            @pl.when((z > 0) & (z + (j - 1) <= Z - 1))
            def _():
                z_copy(i, j, line, False).wait_send()

    def x_arrive(i):
        for z_ in range(Z):
            x_copy(i, z_, True).wait_recv()

    def x_settle(i):
        for z_ in range(Z):
            x_copy(i, z_).wait_send()

    def part_copies(use, batch):
        lane = LANES[use]
        return (
            remote(
                core_send.at[batch], core_recv.at[lane, batch],
                part_send.at[use, batch, 0], part_recv.at[use, batch, 0], over_core,
            ),
            remote(
                side_send.at[batch], side_recv.at[lane, batch],
                part_send.at[use, batch, 1], part_recv.at[use, batch, 1], over_side,
            ),
        )

    def parts_send(use, batch):
        lane = LANES[use]
        to_core, to_side = part_copies(use, batch)
        to_core.wait_recv()
        rows = pl.ds(pl.multiple_of((1 - n) * L, 16), L)
        side_send[batch] = (
            keep[batch, rows, :] + core_recv[lane, batch, rows, :].astype(F32)
        ).astype(BF16)
        to_side.start()

    def parts_begin(use, product, prepare=lambda batch: None):
        for batch in range(2):
            def put_away(cols, value, batch=batch):
                core_send[batch, :, cols] = value.astype(BF16)

            def put_keep(cols, value, batch=batch):
                keep[batch, :, cols] = value

            prepare(batch)
            product(batch, (1 - c) * HALF, put_away)
            part_copies(use, batch)[0].start()
            if batch == 1:
                parts_send(use, 0)
            product(batch, c * HALF, put_keep)

    def parts_middle(use):
        parts_send(use, 1)

    def parts_end(use, batch):
        lane = LANES[use]
        to_core, to_side = part_copies(use, batch)
        to_side.wait_recv()
        rows = pl.ds(pl.multiple_of(n * L, 16), L)
        total = (
            keep[batch, rows, :]
            + core_recv[lane, batch, rows, :].astype(F32)
            + side_recv[lane, batch].astype(F32)
        )
        to_core.wait_send()
        to_side.wait_send()
        return total

    def rx_copy(i, z_):
        return remote(chunk(grads, i, z_, 1 - x), rx[i].at[z_], rx_send.at[i, z_], rx_recv.at[i, z_], over_x)

    at_end = (z == 0) | (z == Z - 1)
    def steps(i):
        if i == DOWN:
            return (
                jnp.where(z < 2, 1 - z, jnp.where(z == 2, 1, 0)),
                jnp.where(z < 2, 2, jnp.where(z == 2, 0, 1)),
                jnp.where(z == 3, 2, 3),
            )
        return (
            jnp.where(z == 0, 3, jnp.where(z == 1, 2, jnp.where(z == 2, 3, 0))),
            jnp.where(z == 0, 2, jnp.where(z == 1, 0, 1)),
            jnp.where(z == 0, 1, jnp.where(z == 1, 3, jnp.where(z == 2, 0, 2))),
        )

    def rz_copy(i, k):
        to_z = lax.rem(z + k, Z)
        return remote(
            chunk(grads, i, to_z, x), rz[i].at[k - 1], rz_send.at[i, k - 1], rz_recv.at[i, k - 1],
            device(to_z, x, c, n),
        )

    def via_copy(i):
        src_z, to_z = jnp.where(z == 0, 3, 0), jnp.where(z == 0, 1, 2)
        return remote(chunk(grads, i, src_z, x), via[i], via_send.at[i], via_recv.at[i], device(to_z, x, c, n))

    def reduce_start(i, places=None):
        for z_ in (*steps(i), z) if places is None else places:
            rx_copy(i, z_).start()

    def reduce_pass(i, step):
        z_ = steps(i)[step - 1]
        k = lax.rem(z_ - z + Z, Z)
        rx_copy(i, z_).wait_recv()
        part = chunk(grads, i, z_, x)
        opposite = at_end & (z + z_ == Z - 1)
        helps = jnp.logical_not(at_end) & ((z_ - z == 2) | (z - z_ == 2))

        @pl.when(helps)
        def _():
            via_copy(i).wait_recv()
            total = part[...].astype(F32) + rx[i][z_].astype(F32) + via[i][...].astype(F32)
            part[...] = total.astype(part.dtype)

        @pl.when(jnp.logical_not(helps))
        def _():
            part[...] = (part[...].astype(F32) + rx[i][z_].astype(F32)).astype(part.dtype)

        @pl.when(opposite)
        def _():
            via_copy(i).start()

        @pl.when(jnp.logical_not(opposite))
        def _():
            rz_copy(i, k).start()

    def reduce_end(i):
        rx_copy(i, z).wait_recv()

        def total(arrivals):
            value = chunk(grads, i, z, x)[...].astype(F32) + rx[i][z].astype(F32)
            for k in arrivals:
                rz_copy(i, k).wait_recv()
                value = value + rz[i][k - 1].astype(F32)
            fin[i][...] = value.astype(fin[i].dtype)

        @pl.when(z == 0)
        def _():
            total((2, 3))

        @pl.when(z == Z - 1)
        def _():
            total((1, 2))

        @pl.when(jnp.logical_not(at_end))
        def _():
            total((1, 2, 3))
            rz_copy(i, 1).wait_send()
            rz_copy(i, 3).wait_send()

        @pl.when(at_end)
        def _():
            via_copy(i).wait_send()
            rz_copy(i, jnp.where(z == 0, 1, 3)).wait_send()

        rz_copy(i, 2).wait_send()
        for z_ in range(Z):
            rx_copy(i, z_).wait_send()

    wholes = {
        IN: (home_in, done_in, in_grad, 3), GATE: (home_gate, done_gate, gate_grad, 1),
        UP: (home_up, done_up, up_grad, 1),
    }

    def back_copies(i):
        s = SLICED.index(i)
        found = []
        for k, (to, member) in enumerate(group):
            src = fin[i] if i == SMALL else fin[i].at[pl.ds(pl.multiple_of(member * piece, 16), piece), :]
            found.append(remote(src, home[i].at[t], back_send.at[s, k], back_recv.at[s, k], to))
        return found

    def back_start(i):
        for copy in back_copies(i):
            copy.start()
        if i == SMALL:
            home_small[t] = fin_small[...]
        else:
            home[i][t] = fin[i][pl.ds(pl.multiple_of(t * piece, 16), piece), :]

    def back_arrive(i):
        s = SLICED.index(i)
        for k, (to, member) in enumerate(group):
            dst = home[i].at[member]
            remote(dst, dst, back_send.at[s, k], back_recv.at[s, k], to).wait_recv()
        for copy in back_copies(i):
            copy.wait_send()

    stores = []

    def store(src, dst):
        copy = pltpu.make_async_copy(src, dst, store_sem.at[len(stores)])
        copy.start()
        stores.append(copy)

    def merge(i):
        for half in i if i in (GATE, UP) else (i,):
            back_arrive(half)
        source, target, result, parts = wholes[i]
        cols = source.shape[2] // parts
        run = cols // Q
        for part in range(parts):
            runs = [
                source[member, :, part * cols + k * run : part * cols + (k + 1) * run].astype(F32)
                for k in range(Q)
                for member in range(T)
            ]
            target[:, part * cols * T : (part + 1) * cols * T] = jnp.concatenate(runs, axis=1)
        store(target, result)

    def merge_small():
        back_arrive(SMALL)
        gains = home_small[0] + home_small[1] + home_small[2] + home_small[3]
        mine = gains
        for member in range(1, T):
            moved = jnp.concatenate([gains[:, member * width :], gains[:, : member * width]], axis=1)
            mine = jnp.where(t == member, moved, mine)
        done_small[...] = mine
        done_small[2:5, :] = home_small[t, 2:5, :]
        store(done_small, small_grad)

    loads["small"].wait()
    for copy in slices(SMALL):
        copy.start()
    loads[OUT].wait()
    z_launch(OUT, 0)
    x_copy(OUT, z).start()
    loads[DOWN].wait()
    x_copy(DOWN1, z).start()
    z_launch(DOWN1, 0)
    loads["in"].wait()
    split(raw_in, stage_in, w_in, 3)
    for copy in slices(IN):
        copy.start()
    slices_arrive(SMALL)
    z_launch(SMALL, 0)
    x_copy(SMALL, z).start()
    loads["gate"].wait()
    split(raw_gate, stage_gate, w_gate, 1)
    for i in GATE:
        for copy in slices(i):
            copy.start()
    for batch in range(2):
        loads["tokens%d" % batch].wait()
        gather_start(toks, 0, batch)
    slices_arrive(IN)
    z_launch(IN, 0)
    x_copy(IN, z).start()
    loads["up"].wait()
    split(raw_up, stage_up, w_up, 1)
    for i in UP:
        for copy in slices(i):
            copy.start()
    for i in (OUT, SMALL, IN):
        z_pass(i, 1, 0, True)
    loads["valid"].wait()
    for batch in range(2):
        loads["cot%d" % batch].wait()
        mine = pl.ds(pl.multiple_of(t * L, 16), L)
        column = jnp.transpose(jnp.broadcast_to(valid_rows[batch : batch + 1, :], (128, L)))[:, :1]
        seeds[batch, mine, :] = (seeds[batch, mine, :].astype(F32) * column).astype(BF16)
    for i in (OUT, SMALL, IN):
        z_pass(i, 2, 0, True)
    slices_arrive(GATE0)
    z_launch(GATE0, 0)
    x_copy(GATE0, z).start()
    gather_relay(toks, 0, 0)
    gather_relay(toks, 0, 1)
    for batch in range(2):
        gather_start(seeds, 1, batch)
    for i in (OUT, SMALL, IN):
        z_pass(i, 3, 0, True)
    x_arrive(SMALL)
    pieces = [
        jnp.concatenate(
            [w_small[k * 16 : (k + 1) * 16, m * 128 : m * 128 + width].astype(F32)[:8] for m in range(T)],
            axis=1,
        )
        for k in range(Q)
    ]
    params[...] = jnp.concatenate(pieces, axis=1)

    def norm_rows(ref, gain):
        block_ = ref.astype(F32)
        return (block_ * row_scale(block_) * gain).astype(BF16)

    for batch in range(2):
        gather_finish(toks, 0, batch)

        @pl.loop(0, GROUP // 64)
        def _(step, batch=batch):
            rows = pl.ds(pl.multiple_of(step * 64, 64), 64)
            normed_one[batch, rows, :] = norm_rows(toks[batch, rows, :], params[0:1, :])

    x_arrive(IN)
    for batch in range(2):
        for start, size in column_tiles(3 * CS, 256):
            projected[batch, :, start : start + size] = nn(normed_one[batch], w_in[:, start : start + size])
        gated[batch, 8 : 8 + GROUP, :] = projected[batch, :, :CS] * projected[batch, :, 2 * CS :]

    def halo_copies(batch):
        ahead = remote(
            gated.at[batch, pl.ds(GROUP, 8), :], gated.at[batch, pl.ds(0, 8), :],
            halo_send.at[0, batch], halo_recv.at[0, batch], over_next,
        )
        back = remote(
            conv.at[batch, pl.ds(0, 8), :], conv.at[batch, pl.ds(GROUP, 8), :],
            halo_send.at[1, batch], halo_recv.at[1, batch], over_prev,
        )
        return ahead, back

    for batch in range(2):
        halo_copies(batch)[0].start()
    slices_arrive(UP0)
    z_launch(UP0, 0)
    x_copy(UP0, z).start()
    z_pass(GATE0, 1, 0, True)
    my_lanes = pl.ds(pl.multiple_of(t * 128, 128), 128)
    taps = jnp.concatenate(
        [w_small[k * 16 : (k + 1) * 16, my_lanes].astype(F32)[2:5, :width] for k in range(Q)], axis=1
    )
    def mix(batch):
        halo_copies(batch)[0].wait_recv()

        @pl.when(q == 0)
        def _():
            gated[batch, 0:8, :] = jnp.zeros((8, CS), F32)

        for r in range(0, GROUP, HALF):
            value = (
                taps[0:1] * gated[batch, r + 6 : r + 6 + HALF, :]
                + taps[1:2] * gated[batch, r + 7 : r + 7 + HALF, :]
                + taps[2:3] * gated[batch, r + 8 : r + 8 + HALF, :]
            )
            branch[batch, r : r + HALF, :] = (projected[batch, r : r + HALF, CS : 2 * CS] * value).astype(BF16)

    z_pass(GATE0, 2, 0, True)
    x_arrive(OUT)

    def product_out(batch, start, put):
        rows = pl.ds(pl.multiple_of(start, 16), HALF)
        for at, size in column_tiles(D, 512):
            put(slice(at, at + size), nn(branch[batch, rows, :], w_out[:, at : at + size]))

    parts_begin(0, product_out, mix)
    z_pass(GATE0, 3, 0, True)
    z_pass(UP0, 1, 0, True)
    parts_middle(0)
    slices_arrive(GATE1)
    z_launch(GATE1, 0)
    x_copy(GATE1, z).start()
    gather_relay(seeds, 1, 0)
    gather_relay(seeds, 1, 1)
    z_pass(UP0, 2, 0, True)
    for batch in range(2):
        mine = pl.ds(pl.multiple_of(t * L, 16), L)
        hidden[batch] = toks[batch, mine, :].astype(F32) + parts_end(0, batch)
        normed_two[batch, mine, :] = norm_rows(hidden[batch], params[1:2, :])
        gather_start(normed_two, 2, batch)
    z_pass(UP0, 3, 0, True)
    slices_arrive(UP1)
    z_launch(UP1, 0)
    x_copy(UP1, z).start()
    z_pass(GATE1, 1, 0, True)
    z_launch(DOWN, 0)
    x_copy(DOWN1, z, True).wait_recv()
    z_launch(DOWN1, 1)
    gather_relay(normed_two, 2, 0)
    gather_relay(normed_two, 2, 1)
    z_pass(GATE1, 2, 0, True)
    for batch in range(2):
        gather_finish(normed_two, 2, batch)
        gather_finish(seeds, 1, batch)
    z_pass(GATE1, 3, 0, True)
    z_pass(UP1, 1, 0, True)

    x_arrive(GATE0)
    x_arrive(UP0)
    for i in SLICED:
        for copy in slices(i):
            copy.wait_send()

    def feed_forward(batch, part):
        for r in range(0, GROUP, HALF):
            for start, size in column_tiles(part.stop - part.start, 384):
                cols = slice(part.start + start, part.start + start + size)
                rows = slice(r, r + HALF)
                left = normed_two[batch, rows, :]
                gate = nn(left, w_gate[:, cols])
                up = nn(left, w_up[:, cols])
                sig = 1.0 / (1.0 + jnp.exp(-gate))
                act = gate * sig
                silu[batch, rows, cols] = act.astype(BF16)
                slope[batch, rows, cols] = (up * sig * (1.0 + gate * (1.0 - sig))).astype(BF16)
                activated[batch, rows, cols] = (act * up).astype(BF16)

    def weight_grad(dst, left, right, most_rows, most_cols):
        for a, rows in column_tiles(dst.shape[0], most_rows):
            for b, cols in column_tiles(dst.shape[1], most_cols):
                value = tn(left[0, :, a : a + rows], right[0, :, b : b + cols])
                value = value + tn(left[1, :, a : a + rows], right[1, :, b : b + cols])
                dst[a : a + rows, b : b + cols] = value.astype(BF16)

    feed_forward(0, halves[0])
    z_pass(UP1, 2, 0, True)
    feed_forward(1, halves[0])
    weight_grad(g_down.at[pl.ds(0, cut), :], activated.at[:, :, pl.ds(0, cut)], seeds, 384, 512)
    z_pass(UP1, 3, 0, True)
    x_copy(DOWN, z).start()

    def down_pass(j):
        z_pass(DOWN, j, 0, True)
        z_pass(DOWN1, j, 0, False)
        z_pass(DOWN1, j, 1, False)

    down_pass(1)
    x_arrive(GATE1)
    x_arrive(UP1)
    feed_forward(0, halves[1])
    down_pass(2)
    feed_forward(1, halves[1])
    down_pass(3)
    ready = cut // (chunk_size(DOWN) * X)
    reduce_start(DOWN, range(ready))
    weight_grad(g_down.at[pl.ds(cut, FS - cut), :], activated.at[:, :, pl.ds(cut, FS - cut)], seeds, 384, 512)
    reduce_start(DOWN, range(ready, Z))

    x_arrive(DOWN)
    def seed_batch(batch):
        for r in range(0, GROUP, HALF):
            for start, size in column_tiles(FS, 384):
                cols = slice(start, start + size)
                rows = slice(r, r + HALF)
                act_grad = nt(seeds[batch, rows, :], w_down[cols, :])
                silu[batch, rows, cols] = (act_grad * silu[batch, rows, cols].astype(F32)).astype(BF16)
                slope[batch, rows, cols] = (act_grad * slope[batch, rows, cols].astype(F32)).astype(BF16)

    up_seed, gate_seed = silu, slope

    def product_ffn(batch, start, put):
        rows = pl.ds(pl.multiple_of(start, 16), HALF)
        for at, size in column_tiles(D, 512):
            put(
                slice(at, at + size),
                nt(gate_seed[batch, rows, :], w_gate[at : at + size, :])
                + nt(up_seed[batch, rows, :], w_up[at : at + size, :]),
            )

    def product_down(batch, start, put):
        rows = pl.ds(pl.multiple_of(start, 16), HALF)
        for at, size in column_tiles(D, 512):
            put(slice(at, at + size), nn(activated[batch, rows, :], w_down[:, at : at + size]))

    parts_begin(2, product_ffn, seed_batch)
    parts_middle(2)
    reduce_pass(DOWN, 1)
    for i in (IN, OUT, *GATE, *UP, DOWN, SMALL, DOWN1):
        z_settle(i, 0)
        if i == DOWN1:
            z_settle(i, 1)
            x_copy(i, z).wait_send()
        else:
            x_settle(i)
    for i, part in zip(GATE, halves):
        weight_grad(grads[i], normed_two, gate_seed.at[:, :, pl.ds(part.start, part.stop - part.start)], 256, 384)
        reduce_start(i)
    reduce_pass(DOWN, 2)
    weight_grad(w_up, normed_two, up_seed, 256, 384)
    pass
    reduce_pass(DOWN, 3)
    gain_two = jnp.zeros((1, D), F32)
    for batch in range(2):
        mine = pl.ds(pl.multiple_of(t * L, 16), L)
        n2g = parts_end(2, batch)
        hid = hidden[batch]
        scale = row_scale(hid)
        gain_two = gain_two + jnp.sum(n2g * hid * scale, axis=0, keepdims=True)
        scaled = n2g * params[1:2, :]
        value = (
            seeds[batch, mine, :].astype(F32)
            + scale * scaled
            - hid * (scale * scale * scale) * jnp.mean(scaled * hid, axis=-1, keepdims=True)
        )
        hidden_grad[batch] = value
        out_seed[batch, mine, :] = value.astype(BF16)
        gather_start(out_seed, 3, batch)
    parts_begin(1, product_down)
    gather_relay(out_seed, 3, 0)
    gather_relay(out_seed, 3, 1)
    parts_middle(1)
    reduce_pass(GATE0, 1)
    for batch in range(2):
        gather_finish(out_seed, 3, batch)
        for r in range(0, GROUP, HALF):
            rows = slice(r, r + HALF)
            branch_grad = nt(out_seed[batch, rows, :], w_out[...])
            conv_grad = branch_grad * projected[batch, rows, CS : 2 * CS]
            conv[batch, rows, :] = conv_grad
            mixed = (
                taps[0:1] * gated[batch, r + 6 : r + 6 + HALF, :]
                + taps[1:2] * gated[batch, r + 7 : r + 7 + HALF, :]
                + taps[2:3] * gated[batch, r + 8 : r + 8 + HALF, :]
            )
            proj_seed[batch, rows, CS : 2 * CS] = (branch_grad * mixed).astype(BF16)
        halo_copies(batch)[1].start()
    reduce_start(UP0)
    reduce_start(UP1)
    kernel_grad = [jnp.zeros((1, CS), F32) for _ in range(3)]
    for batch in range(2):
        for r in range(0, GROUP, HALF):
            conv_grad = conv[batch, r : r + HALF, :]
            for k in range(3):
                kernel_grad[k] = kernel_grad[k] + jnp.sum(
                    conv_grad * gated[batch, r + 6 + k : r + 6 + k + HALF, :], axis=0, keepdims=True
                )
    weight_grad(w_out, branch, out_seed, 256, 512)
    reduce_pass(GATE0, 2)
    reduce_pass(GATE0, 3)
    def unmix(batch):
        halo_copies(batch)[1].wait_recv()

        @pl.when(q == Q - 1)
        def _():
            conv[batch, GROUP : GROUP + 8, :] = jnp.zeros((8, CS), F32)

        for r in range(0, GROUP, HALF):
            rows = slice(r, r + HALF)
            value = (
                taps[2:3] * conv[batch, r : r + HALF, :]
                + taps[1:2] * conv[batch, r + 1 : r + 1 + HALF, :]
                + taps[0:1] * conv[batch, r + 2 : r + 2 + HALF, :]
            )
            proj_seed[batch, rows, :CS] = (value * projected[batch, rows, 2 * CS :]).astype(BF16)
            proj_seed[batch, rows, 2 * CS :] = (value * projected[batch, rows, :CS]).astype(BF16)

    def product_in(batch, start, put):
        rows = pl.ds(pl.multiple_of(start, 16), HALF)
        for at, size in column_tiles(D, 512):
            put(slice(at, at + size), nt(proj_seed[batch, rows, :], w_in[at : at + size, :]))

    for batch in range(2):
        mine = pl.ds(pl.multiple_of(t * L, 16), L)
        seeds[batch, mine, :] = (hidden[batch] + parts_end(1, batch)).astype(BF16)
    out_copies = [
        pltpu.make_async_copy(block(seeds, batch, t), block_out.at[batch], local_sem.at[2 + batch])
        for batch in range(2)
    ]
    for copy in out_copies:
        copy.start()
    parts_begin(3, product_in, unmix)
    parts_middle(3)
    reduce_pass(GATE1, 1)
    reduce_pass(GATE1, 2)
    reduce_pass(GATE1, 3)
    weight_grad(w_in, normed_one, proj_seed, 256, 384)
    reduce_start(IN)
    reduce_start(OUT)
    reduce_pass(UP0, 1)
    reduce_pass(UP0, 2)
    reduce_pass(UP0, 3)
    reduce_end(DOWN)
    store(fin_down, down_grad)
    gain_one = jnp.zeros((1, D), F32)
    for batch in range(2):
        mine = pl.ds(pl.multiple_of(t * L, 16), L)
        n1g = parts_end(3, batch)
        inputs = toks[batch, mine, :].astype(F32)
        scale = row_scale(inputs)
        gain_one = gain_one + jnp.sum(n1g * inputs * scale, axis=0, keepdims=True)
        scaled = n1g * params[0:1, :]
        hidden_grad[batch] = (
            hidden_grad[batch]
            + scale * scaled
            - inputs * (scale * scale * scale) * jnp.mean(scaled * inputs, axis=-1, keepdims=True)
        )
    grad_copy = pltpu.make_async_copy(hidden_grad, input_grad, local_sem.at[1])
    grad_copy.start()
    for k in range(Q):
        lanes = slice(k * 128, (k + 1) * 128)
        runs = [jnp.pad(g[:, k * width : (k + 1) * width], ((0, 0), (0, 128 - width))) for g in kernel_grad]
        rows = [gain_one[:, lanes], gain_two[:, lanes], *runs, jnp.zeros((3, 128), F32)]
        g_small[k * 8 : (k + 1) * 8, :] = jnp.concatenate(rows, axis=0)
    reduce_start(SMALL)
    reduce_end(GATE0)
    back_start(GATE0)
    reduce_end(GATE1)
    back_start(GATE1)
    for step in (1, 2, 3):
        reduce_pass(UP1, step)
    merge(GATE)
    for step in (1, 2, 3):
        reduce_pass(IN, step)
    reduce_end(UP0)
    back_start(UP0)
    reduce_end(UP1)
    back_start(UP1)
    for i in (OUT, SMALL):
        for step in (1, 2, 3):
            reduce_pass(i, step)
    reduce_end(IN)
    back_start(IN)
    reduce_end(OUT)
    store(fin_out, out_grad)
    reduce_end(SMALL)
    back_start(SMALL)
    merge(UP)
    for batch in range(2):
        for copy in halo_copies(batch):
            copy.wait_send()
    merge(IN)
    merge_small()
    for copy in stores:
        copy.wait()
    for copy in out_copies:
        copy.wait()
    grad_copy.wait()


def hand_over(*refs):
    count = (len(refs) - 2) // 3
    sources, targets, held = refs[:count], refs[count : 2 * count], refs[2 * count : 3 * count]
    load_sem, store_sem = refs[3 * count :]
    loads = [pltpu.make_async_copy(sources[k], held[k], load_sem.at[k]) for k in range(count)]
    stores = [pltpu.make_async_copy(held[k], targets[k], store_sem.at[k]) for k in range(count)]
    for load in loads:
        load.start()
    for load, store in zip(loads, stores):
        load.wait()
        store.start()
    for store in stores:
        store.wait()


def fused(plan, tokens, cotangent, lengths, loss_mask, norm_gain, in_weight, conv_kernel, out_weight, ffn_gain, gate_weight, up_weight, down_weight):
    Z, Q, T = plan["Z"], plan["Q"], 4
    L, D, FS, CS = plan["L"], plan["D"], plan["FS"], plan["CS"]
    width, hid, rows = out_weight.shape[0], down_weight.shape[0], in_weight.shape[0]
    place = lax.axis_index(("wide", "narrow"))
    positions = place * L + jnp.arange(L, dtype=jnp.int32)
    valid = ((positions[None, :] < lengths[:, None]) & (loss_mask != 0)).astype(F32)
    valid = jnp.pad(valid, ((0, 6), (0, 0)))
    small = jnp.concatenate([norm_gain[None], ffn_gain[None], conv_kernel], axis=0)
    small = jnp.pad(small, ((0, 11), (0, 128 - width)))

    shapes = [(T * rows, 3 * CS), (width, D), (T * rows, FS), (T * rows, FS), (hid, D)]
    vm, dma = pltpu.VMEM, pltpu.SemaphoreType.DMA
    group = T * L
    scratch = [vm((Q * r, k), BF16) for r, k in shapes]
    scratch += [vm((Q * 16, T * 128), BF16), vm((Q * hid, D), BF16), vm((Q * 8, 128), F32)]
    scratch += [vm((Z, r, k), BF16) for r, k in shapes] + [vm((Z, 8, 128), F32)]
    scratch += [vm((Z - 1, r, k), BF16) for r, k in shapes] + [vm((Z - 1, 8, 128), F32)]
    scratch += [vm((r, k), BF16) for r, k in shapes] + [vm((8, 128), F32)]
    scratch += [vm((r, k), F32 if r in (width, hid) else BF16) for r, k in shapes]
    scratch += [vm((8, 128), F32)]
    scratch += [vm((T, rows, 3 * CS), BF16), vm((T, rows, FS), BF16), vm((T, rows, FS), BF16), vm((T, 8, 128), F32)]
    scratch += [vm(a.shape, F32) for a in (in_weight, gate_weight, up_weight)] + [vm((8, 128), F32)]
    scratch += [vm(a.shape, BF16) for a in (in_weight, gate_weight, up_weight)] + [vm((8, L), F32), vm((8, D), F32)]
    scratch += [vm((2, group, D), BF16) for _ in range(5)]
    scratch += [vm((2, L, D), F32), vm((2, L, D), F32)]
    scratch += [
        vm((2, group, 3 * CS), F32), vm((2, group + 8, CS), F32), vm((2, group + 8, CS), F32),
        vm((2, group, CS), BF16), vm((2, group, 3 * CS), BF16),
    ]
    scratch += [vm((2, group, FS), BF16) for _ in range(3)]
    scratch += [
        vm((2, 2 * L, D), BF16), vm((2, 2, 2 * L, D), BF16),
        vm((2, L, D), BF16), vm((2, 2, L, D), BF16), vm((2, 2 * L, D), F32),
    ]
    scratch += [
        dma((11,)), dma((6, 3)), dma((6, 3)),
        dma((9, Z - 1, 2)), dma((9, Z - 1, 2)), dma((9, Z - 1, 2)), dma((9, Z - 1, 2)),
        dma((9, Z)), dma((9, Z)),
        dma((4, 2, 3)), dma((4, 2, 3)), dma((4, 2, 2)), dma((4, 2, 2)), dma((2, 2)), dma((2, 2)),
        dma((8, Z)), dma((8, Z)), dma((8, Z - 1)), dma((8, Z - 1)), dma((8,)), dma((8,)), dma((6, 3)), dma((6, 3)), dma((6,)),
    ]
    out_shape = (
        jax.ShapeDtypeStruct((2, L, D), BF16),
        jax.ShapeDtypeStruct((2, L, D), F32),
        jax.ShapeDtypeStruct(in_weight.shape, F32),
        jax.ShapeDtypeStruct(out_weight.shape, F32),
        jax.ShapeDtypeStruct(gate_weight.shape, F32),
        jax.ShapeDtypeStruct(up_weight.shape, F32),
        jax.ShapeDtypeStruct(down_weight.shape, F32),
        jax.ShapeDtypeStruct((8, 128), F32),
    )
    block_out, input_grad, in_g, out_g, gate_g, up_g, down_g, small_g = pl.pallas_call(
        functools.partial(block_kernel, plan),
        out_shape=out_shape,
        in_specs=[pl.BlockSpec(memory_space=pl.ANY)] * 9,
        out_specs=[pl.BlockSpec(memory_space=pl.ANY)] * 8,
        scratch_shapes=scratch,
        compiler_params=pltpu.CompilerParams(
            collective_id=0, has_side_effects=True, vmem_limit_bytes=VMEM_LIMIT
        ),
    )(tokens, cotangent, valid, small, in_weight, out_weight, gate_weight, up_weight, down_weight)
    arrays = (block_out, input_grad, in_g, out_g, gate_g, up_g, down_g)
    block_out, input_grad, in_g, out_g, gate_g, up_g, down_g = pl.pallas_call(
        hand_over,
        out_shape=tuple(jax.ShapeDtypeStruct(a.shape, a.dtype) for a in arrays),
        in_specs=[pl.BlockSpec(memory_space=pltpu.HBM)] * len(arrays),
        out_specs=[pl.BlockSpec(memory_space=pltpu.HBM)] * len(arrays),
        scratch_shapes=[vm(a.shape, a.dtype) for a in arrays] + [dma((len(arrays),)), dma((len(arrays),))],
        compiler_params=pltpu.CompilerParams(vmem_limit_bytes=VMEM_LIMIT),
    )(*arrays)
    return (
        block_out, input_grad, small_g[0, :width], in_g, small_g[2:5, :width], out_g, small_g[1, :width],
        gate_g, up_g, down_g,
    )


def planned(wide, narrow, arrays):
    tokens, in_weight, down_weight = arrays[0], arrays[5], arrays[11]
    if narrow != 2 or wide != 16 or tokens.shape[0] != 2:
        return None
    groups = wide // 2
    rows, hid = in_weight.shape[0], down_weight.shape[0]
    sizes = {
        "Z": groups // 2, "Q": groups, "L": tokens.shape[1], "D": tokens.shape[2],
        "FS": hid * groups, "CS": rows * groups,
    }
    if rows % 16 or hid % 16 or sizes["L"] != 128 or sizes["FS"] % 128 or sizes["CS"] % 128 or rows != 32:
        return None
    return sizes


def solution(mesh):
    in_specs = (
        P(None, ("wide", "narrow"), None),
        P(None, ("wide", "narrow"), None),
        P(),
        P(None, ("wide", "narrow")),
        P(("wide", "narrow")),
        P(("wide", "narrow"), None),
        P(None, ("wide", "narrow")),
        P(("wide", "narrow"), None),
        P(("wide", "narrow")),
        P(("wide", "narrow"), None),
        P(("wide", "narrow"), None),
        P(("wide", "narrow"), None),
    )
    out_specs = (
        P(None, ("wide", "narrow"), None),
        P(None, ("wide", "narrow"), None),
        P(("wide", "narrow")),
        P(("wide", "narrow"), None),
        P(None, ("wide", "narrow")),
        P(("wide", "narrow"), None),
        P(("wide", "narrow")),
        P(("wide", "narrow"), None),
        P(("wide", "narrow"), None),
        P(("wide", "narrow"), None),
    )
    wide, narrow = mesh.shape["wide"], mesh.shape["narrow"]

    def step(*arrays):
        plan = planned(wide, narrow, arrays)
        run = body if plan is None else functools.partial(fused, plan)
        return run(*arrays)

    return jax.shard_map(step, mesh=mesh, in_specs=in_specs, out_specs=out_specs, check_vma=False)
```

```python
import functools

import jax
import jax.numpy as jnp
from jax import lax
from jax.experimental import pallas as pl
from jax.experimental.pallas import tpu as pltpu
from jax.sharding import PartitionSpec as P

EPSILON = 1e-05


def shifted(block, axis, distance):
    devices = range(lax.axis_size(axis))
    route = [(i - distance, i) for i in devices if i - distance in devices]
    return lax.ppermute(block, axis, route)


def along_rows(left, weight):
    return lax.dot_general(
        left, weight, (((1,), (1,)), ((), ())), preferred_element_type=jnp.float32
    )


def over_rows(left, right):
    return lax.dot_general(
        left, right, (((0,), (0,)), ((), ())), preferred_element_type=jnp.float32
    )


def collect(shards):
    partial_set = (
        lax.all_gather(shards[0], "narrow", axis=0, tiled=True),
        lax.all_gather(shards[1], "narrow", axis=0, tiled=True),
        lax.all_gather(shards[2], "narrow", axis=1, tiled=True),
        lax.all_gather(shards[3], "narrow", axis=0, tiled=True),
        lax.all_gather(shards[4], "narrow", axis=0, tiled=True),
        lax.all_gather(shards[5], "narrow", axis=0, tiled=True),
        lax.all_gather(shards[6], "narrow", axis=0, tiled=True),
        lax.all_gather(shards[7], "narrow", axis=0, tiled=True),
    )
    return (
        lax.all_gather(partial_set[0], "wide", axis=0, tiled=True),
        lax.all_gather(partial_set[1], "wide", axis=0, tiled=True),
        lax.all_gather(partial_set[2], "wide", axis=1, tiled=True),
        lax.all_gather(partial_set[3], "wide", axis=0, tiled=True),
        lax.all_gather(partial_set[4], "wide", axis=0, tiled=True),
        lax.all_gather(partial_set[5], "wide", axis=0, tiled=True),
        lax.all_gather(partial_set[6], "wide", axis=0, tiled=True),
        lax.all_gather(partial_set[7], "wide", axis=0, tiled=True),
    )


def collect_tied(shards, anchor):
    tied_shards, _ = lax.optimization_barrier((shards, anchor))
    return collect(tied_shards)


def body(
    tokens,
    cotangent,
    lengths,
    loss_mask,
    norm_gain,
    in_weight,
    conv_kernel,
    out_weight,
    ffn_gain,
    gate_weight,
    up_weight,
    down_weight,
):
    micro_count = tokens.shape[0]
    local_rows = tokens.shape[1]
    width = tokens.shape[2]
    shards = (
        norm_gain,
        in_weight,
        conv_kernel,
        out_weight,
        ffn_gain,
        gate_weight,
        up_weight,
        down_weight,
    )
    positions = lax.axis_index(("wide", "narrow")) * local_rows + jnp.arange(
        local_rows, dtype=jnp.int32
    )
    gain_one_grad = jnp.zeros((width,), jnp.float32)
    gain_two_grad = jnp.zeros((width,), jnp.float32)
    kernel_grad = jnp.zeros((3, width), jnp.float32)
    outputs = []
    input_grads = []
    kept_normed_one = []
    kept_proj_seed = []
    kept_branch = []
    kept_out_seed = []
    kept_normed_two = []
    kept_gate_seed = []
    kept_up_seed = []
    kept_activated = []
    kept_down_seed = []
    for batch in range(micro_count):
        gathered = collect_tied(shards, tokens[batch])
        gain_full, in_full, kernel_full, out_full, ffn_full, gate_full, up_full, down_full = (
            gathered
        )
        gain_f32 = gain_full.astype(jnp.float32)
        ffn_f32 = ffn_full.astype(jnp.float32)
        kernel_f32 = kernel_full.astype(jnp.float32)
        inputs = tokens[batch].astype(jnp.float32)
        scale_one = lax.rsqrt(jnp.mean(inputs * inputs, axis=-1, keepdims=True) + EPSILON)
        normed_one = (inputs * scale_one * gain_f32).astype(jnp.bfloat16)
        projected = jnp.dot(normed_one, in_full, preferred_element_type=jnp.float32)
        b_gate = projected[:, :width]
        c_gate = projected[:, width : 2 * width]
        conv_input = projected[:, 2 * width :]
        gated_input = b_gate * conv_input
        earlier = shifted(gated_input[local_rows - 2 :], ("wide", "narrow"), 1)
        padded = jnp.concatenate([earlier, gated_input], axis=0)
        mixed_conv = (
            kernel_f32[0] * padded[:-2] + kernel_f32[1] * padded[1:-1] + kernel_f32[2] * gated_input
        )
        branch = (c_gate * mixed_conv).astype(jnp.bfloat16)
        hidden = inputs + jnp.dot(branch, out_full, preferred_element_type=jnp.float32)
        scale_two = lax.rsqrt(jnp.mean(hidden * hidden, axis=-1, keepdims=True) + EPSILON)
        normed_two = (hidden * scale_two * ffn_f32).astype(jnp.bfloat16)
        gate_out = jnp.dot(normed_two, gate_full, preferred_element_type=jnp.float32)
        up_out = jnp.dot(normed_two, up_full, preferred_element_type=jnp.float32)
        sigmoid_gate = jax.nn.sigmoid(gate_out)
        silu_gate = gate_out * sigmoid_gate
        activated = (silu_gate * up_out).astype(jnp.bfloat16)
        result = hidden + jnp.dot(activated, down_full, preferred_element_type=jnp.float32)
        outputs.append(result.astype(jnp.bfloat16))
        validity = (positions < lengths[batch]).astype(jnp.float32) * loss_mask[batch].astype(
            jnp.float32
        )
        seed = cotangent[batch].astype(jnp.float32) * validity[:, None]
        down_seed = seed.astype(jnp.bfloat16)
        act_grad = along_rows(down_seed, down_full)
        up_seed = (act_grad * silu_gate).astype(jnp.bfloat16)
        gate_seed = (
            act_grad * up_out * sigmoid_gate * (1.0 + gate_out * (1.0 - sigmoid_gate))
        ).astype(jnp.bfloat16)
        normed_two_grad = along_rows(gate_seed, gate_full) + along_rows(up_seed, up_full)
        gain_two_grad = gain_two_grad + jnp.sum(normed_two_grad * hidden * scale_two, axis=0)
        scaled_two = normed_two_grad * ffn_f32
        hidden_grad = (
            seed
            + scale_two * scaled_two
            - hidden
            * (scale_two * scale_two * scale_two)
            * jnp.mean(scaled_two * hidden, axis=-1, keepdims=True)
        )
        out_seed = hidden_grad.astype(jnp.bfloat16)
        branch_grad = along_rows(out_seed, out_full)
        c_grad = branch_grad * mixed_conv
        conv_grad = branch_grad * c_gate
        kernel_grad = kernel_grad + jnp.stack(
            [
                jnp.sum(conv_grad * padded[:-2], axis=0),
                jnp.sum(conv_grad * padded[1:-1], axis=0),
                jnp.sum(conv_grad * gated_input, axis=0),
            ],
            axis=0,
        )
        later = shifted(conv_grad[:2], ("wide", "narrow"), -1)
        extended = jnp.concatenate([conv_grad, later], axis=0)
        gated_grad = (
            kernel_f32[2] * conv_grad
            + kernel_f32[1] * extended[1 : local_rows + 1]
            + kernel_f32[0] * extended[2:]
        )
        proj_seed = jnp.concatenate(
            [gated_grad * conv_input, c_grad, gated_grad * b_gate], axis=1
        ).astype(jnp.bfloat16)
        normed_one_grad = along_rows(proj_seed, in_full)
        gain_one_grad = gain_one_grad + jnp.sum(normed_one_grad * inputs * scale_one, axis=0)
        scaled_one = normed_one_grad * gain_f32
        input_grads.append(
            hidden_grad
            + scale_one * scaled_one
            - inputs
            * (scale_one * scale_one * scale_one)
            * jnp.mean(scaled_one * inputs, axis=-1, keepdims=True)
        )
        kept_normed_one.append(normed_one)
        kept_proj_seed.append(proj_seed)
        kept_branch.append(branch)
        kept_out_seed.append(out_seed)
        kept_normed_two.append(normed_two)
        kept_gate_seed.append(gate_seed)
        kept_up_seed.append(up_seed)
        kept_activated.append(activated)
        kept_down_seed.append(down_seed)
    all_normed_two = jnp.concatenate(kept_normed_two, axis=0)
    in_grad = over_rows(
        jnp.concatenate(kept_normed_one, axis=0), jnp.concatenate(kept_proj_seed, axis=0)
    )
    out_grad = over_rows(
        jnp.concatenate(kept_branch, axis=0), jnp.concatenate(kept_out_seed, axis=0)
    )
    gate_grad = over_rows(all_normed_two, jnp.concatenate(kept_gate_seed, axis=0))
    up_grad = over_rows(all_normed_two, jnp.concatenate(kept_up_seed, axis=0))
    down_grad = over_rows(
        jnp.concatenate(kept_activated, axis=0), jnp.concatenate(kept_down_seed, axis=0)
    )
    gain_one_part, in_part, kernel_part, out_part, gain_two_part, gate_part, up_part, down_part = (
        lax.psum_scatter(gain_one_grad, "wide", scatter_dimension=0, tiled=True),
        lax.psum_scatter(in_grad, "wide", scatter_dimension=0, tiled=True),
        lax.psum_scatter(kernel_grad, "wide", scatter_dimension=1, tiled=True),
        lax.psum_scatter(out_grad, "wide", scatter_dimension=0, tiled=True),
        lax.psum_scatter(gain_two_grad, "wide", scatter_dimension=0, tiled=True),
        lax.psum_scatter(gate_grad, "wide", scatter_dimension=0, tiled=True),
        lax.psum_scatter(up_grad, "wide", scatter_dimension=0, tiled=True),
        lax.psum_scatter(down_grad, "wide", scatter_dimension=0, tiled=True),
    )
    gain_one_sum, in_sum, kernel_sum, out_sum, gain_two_sum, gate_sum, up_sum, down_sum = (
        lax.psum_scatter(gain_one_part, "narrow", scatter_dimension=0, tiled=True),
        lax.psum_scatter(in_part, "narrow", scatter_dimension=0, tiled=True),
        lax.psum_scatter(kernel_part, "narrow", scatter_dimension=1, tiled=True),
        lax.psum_scatter(out_part, "narrow", scatter_dimension=0, tiled=True),
        lax.psum_scatter(gain_two_part, "narrow", scatter_dimension=0, tiled=True),
        lax.psum_scatter(gate_part, "narrow", scatter_dimension=0, tiled=True),
        lax.psum_scatter(up_part, "narrow", scatter_dimension=0, tiled=True),
        lax.psum_scatter(down_part, "narrow", scatter_dimension=0, tiled=True),
    )
    block_out = jnp.stack(outputs, axis=0)
    input_grad = jnp.stack(input_grads, axis=0)
    return (
        block_out,
        input_grad,
        gain_one_sum,
        in_sum,
        kernel_sum,
        out_sum,
        gain_two_sum,
        gate_sum,
        up_sum,
        down_sum,
    )


MESH = pl.DeviceIdType.MESH
BF16, F32 = jnp.bfloat16, jnp.float32
VMEM_LIMIT = 62 * 1024 * 1024


def nn(a, b):
    return lax.dot_general(a, b, (((1,), (0,)), ((), ())), preferred_element_type=F32)


def nt(a, b):
    return lax.dot_general(a, b, (((1,), (1,)), ((), ())), preferred_element_type=F32)


def tn(a, b):
    return lax.dot_general(a, b, (((0,), (0,)), ((), ())), preferred_element_type=F32)


def column_tiles(total, most):
    units = total // 128
    count = -(-units // (most // 128))
    edges = [-(-units * k // count) * 128 for k in range(count + 1)]
    return [(a, b - a) for a, b in zip(edges, edges[1:])]


def row_scale(block):
    return lax.rsqrt(jnp.mean(block * block, axis=-1, keepdims=True) + EPSILON)


IN, OUT, GATE0, GATE1, UP0, UP1, DOWN, SMALL, DOWN1 = range(9)
GATE, UP = (GATE0, GATE1), (UP0, UP1)
SLICED = (IN, GATE0, GATE1, UP0, UP1, SMALL)
LANES = (0, 0, 1, 1)


def block_kernel(
    plan,
    tokens, cotangent, valid, small, in_weight, out_own, gate_weight, up_weight, down_own,
    block_out, input_grad, in_grad, out_grad, gate_grad, up_grad, down_grad, small_grad,
    w_in, w_out, w_gate, w_up, w_down, w_small, g_down, g_small,
    rx_in, rx_out, rx_gate, rx_up, rx_down, rx_small,
    rz_in, rz_out, rz_gate, rz_up, rz_down, rz_small,
    via_in, via_out, via_gate, via_up, via_down, via_small,
    fin_in, fin_out, fin_gate, fin_up, fin_down, fin_small,
    home_in, home_gate, home_up, home_small, done_in, done_gate, done_up, done_small,
    raw_in, raw_gate, raw_up, valid_rows, params,
    toks, seeds, normed_one, normed_two, out_seed,
    hidden, hidden_grad,
    projected, gated, conv, branch, proj_seed,
    silu, slope, activated,
    core_send, core_recv, side_send, side_recv, keep,
    local_sem, a_send, a_recv, up_send, up_recv, dn_send, dn_recv, x_send, x_recv,
    gather_send, gather_recv, part_send, part_recv, halo_send, halo_recv,
    rx_send, rx_recv, rz_send, rz_recv, via_send, via_recv, back_send, back_recv, store_sem,
):
    Z, X, N, T, Q = plan["Z"], 2, 2, 4, plan["Z"] * 2
    L, D, FS, CS = plan["L"], plan["D"], plan["FS"], plan["CS"]
    HALF, GROUP = 2 * L, 4 * L
    wide, n = lax.axis_index("wide"), lax.axis_index("narrow")
    c, q = lax.rem(wide, 2), wide // 2
    x, z = lax.rem(q, X), q // X
    t = c * N + n

    def device(z_, x_, c_, n_):
        return ((z_ * X + x_) * 2 + c_, n_)

    over_core = device(z, x, 1 - c, n)
    over_side = device(z, x, c, 1 - n)
    over_both = device(z, x, 1 - c, 1 - n)
    over_x = device(z, 1 - x, c, n)
    z_ahead = [lax.rem(z + k, Z) for k in range(Z)]
    z_behind = [lax.rem(z - k + Z, Z) for k in range(Z)]
    q_next, q_prev = lax.rem(q + 1, Q), lax.rem(q - 1 + Q, Q)
    over_next, over_prev = (q_next * 2 + c, n), (q_prev * 2 + c, n)

    def remote(src, dst, send, recv, to):
        return pltpu.make_async_remote_copy(
            src_ref=src, dst_ref=dst, send_sem=send, recv_sem=recv, device_id=to, device_id_type=MESH
        )

    cut = -(-FS // 256) * 128
    halves = (slice(0, cut), slice(cut, FS))

    def views(in_, out, gate, up, down, small_):
        def half(ref, cols):
            return None if ref is None else ref.at[..., pl.ds(cols.start, cols.stop - cols.start)]

        return (in_, out, *(half(gate, h) for h in halves), *(half(up, h) for h in halves), down, small_)

    weights = views(w_in, w_out, w_gate, w_up, w_down.at[:, pl.ds(0, D // 2)], w_small)
    weights += (w_down.at[:, pl.ds(D // 2, D - D // 2)],)
    grads = views(w_in, w_out, w_gate, w_up, g_down, g_small)
    rx = views(rx_in, rx_out, rx_gate, rx_up, rx_down, rx_small)
    rz = views(rz_in, rz_out, rz_gate, rz_up, rz_down, rz_small)
    via = views(via_in, via_out, via_gate, via_up, via_down, via_small)
    fin = views(fin_in, fin_out, fin_gate, fin_up, fin_down, fin_small)
    home = views(home_in, None, home_gate, home_up, None, home_small)
    piece = in_weight.shape[0]
    width = out_own.shape[0]
    stage_in = proj_seed.at[0, pl.ds(0, T * piece), :]
    stage_gate = silu.at[0, pl.ds(0, T * piece), :]
    stage_up = slope.at[0, pl.ds(0, T * piece), :]
    staged = views(stage_in, None, stage_gate, stage_up, None, None)

    def chunk_size(i):
        return weights[i].shape[0] // Q

    def chunk(refs, i, z_, x_):
        rows = refs[i].shape[0] // Q
        start = pl.multiple_of((z_ * X + x_) * rows, 8 if rows == 8 else 16)
        return refs[i].at[pl.ds(start, rows), :]

    def block(ref, batch, member, rows=L):
        return ref.at[batch, pl.ds(pl.multiple_of(member * L, 16), rows), :]

    def own_rows(i):
        start = q * T * piece + t * piece
        return weights[i].at[pl.ds(pl.multiple_of(start, 16), piece), :]

    def small_block(member):
        lanes = pl.ds(pl.multiple_of(member * 128, 128), 128)
        return w_small.at[pl.ds(pl.multiple_of(q * 16, 16), 16), lanes]

    loads = {}
    for name, src, dst in (
        ("small", small, small_block(t)),
        ("in", in_weight, raw_in),
        (OUT, out_own, chunk(weights, OUT, z, x)),
        (DOWN, down_own, chunk([w_down], 0, z, x)),
        ("tokens0", tokens.at[0], block(toks, 0, t)),
        ("tokens1", tokens.at[1], block(toks, 1, t)),
        ("gate", gate_weight, raw_gate),
        ("up", up_weight, raw_up),
        ("valid", valid, valid_rows),
        ("cot0", cotangent.at[0], block(seeds, 0, t)),
        ("cot1", cotangent.at[1], block(seeds, 1, t)),
    ):
        loads[name] = pltpu.make_async_copy(src, dst, local_sem.at[len(loads)])
        loads[name].start()

    def split(raw, stage, full, parts):
        cols = raw.shape[1] // (parts * T)
        run = cols // Q
        for member in range(T):
            for part in range(parts):
                first = part * cols * T + member * run
                runs = [raw[:, first + k * T * run : first + (k * T + 1) * run].astype(F32) for k in range(Q)]
                stage[member * piece : (member + 1) * piece, part * cols : (part + 1) * cols] = (
                    jnp.concatenate(runs, axis=1).astype(BF16)
                )
        mine = stage[pl.ds(pl.multiple_of(t * piece, 16), piece), :]
        full[pl.ds(pl.multiple_of(q * T * piece + t * piece, 16), piece), :] = mine

    barrier = pltpu.get_barrier_semaphore()
    partners = [over_core, over_side, over_both, over_x, over_next, over_prev]
    partners += [device(z_ahead[k], x, c, n) for k in range(1, Z)]
    for partner in partners:
        pl.semaphore_signal(barrier, inc=1, device_id=partner, device_id_type=MESH)
    loads["in"].wait()
    split(raw_in, stage_in, w_in, 3)
    pl.semaphore_wait(barrier, len(partners))

    group = [(over_core, (1 - c) * N + n), (over_side, c * N + 1 - n), (over_both, (1 - c) * N + 1 - n)]

    def slices(i):
        s = SLICED.index(i)
        found = []
        for k, (to, member) in enumerate(group):
            if i == SMALL:
                src, dst = small_block(t), small_block(t)
            else:
                src, dst = staged[i].at[pl.ds(pl.multiple_of(member * piece, 16), piece), :], own_rows(i)
            found.append(remote(src, dst, a_send.at[s, k], a_recv.at[s, k], to))
        return found

    def slices_arrive(i):
        s = SLICED.index(i)
        for k, (to, member) in enumerate(group):
            if i == SMALL:
                dst = small_block(member)
            else:
                start = q * T * piece + member * piece
                dst = weights[i].at[pl.ds(pl.multiple_of(start, 16), piece), :]
            remote(dst, dst, a_send.at[s, k], a_recv.at[s, k], to).wait_recv()

    def gather_copies(ref, use, batch):
        mine = block(ref, batch, t)
        side = block(ref, batch, c * N + 1 - n)
        return (
            remote(mine, mine, gather_send.at[use, batch, 0], gather_recv.at[use, batch, 0], over_side),
            remote(mine, mine, gather_send.at[use, batch, 1], gather_recv.at[use, batch, 1], over_core),
            remote(side, side, gather_send.at[use, batch, 2], gather_recv.at[use, batch, 2], over_core),
        )

    def gather_start(ref, use, batch):
        to_side, to_core, _ = gather_copies(ref, use, batch)
        to_side.start()
        to_core.start()

    def gather_relay(ref, use, batch):
        to_side, _, relay = gather_copies(ref, use, batch)
        to_side.wait_recv()
        relay.start()

    def gather_finish(ref, use, batch):
        to_side, to_core, relay = gather_copies(ref, use, batch)
        to_core.wait_recv()
        relay.wait_recv()
        for copy in (to_side, to_core, relay):
            copy.wait_send()

    def z_copy(i, j, line, upward):
        if upward:
            src_z, to, send, recv = z - (j - 1), device(z + 1, line_x(0), c, n), up_send, up_recv
        else:
            src_z, to, send, recv = z + (j - 1), device(z - 1, line_x(0), c, n), dn_send, dn_recv
        part = chunk(weights, i, src_z, line_x(line))
        return remote(part, part, send.at[i, j - 1, line], recv.at[i, j - 1, line], to)

    def z_arrival(i, j, line, upward):
        src_z = z - j if upward else z + j
        part = chunk(weights, i, src_z, line_x(line))
        send, recv = (up_send, up_recv) if upward else (dn_send, dn_recv)
        return remote(part, part, send.at[i, j - 1, line], recv.at[i, j - 1, line], over_x)

    def line_x(line):
        return x if line == 0 else 1 - x

    def z_launch(i, line):
        @pl.when(z < Z - 1)
        def _():
            z_copy(i, 1, line, True).start()

        @pl.when(z > 0)
        def _():
            z_copy(i, 1, line, False).start()

    def x_copy(i, z_, arrival=False):
        part = chunk(weights, i, z_, 1 - x if arrival else x)
        return remote(part, part, x_send.at[i, z_], x_recv.at[i, z_], over_x)

    def z_pass(i, j, line, to_x):
        @pl.when(z - j >= 0)
        def _():
            z_arrival(i, j, line, True).wait_recv()
            if j < Z - 1:
                @pl.when(z < Z - 1)
                def _():
                    z_copy(i, j + 1, line, True).start()
            if to_x:
                x_copy(i, z - j).start()

        @pl.when(z + j <= Z - 1)
        def _():
            z_arrival(i, j, line, False).wait_recv()
            if j < Z - 1:
                @pl.when(z > 0)
                def _():
                    z_copy(i, j + 1, line, False).start()
            if to_x:
                x_copy(i, z + j).start()

    def z_settle(i, line):
        for j in range(1, Z):
            @pl.when((z < Z - 1) & (z - (j - 1) >= 0))
            def _():
                z_copy(i, j, line, True).wait_send()

            @pl.when((z > 0) & (z + (j - 1) <= Z - 1))
            def _():
                z_copy(i, j, line, False).wait_send()

    def x_arrive(i):
        for z_ in range(Z):
            x_copy(i, z_, True).wait_recv()

    def x_settle(i):
        for z_ in range(Z):
            x_copy(i, z_).wait_send()

    def part_copies(use, batch):
        lane = LANES[use]
        return (
            remote(
                core_send.at[batch], core_recv.at[lane, batch],
                part_send.at[use, batch, 0], part_recv.at[use, batch, 0], over_core,
            ),
            remote(
                side_send.at[batch], side_recv.at[lane, batch],
                part_send.at[use, batch, 1], part_recv.at[use, batch, 1], over_side,
            ),
        )

    def parts_send(use, batch):
        lane = LANES[use]
        to_core, to_side = part_copies(use, batch)
        to_core.wait_recv()
        rows = pl.ds(pl.multiple_of((1 - n) * L, 16), L)
        side_send[batch] = (
            keep[batch, rows, :] + core_recv[lane, batch, rows, :].astype(F32)
        ).astype(BF16)
        to_side.start()

    def parts_begin(use, product, prepare=lambda batch: None):
        for batch in range(2):
            def put_away(cols, value, batch=batch):
                core_send[batch, :, cols] = value.astype(BF16)

            def put_keep(cols, value, batch=batch):
                keep[batch, :, cols] = value

            prepare(batch)
            product(batch, (1 - c) * HALF, put_away)
            part_copies(use, batch)[0].start()
            if batch == 1:
                parts_send(use, 0)
            product(batch, c * HALF, put_keep)

    def parts_middle(use):
        parts_send(use, 1)

    def parts_end(use, batch):
        lane = LANES[use]
        to_core, to_side = part_copies(use, batch)
        to_side.wait_recv()
        rows = pl.ds(pl.multiple_of(n * L, 16), L)
        total = (
            keep[batch, rows, :]
            + core_recv[lane, batch, rows, :].astype(F32)
            + side_recv[lane, batch].astype(F32)
        )
        to_core.wait_send()
        to_side.wait_send()
        return total

    def rx_copy(i, z_):
        return remote(chunk(grads, i, z_, 1 - x), rx[i].at[z_], rx_send.at[i, z_], rx_recv.at[i, z_], over_x)

    at_end = (z == 0) | (z == Z - 1)
    def steps(i):
        if i == DOWN:
            return (
                jnp.where(z < 2, 1 - z, jnp.where(z == 2, 1, 0)),
                jnp.where(z < 2, 2, jnp.where(z == 2, 0, 1)),
                jnp.where(z == 3, 2, 3),
            )
        return (
            jnp.where(z == 0, 3, jnp.where(z == 1, 2, jnp.where(z == 2, 3, 0))),
            jnp.where(z == 0, 2, jnp.where(z == 1, 0, 1)),
            jnp.where(z == 0, 1, jnp.where(z == 1, 3, jnp.where(z == 2, 0, 2))),
        )

    def rz_copy(i, k):
        to_z = lax.rem(z + k, Z)
        return remote(
            chunk(grads, i, to_z, x), rz[i].at[k - 1], rz_send.at[i, k - 1], rz_recv.at[i, k - 1],
            device(to_z, x, c, n),
        )

    def via_copy(i):
        src_z, to_z = jnp.where(z == 0, 3, 0), jnp.where(z == 0, 1, 2)
        return remote(chunk(grads, i, src_z, x), via[i], via_send.at[i], via_recv.at[i], device(to_z, x, c, n))

    def reduce_start(i, places=None):
        for z_ in (*steps(i), z) if places is None else places:
            rx_copy(i, z_).start()

    def reduce_pass(i, step):
        z_ = steps(i)[step - 1]
        k = lax.rem(z_ - z + Z, Z)
        rx_copy(i, z_).wait_recv()
        part = chunk(grads, i, z_, x)
        opposite = at_end & (z + z_ == Z - 1)
        helps = jnp.logical_not(at_end) & ((z_ - z == 2) | (z - z_ == 2))

        @pl.when(helps)
        def _():
            via_copy(i).wait_recv()
            total = part[...].astype(F32) + rx[i][z_].astype(F32) + via[i][...].astype(F32)
            part[...] = total.astype(part.dtype)

        @pl.when(jnp.logical_not(helps))
        def _():
            part[...] = (part[...].astype(F32) + rx[i][z_].astype(F32)).astype(part.dtype)

        @pl.when(opposite)
        def _():
            via_copy(i).start()

        @pl.when(jnp.logical_not(opposite))
        def _():
            rz_copy(i, k).start()

    def reduce_end(i):
        rx_copy(i, z).wait_recv()

        def total(arrivals):
            value = chunk(grads, i, z, x)[...].astype(F32) + rx[i][z].astype(F32)
            for k in arrivals:
                rz_copy(i, k).wait_recv()
                value = value + rz[i][k - 1].astype(F32)
            fin[i][...] = value.astype(fin[i].dtype)

        @pl.when(z == 0)
        def _():
            total((2, 3))

        @pl.when(z == Z - 1)
        def _():
            total((1, 2))

        @pl.when(jnp.logical_not(at_end))
        def _():
            total((1, 2, 3))
            rz_copy(i, 1).wait_send()
            rz_copy(i, 3).wait_send()

        @pl.when(at_end)
        def _():
            via_copy(i).wait_send()
            rz_copy(i, jnp.where(z == 0, 1, 3)).wait_send()

        rz_copy(i, 2).wait_send()
        for z_ in range(Z):
            rx_copy(i, z_).wait_send()

    wholes = {
        IN: (home_in, done_in, in_grad, 3), GATE: (home_gate, done_gate, gate_grad, 1),
        UP: (home_up, done_up, up_grad, 1),
    }

    def back_copies(i):
        s = SLICED.index(i)
        found = []
        for k, (to, member) in enumerate(group):
            src = fin[i] if i == SMALL else fin[i].at[pl.ds(pl.multiple_of(member * piece, 16), piece), :]
            found.append(remote(src, home[i].at[t], back_send.at[s, k], back_recv.at[s, k], to))
        return found

    def back_start(i):
        for copy in back_copies(i):
            copy.start()
        if i == SMALL:
            home_small[t] = fin_small[...]
        else:
            home[i][t] = fin[i][pl.ds(pl.multiple_of(t * piece, 16), piece), :]

    def back_arrive(i):
        s = SLICED.index(i)
        for k, (to, member) in enumerate(group):
            dst = home[i].at[member]
            remote(dst, dst, back_send.at[s, k], back_recv.at[s, k], to).wait_recv()
        for copy in back_copies(i):
            copy.wait_send()

    stores = []

    def store(src, dst):
        copy = pltpu.make_async_copy(src, dst, store_sem.at[len(stores)])
        copy.start()
        stores.append(copy)

    def merge(i):
        for half in i if i in (GATE, UP) else (i,):
            back_arrive(half)
        source, target, result, parts = wholes[i]
        cols = source.shape[2] // parts
        run = cols // Q
        for part in range(parts):
            runs = [
                source[member, :, part * cols + k * run : part * cols + (k + 1) * run].astype(F32)
                for k in range(Q)
                for member in range(T)
            ]
            target[:, part * cols * T : (part + 1) * cols * T] = jnp.concatenate(runs, axis=1)
        store(target, result)

    def merge_small():
        back_arrive(SMALL)
        gains = home_small[0] + home_small[1] + home_small[2] + home_small[3]
        mine = gains
        for member in range(1, T):
            moved = jnp.concatenate([gains[:, member * width :], gains[:, : member * width]], axis=1)
            mine = jnp.where(t == member, moved, mine)
        done_small[...] = mine
        done_small[2:5, :] = home_small[t, 2:5, :]
        store(done_small, small_grad)

    loads["small"].wait()
    for copy in slices(SMALL):
        copy.start()
    loads[OUT].wait()
    z_launch(OUT, 0)
    x_copy(OUT, z).start()
    loads[DOWN].wait()
    x_copy(DOWN1, z).start()
    z_launch(DOWN1, 0)
    for copy in slices(IN):
        copy.start()
    slices_arrive(SMALL)
    z_launch(SMALL, 0)
    x_copy(SMALL, z).start()
    loads["gate"].wait()
    split(raw_gate, stage_gate, w_gate, 1)
    for i in GATE:
        for copy in slices(i):
            copy.start()
    for batch in range(2):
        loads["tokens%d" % batch].wait()
        gather_start(toks, 0, batch)
    slices_arrive(IN)
    z_launch(IN, 0)
    x_copy(IN, z).start()
    loads["up"].wait()
    split(raw_up, stage_up, w_up, 1)
    for i in UP:
        for copy in slices(i):
            copy.start()
    for i in (OUT, SMALL, IN):
        z_pass(i, 1, 0, True)
    loads["valid"].wait()
    for batch in range(2):
        loads["cot%d" % batch].wait()
        mine = pl.ds(pl.multiple_of(t * L, 16), L)
        column = jnp.transpose(jnp.broadcast_to(valid_rows[batch : batch + 1, :], (128, L)))[:, :1]
        seeds[batch, mine, :] = (seeds[batch, mine, :].astype(F32) * column).astype(BF16)
    for i in (OUT, SMALL, IN):
        z_pass(i, 2, 0, True)
    slices_arrive(GATE0)
    z_launch(GATE0, 0)
    x_copy(GATE0, z).start()
    gather_relay(toks, 0, 0)
    gather_relay(toks, 0, 1)
    for batch in range(2):
        gather_start(seeds, 1, batch)
    for i in (OUT, SMALL, IN):
        z_pass(i, 3, 0, True)
    x_arrive(SMALL)
    pieces = [
        jnp.concatenate(
            [w_small[k * 16 : (k + 1) * 16, m * 128 : m * 128 + width].astype(F32)[:8] for m in range(T)],
            axis=1,
        )
        for k in range(Q)
    ]
    params[...] = jnp.concatenate(pieces, axis=1)

    def norm_rows(ref, gain):
        block_ = ref.astype(F32)
        return (block_ * row_scale(block_) * gain).astype(BF16)

    for batch in range(2):
        gather_finish(toks, 0, batch)

        @pl.loop(0, GROUP // 64)
        def _(step, batch=batch):
            rows = pl.ds(pl.multiple_of(step * 64, 64), 64)
            normed_one[batch, rows, :] = norm_rows(toks[batch, rows, :], params[0:1, :])

    x_arrive(IN)
    for batch in range(2):
        for start, size in column_tiles(3 * CS, 256):
            projected[batch, :, start : start + size] = nn(normed_one[batch], w_in[:, start : start + size])
        gated[batch, 8 : 8 + GROUP, :] = projected[batch, :, :CS] * projected[batch, :, 2 * CS :]

    def halo_copies(batch):
        ahead = remote(
            gated.at[batch, pl.ds(GROUP, 8), :], gated.at[batch, pl.ds(0, 8), :],
            halo_send.at[0, batch], halo_recv.at[0, batch], over_next,
        )
        back = remote(
            conv.at[batch, pl.ds(0, 8), :], conv.at[batch, pl.ds(GROUP, 8), :],
            halo_send.at[1, batch], halo_recv.at[1, batch], over_prev,
        )
        return ahead, back

    for batch in range(2):
        halo_copies(batch)[0].start()
    slices_arrive(UP0)
    z_launch(UP0, 0)
    x_copy(UP0, z).start()
    z_pass(GATE0, 1, 0, True)
    my_lanes = pl.ds(pl.multiple_of(t * 128, 128), 128)
    taps = jnp.concatenate(
        [w_small[k * 16 : (k + 1) * 16, my_lanes].astype(F32)[2:5, :width] for k in range(Q)], axis=1
    )
    def mix(batch):
        halo_copies(batch)[0].wait_recv()

        @pl.when(q == 0)
        def _():
            gated[batch, 0:8, :] = jnp.zeros((8, CS), F32)

        for r in range(0, GROUP, HALF):
            value = (
                taps[0:1] * gated[batch, r + 6 : r + 6 + HALF, :]
                + taps[1:2] * gated[batch, r + 7 : r + 7 + HALF, :]
                + taps[2:3] * gated[batch, r + 8 : r + 8 + HALF, :]
            )
            branch[batch, r : r + HALF, :] = (projected[batch, r : r + HALF, CS : 2 * CS] * value).astype(BF16)

    z_pass(GATE0, 2, 0, True)
    x_arrive(OUT)

    def product_out(batch, start, put):
        rows = pl.ds(pl.multiple_of(start, 16), HALF)
        for at, size in column_tiles(D, 512):
            put(slice(at, at + size), nn(branch[batch, rows, :], w_out[:, at : at + size]))

    parts_begin(0, product_out, mix)
    z_pass(GATE0, 3, 0, True)
    z_pass(UP0, 1, 0, True)
    parts_middle(0)
    slices_arrive(GATE1)
    z_launch(GATE1, 0)
    x_copy(GATE1, z).start()
    gather_relay(seeds, 1, 0)
    gather_relay(seeds, 1, 1)
    z_pass(UP0, 2, 0, True)
    for batch in range(2):
        mine = pl.ds(pl.multiple_of(t * L, 16), L)
        hidden[batch] = toks[batch, mine, :].astype(F32) + parts_end(0, batch)
        normed_two[batch, mine, :] = norm_rows(hidden[batch], params[1:2, :])
        gather_start(normed_two, 2, batch)
    z_pass(UP0, 3, 0, True)
    slices_arrive(UP1)
    z_launch(UP1, 0)
    x_copy(UP1, z).start()
    z_pass(GATE1, 1, 0, True)
    z_launch(DOWN, 0)
    x_copy(DOWN1, z, True).wait_recv()
    z_launch(DOWN1, 1)
    gather_relay(normed_two, 2, 0)
    gather_relay(normed_two, 2, 1)
    z_pass(GATE1, 2, 0, True)
    for batch in range(2):
        gather_finish(normed_two, 2, batch)
        gather_finish(seeds, 1, batch)
    z_pass(GATE1, 3, 0, True)
    z_pass(UP1, 1, 0, True)

    x_arrive(GATE0)
    x_arrive(UP0)
    for i in SLICED:
        for copy in slices(i):
            copy.wait_send()

    def feed_forward(batch, part):
        for r in range(0, GROUP, HALF):
            for start, size in column_tiles(part.stop - part.start, 384):
                cols = slice(part.start + start, part.start + start + size)
                rows = slice(r, r + HALF)
                left = normed_two[batch, rows, :]
                gate = nn(left, w_gate[:, cols])
                up = nn(left, w_up[:, cols])
                sig = 1.0 / (1.0 + jnp.exp(-gate))
                act = gate * sig
                silu[batch, rows, cols] = act.astype(BF16)
                slope[batch, rows, cols] = (up * sig * (1.0 + gate * (1.0 - sig))).astype(BF16)
                activated[batch, rows, cols] = (act * up).astype(BF16)

    def weight_grad(dst, left, right, most_rows, most_cols):
        for a, rows in column_tiles(dst.shape[0], most_rows):
            for b, cols in column_tiles(dst.shape[1], most_cols):
                value = tn(left[0, :, a : a + rows], right[0, :, b : b + cols])
                value = value + tn(left[1, :, a : a + rows], right[1, :, b : b + cols])
                dst[a : a + rows, b : b + cols] = value.astype(BF16)

    feed_forward(0, halves[0])
    z_pass(UP1, 2, 0, True)
    feed_forward(1, halves[0])
    weight_grad(g_down.at[pl.ds(0, cut), :], activated.at[:, :, pl.ds(0, cut)], seeds, 384, 512)
    z_pass(UP1, 3, 0, True)
    x_copy(DOWN, z).start()

    def down_pass(j):
        z_pass(DOWN, j, 0, True)
        z_pass(DOWN1, j, 0, False)
        z_pass(DOWN1, j, 1, False)

    down_pass(1)
    x_arrive(GATE1)
    x_arrive(UP1)
    feed_forward(0, halves[1])
    down_pass(2)
    feed_forward(1, halves[1])
    down_pass(3)
    ready = cut // (chunk_size(DOWN) * X)
    reduce_start(DOWN, range(ready))
    weight_grad(g_down.at[pl.ds(cut, FS - cut), :], activated.at[:, :, pl.ds(cut, FS - cut)], seeds, 384, 512)
    reduce_start(DOWN, range(ready, Z))

    x_arrive(DOWN)
    def seed_batch(batch):
        for r in range(0, GROUP, HALF):
            for start, size in column_tiles(FS, 384):
                cols = slice(start, start + size)
                rows = slice(r, r + HALF)
                act_grad = nt(seeds[batch, rows, :], w_down[cols, :])
                silu[batch, rows, cols] = (act_grad * silu[batch, rows, cols].astype(F32)).astype(BF16)
                slope[batch, rows, cols] = (act_grad * slope[batch, rows, cols].astype(F32)).astype(BF16)

    up_seed, gate_seed = silu, slope

    def product_ffn(batch, start, put):
        rows = pl.ds(pl.multiple_of(start, 16), HALF)
        for at, size in column_tiles(D, 512):
            put(
                slice(at, at + size),
                nt(gate_seed[batch, rows, :], w_gate[at : at + size, :])
                + nt(up_seed[batch, rows, :], w_up[at : at + size, :]),
            )

    def product_down(batch, start, put):
        rows = pl.ds(pl.multiple_of(start, 16), HALF)
        for at, size in column_tiles(D, 512):
            put(slice(at, at + size), nn(activated[batch, rows, :], w_down[:, at : at + size]))

    parts_begin(2, product_ffn, seed_batch)
    parts_middle(2)
    reduce_pass(DOWN, 1)
    for i in (IN, OUT, *GATE, *UP, DOWN, SMALL, DOWN1):
        z_settle(i, 0)
        if i == DOWN1:
            z_settle(i, 1)
            x_copy(i, z).wait_send()
        else:
            x_settle(i)
    for i, part in zip(GATE, halves):
        weight_grad(grads[i], normed_two, gate_seed.at[:, :, pl.ds(part.start, part.stop - part.start)], 256, 384)
        reduce_start(i)
    reduce_pass(DOWN, 2)
    weight_grad(w_up, normed_two, up_seed, 256, 384)
    pass
    reduce_pass(DOWN, 3)
    gain_two = jnp.zeros((1, D), F32)
    for batch in range(2):
        mine = pl.ds(pl.multiple_of(t * L, 16), L)
        n2g = parts_end(2, batch)
        hid = hidden[batch]
        scale = row_scale(hid)
        gain_two = gain_two + jnp.sum(n2g * hid * scale, axis=0, keepdims=True)
        scaled = n2g * params[1:2, :]
        value = (
            seeds[batch, mine, :].astype(F32)
            + scale * scaled
            - hid * (scale * scale * scale) * jnp.mean(scaled * hid, axis=-1, keepdims=True)
        )
        hidden_grad[batch] = value
        out_seed[batch, mine, :] = value.astype(BF16)
        gather_start(out_seed, 3, batch)
    parts_begin(1, product_down)
    gather_relay(out_seed, 3, 0)
    gather_relay(out_seed, 3, 1)
    parts_middle(1)
    reduce_pass(GATE0, 1)
    for batch in range(2):
        gather_finish(out_seed, 3, batch)
        for r in range(0, GROUP, HALF):
            rows = slice(r, r + HALF)
            branch_grad = nt(out_seed[batch, rows, :], w_out[...])
            conv_grad = branch_grad * projected[batch, rows, CS : 2 * CS]
            conv[batch, rows, :] = conv_grad
            mixed = (
                taps[0:1] * gated[batch, r + 6 : r + 6 + HALF, :]
                + taps[1:2] * gated[batch, r + 7 : r + 7 + HALF, :]
                + taps[2:3] * gated[batch, r + 8 : r + 8 + HALF, :]
            )
            proj_seed[batch, rows, CS : 2 * CS] = (branch_grad * mixed).astype(BF16)
        halo_copies(batch)[1].start()
    reduce_start(UP0)
    reduce_start(UP1)
    kernel_grad = [jnp.zeros((1, CS), F32) for _ in range(3)]
    for batch in range(2):
        for r in range(0, GROUP, HALF):
            conv_grad = conv[batch, r : r + HALF, :]
            for k in range(3):
                kernel_grad[k] = kernel_grad[k] + jnp.sum(
                    conv_grad * gated[batch, r + 6 + k : r + 6 + k + HALF, :], axis=0, keepdims=True
                )
    weight_grad(w_out, branch, out_seed, 256, 512)
    reduce_pass(GATE0, 2)
    reduce_pass(GATE0, 3)
    def unmix(batch):
        halo_copies(batch)[1].wait_recv()

        @pl.when(q == Q - 1)
        def _():
            conv[batch, GROUP : GROUP + 8, :] = jnp.zeros((8, CS), F32)

        for r in range(0, GROUP, HALF):
            rows = slice(r, r + HALF)
            value = (
                taps[2:3] * conv[batch, r : r + HALF, :]
                + taps[1:2] * conv[batch, r + 1 : r + 1 + HALF, :]
                + taps[0:1] * conv[batch, r + 2 : r + 2 + HALF, :]
            )
            proj_seed[batch, rows, :CS] = (value * projected[batch, rows, 2 * CS :]).astype(BF16)
            proj_seed[batch, rows, 2 * CS :] = (value * projected[batch, rows, :CS]).astype(BF16)

    def product_in(batch, start, put):
        rows = pl.ds(pl.multiple_of(start, 16), HALF)
        for at, size in column_tiles(D, 512):
            put(slice(at, at + size), nt(proj_seed[batch, rows, :], w_in[at : at + size, :]))

    for batch in range(2):
        mine = pl.ds(pl.multiple_of(t * L, 16), L)
        seeds[batch, mine, :] = (hidden[batch] + parts_end(1, batch)).astype(BF16)
    out_copies = [
        pltpu.make_async_copy(block(seeds, batch, t), block_out.at[batch], local_sem.at[2 + batch])
        for batch in range(2)
    ]
    for copy in out_copies:
        copy.start()
    parts_begin(3, product_in, unmix)
    parts_middle(3)
    reduce_pass(GATE1, 1)
    reduce_pass(GATE1, 2)
    reduce_pass(GATE1, 3)
    weight_grad(w_in, normed_one, proj_seed, 256, 384)
    reduce_start(IN)
    reduce_start(OUT)
    reduce_pass(UP0, 1)
    reduce_pass(UP0, 2)
    reduce_pass(UP0, 3)
    reduce_end(DOWN)
    store(fin_down, down_grad)
    gain_one = jnp.zeros((1, D), F32)
    for batch in range(2):
        mine = pl.ds(pl.multiple_of(t * L, 16), L)
        n1g = parts_end(3, batch)
        inputs = toks[batch, mine, :].astype(F32)
        scale = row_scale(inputs)
        gain_one = gain_one + jnp.sum(n1g * inputs * scale, axis=0, keepdims=True)
        scaled = n1g * params[0:1, :]
        hidden_grad[batch] = (
            hidden_grad[batch]
            + scale * scaled
            - inputs * (scale * scale * scale) * jnp.mean(scaled * inputs, axis=-1, keepdims=True)
        )
    grad_copy = pltpu.make_async_copy(hidden_grad, input_grad, local_sem.at[1])
    grad_copy.start()
    for k in range(Q):
        lanes = slice(k * 128, (k + 1) * 128)
        runs = [jnp.pad(g[:, k * width : (k + 1) * width], ((0, 0), (0, 128 - width))) for g in kernel_grad]
        rows = [gain_one[:, lanes], gain_two[:, lanes], *runs, jnp.zeros((3, 128), F32)]
        g_small[k * 8 : (k + 1) * 8, :] = jnp.concatenate(rows, axis=0)
    reduce_start(SMALL)
    reduce_end(GATE0)
    back_start(GATE0)
    reduce_end(GATE1)
    back_start(GATE1)
    for step in (1, 2, 3):
        reduce_pass(UP1, step)
    merge(GATE)
    for step in (1, 2, 3):
        reduce_pass(IN, step)
    reduce_end(UP0)
    back_start(UP0)
    reduce_end(UP1)
    back_start(UP1)
    for i in (OUT, SMALL):
        for step in (1, 2, 3):
            reduce_pass(i, step)
    reduce_end(IN)
    back_start(IN)
    reduce_end(OUT)
    store(fin_out, out_grad)
    reduce_end(SMALL)
    back_start(SMALL)
    merge(UP)
    for batch in range(2):
        for copy in halo_copies(batch):
            copy.wait_send()
    merge(IN)
    merge_small()
    for copy in stores:
        copy.wait()
    for copy in out_copies:
        copy.wait()
    grad_copy.wait()


def hand_over(*refs):
    count = (len(refs) - 2) // 3
    sources, targets, held = refs[:count], refs[count : 2 * count], refs[2 * count : 3 * count]
    load_sem, store_sem = refs[3 * count :]
    loads = [pltpu.make_async_copy(sources[k], held[k], load_sem.at[k]) for k in range(count)]
    stores = [pltpu.make_async_copy(held[k], targets[k], store_sem.at[k]) for k in range(count)]
    for load in loads:
        load.start()
    for load, store in zip(loads, stores):
        load.wait()
        store.start()
    for store in stores:
        store.wait()


def fused(plan, tokens, cotangent, lengths, loss_mask, norm_gain, in_weight, conv_kernel, out_weight, ffn_gain, gate_weight, up_weight, down_weight):
    Z, Q, T = plan["Z"], plan["Q"], 4
    L, D, FS, CS = plan["L"], plan["D"], plan["FS"], plan["CS"]
    width, hid, rows = out_weight.shape[0], down_weight.shape[0], in_weight.shape[0]
    place = lax.axis_index(("wide", "narrow"))
    positions = place * L + jnp.arange(L, dtype=jnp.int32)
    valid = ((positions[None, :] < lengths[:, None]) & (loss_mask != 0)).astype(F32)
    valid = jnp.pad(valid, ((0, 6), (0, 0)))
    small = jnp.concatenate([norm_gain[None], ffn_gain[None], conv_kernel], axis=0)
    small = jnp.pad(small, ((0, 11), (0, 128 - width)))

    shapes = [(T * rows, 3 * CS), (width, D), (T * rows, FS), (T * rows, FS), (hid, D)]
    vm, dma = pltpu.VMEM, pltpu.SemaphoreType.DMA
    group = T * L
    scratch = [vm((Q * r, k), BF16) for r, k in shapes]
    scratch += [vm((Q * 16, T * 128), BF16), vm((Q * hid, D), BF16), vm((Q * 8, 128), F32)]
    scratch += [vm((Z, r, k), BF16) for r, k in shapes] + [vm((Z, 8, 128), F32)]
    scratch += [vm((Z - 1, r, k), BF16) for r, k in shapes] + [vm((Z - 1, 8, 128), F32)]
    scratch += [vm((r, k), BF16) for r, k in shapes] + [vm((8, 128), F32)]
    scratch += [vm((r, k), F32 if r in (width, hid) else BF16) for r, k in shapes]
    scratch += [vm((8, 128), F32)]
    scratch += [vm((T, rows, 3 * CS), BF16), vm((T, rows, FS), BF16), vm((T, rows, FS), BF16), vm((T, 8, 128), F32)]
    scratch += [vm(a.shape, F32) for a in (in_weight, gate_weight, up_weight)] + [vm((8, 128), F32)]
    scratch += [vm(a.shape, BF16) for a in (in_weight, gate_weight, up_weight)] + [vm((8, L), F32), vm((8, D), F32)]
    scratch += [vm((2, group, D), BF16) for _ in range(5)]
    scratch += [vm((2, L, D), F32), vm((2, L, D), F32)]
    scratch += [
        vm((2, group, 3 * CS), F32), vm((2, group + 8, CS), F32), vm((2, group + 8, CS), F32),
        vm((2, group, CS), BF16), vm((2, group, 3 * CS), BF16),
    ]
    scratch += [vm((2, group, FS), BF16) for _ in range(3)]
    scratch += [
        vm((2, 2 * L, D), BF16), vm((2, 2, 2 * L, D), BF16),
        vm((2, L, D), BF16), vm((2, 2, L, D), BF16), vm((2, 2 * L, D), F32),
    ]
    scratch += [
        dma((11,)), dma((6, 3)), dma((6, 3)),
        dma((9, Z - 1, 2)), dma((9, Z - 1, 2)), dma((9, Z - 1, 2)), dma((9, Z - 1, 2)),
        dma((9, Z)), dma((9, Z)),
        dma((4, 2, 3)), dma((4, 2, 3)), dma((4, 2, 2)), dma((4, 2, 2)), dma((2, 2)), dma((2, 2)),
        dma((8, Z)), dma((8, Z)), dma((8, Z - 1)), dma((8, Z - 1)), dma((8,)), dma((8,)), dma((6, 3)), dma((6, 3)), dma((6,)),
    ]
    out_shape = (
        jax.ShapeDtypeStruct((2, L, D), BF16),
        jax.ShapeDtypeStruct((2, L, D), F32),
        jax.ShapeDtypeStruct(in_weight.shape, F32),
        jax.ShapeDtypeStruct(out_weight.shape, F32),
        jax.ShapeDtypeStruct(gate_weight.shape, F32),
        jax.ShapeDtypeStruct(up_weight.shape, F32),
        jax.ShapeDtypeStruct(down_weight.shape, F32),
        jax.ShapeDtypeStruct((8, 128), F32),
    )
    block_out, input_grad, in_g, out_g, gate_g, up_g, down_g, small_g = pl.pallas_call(
        functools.partial(block_kernel, plan),
        out_shape=out_shape,
        in_specs=[pl.BlockSpec(memory_space=pl.ANY)] * 9,
        out_specs=[pl.BlockSpec(memory_space=pl.ANY)] * 8,
        scratch_shapes=scratch,
        compiler_params=pltpu.CompilerParams(
            collective_id=0, has_side_effects=True, vmem_limit_bytes=VMEM_LIMIT
        ),
    )(tokens, cotangent, valid, small, in_weight, out_weight, gate_weight, up_weight, down_weight)
    arrays = (block_out, input_grad, in_g, out_g, gate_g, up_g, down_g)
    block_out, input_grad, in_g, out_g, gate_g, up_g, down_g = pl.pallas_call(
        hand_over,
        out_shape=tuple(jax.ShapeDtypeStruct(a.shape, a.dtype) for a in arrays),
        in_specs=[pl.BlockSpec(memory_space=pltpu.HBM)] * len(arrays),
        out_specs=[pl.BlockSpec(memory_space=pltpu.HBM)] * len(arrays),
        scratch_shapes=[vm(a.shape, a.dtype) for a in arrays] + [dma((len(arrays),)), dma((len(arrays),))],
        compiler_params=pltpu.CompilerParams(vmem_limit_bytes=VMEM_LIMIT),
    )(*arrays)
    return (
        block_out, input_grad, small_g[0, :width], in_g, small_g[2:5, :width], out_g, small_g[1, :width],
        gate_g, up_g, down_g,
    )


def planned(wide, narrow, arrays):
    tokens, in_weight, down_weight = arrays[0], arrays[5], arrays[11]
    if narrow != 2 or wide != 16 or tokens.shape[0] != 2:
        return None
    groups = wide // 2
    rows, hid = in_weight.shape[0], down_weight.shape[0]
    sizes = {
        "Z": groups // 2, "Q": groups, "L": tokens.shape[1], "D": tokens.shape[2],
        "FS": hid * groups, "CS": rows * groups,
    }
    if rows % 16 or hid % 16 or sizes["L"] != 128 or sizes["FS"] % 128 or sizes["CS"] % 128 or rows != 32:
        return None
    return sizes


def solution(mesh):
    in_specs = (
        P(None, ("wide", "narrow"), None),
        P(None, ("wide", "narrow"), None),
        P(),
        P(None, ("wide", "narrow")),
        P(("wide", "narrow")),
        P(("wide", "narrow"), None),
        P(None, ("wide", "narrow")),
        P(("wide", "narrow"), None),
        P(("wide", "narrow")),
        P(("wide", "narrow"), None),
        P(("wide", "narrow"), None),
        P(("wide", "narrow"), None),
    )
    out_specs = (
        P(None, ("wide", "narrow"), None),
        P(None, ("wide", "narrow"), None),
        P(("wide", "narrow")),
        P(("wide", "narrow"), None),
        P(None, ("wide", "narrow")),
        P(("wide", "narrow"), None),
        P(("wide", "narrow")),
        P(("wide", "narrow"), None),
        P(("wide", "narrow"), None),
        P(("wide", "narrow"), None),
    )
    wide, narrow = mesh.shape["wide"], mesh.shape["narrow"]

    def step(*arrays):
        plan = planned(wide, narrow, arrays)
        run = body if plan is None else functools.partial(fused, plan)
        return run(*arrays)

    return jax.shard_map(step, mesh=mesh, in_specs=in_specs, out_specs=out_specs, check_vma=False)
```
